32 devices in a mesh: dp: 4 (over z), fsdp: 8 (over y, x, core).
Axes of the slice: x: 2, y: 2, z: 4, core: 2. Of those that a mesh axis runs over, the one named last changes fastest.
Arguments:
- tokens: bfloat16 [32768, 768], P(('dp', 'fsdp')), may hold values from -6 to 6
- first_values: bfloat16 [32768, 384], P(('dp', 'fsdp')), may hold values from -6 to 6
- cotangent: bfloat16 [32768, 768], P(('dp', 'fsdp')), may hold values from -6 to 6
- lengths: int32 [32, 2], P(('dp', 'fsdp')), may hold values from 0 to 1024, as said below
- vectors: float32 [8832], P('fsdp'), may hold values from -1 to 1.5
- w_qkv: bfloat16 [768, 1920], P(('dp', 'fsdp')), may hold values from -0.21875 to 0.21875
- w_out: bfloat16 [768, 768], P(('dp', 'fsdp')), may hold values from -1.75 to 1.75
- w_up: bfloat16 [768, 3072], P(('dp', 'fsdp')), may hold values from -0.21875 to 0.21875
- w_down: bfloat16 [3072, 768], P(('dp', 'fsdp')), may hold values from -0.109375 to 0.109375
Outputs:
- output: bfloat16 [32768, 768], P(('dp', 'fsdp'))
- grad_tokens: bfloat16 [32768, 768], P(('dp', 'fsdp'))
- grad_first_values: bfloat16 [32768, 384], P(('dp', 'fsdp'))
- grad_vectors: float32 [8832], P('fsdp')
- grad_qkv: float32 [768, 1920], P(('dp', 'fsdp'))
- grad_out: float32 [768, 768], P(('dp', 'fsdp'))
- grad_up: float32 [768, 3072], P(('dp', 'fsdp'))
- grad_down: float32 [3072, 768], P(('dp', 'fsdp'))
The draws below stay inside these ranges and needn't reach their ends.
Inputs may be any that keep to these rules, and one draw needn't show every extreme that they name: `lengths`: each row is either (1024, 0) or (512, 512); the first row is the former and the last row the latter.
All inputs are finite; a program needn't handle non-finite values.
Results may differ from the reference program's by a relative error of at most 0.012.
Values may be sent and summed in bfloat16 or wider, within the bound.
No kernel may reach another device: no remote copies, remote signals or barrier semaphores. Data moves between devices by JAX's collectives and lax.ppermute only.
A program may use at most 320 MiB of HBM per device.

```python
import math
import jax
import jax.numpy as jnp
from jax import lax

D = 768
H = 12
HD = 64
FF = 3072
TOK_DEV = 1024
VD = 384
QKV = 1920
VEC = 8832
RANKS = 32
TOKENS = 32768


def draw_lengths(key, part):
    key = jax.random.fold_in(key, 11)
    split = jax.random.randint(key, (RANKS,), 0, 2, dtype=jnp.int32)
    ranks = jnp.arange(RANKS, dtype=jnp.int32)
    split = jnp.where(ranks == 0, 0, split)
    split = jnp.where(ranks == RANKS - 1, 1, split)
    first = TOK_DEV - split * (TOK_DEV // 2)
    second = TOK_DEV - first
    return jnp.stack([first, second], axis=1).astype(jnp.int32)


def draw_vectors(key, part):
    key = jax.random.fold_in(key, 5)
    gain_key, shift_key = jax.random.split(key)
    gains = jax.random.uniform(gain_key, (2, D), jnp.float32, 0.5, 1.5)
    shifts = jnp.clip(0.3 * jax.random.normal(shift_key, (VEC,), jnp.float32), -1.0, 1.0)
    return jnp.concatenate([gains[0], shifts[D:4 * D + VD], gains[1], shifts[5 * D + VD:]]).astype(jnp.float32)


def level_of(own_key, dims, cuts, smallest, top_value):
    def one(dim, shards_of):
        steps = jax.random.uniform(jax.random.fold_in(jax.random.fold_in(own_key, 6), dim), (shards_of,), jnp.float32, smallest / len(cuts), top_value / len(cuts))
        return jnp.repeat(jnp.exp(steps), dims[dim] // shards_of).reshape((-1,) + (1,) * (len(dims) - dim - 1))

    level = one(*cuts[0])
    for cut in cuts[1:]:
        level = level * one(*cut)
    return level


def normal_values(own_key, extent, width, bound, shards=(), kind=jnp.bfloat16):
    drawn = width * jax.random.normal(own_key, extent, jnp.float32)
    if shards:
        drawn = drawn * level_of(own_key, extent, shards, -0.22, 0.18)
    return jnp.clip(drawn, -bound, bound).astype(kind)


def setup_inputs(seed: int = 0) -> dict:
    streams_of = jax.random.split(jax.random.key(seed), 10)
    tokens = normal_values(streams_of[0], (TOKENS, D), 1.0, 6.0, ((0, 32),))
    first_values = normal_values(streams_of[1], (TOKENS, VD), 1.0, 6.0, ((0, 32),))
    cotangent = normal_values(streams_of[2], (TOKENS, D), 1.0, 6.0, ((0, 32),))
    lengths = draw_lengths(jax.random.fold_in(streams_of[9], 71), 0)
    vectors = draw_vectors(jax.random.fold_in(streams_of[9], 71), 0)
    w_qkv = normal_values(streams_of[5], (D, QKV), D ** -0.5, 0.21875, ((0, 32),))
    w_out = normal_values(streams_of[6], (D, D), (D // 64) ** -0.5, 1.75, ((0, 32),))
    w_up = normal_values(streams_of[7], (D, FF), D ** -0.5, 0.21875, ((0, 32),))
    w_down = normal_values(streams_of[8], (FF, D), FF ** -0.5, 0.109375, ((0, 32),))
    return dict(tokens=tokens, first_values=first_values, cotangent=cotangent, lengths=lengths, vectors=vectors, w_qkv=w_qkv, w_out=w_out, w_up=w_up, w_down=w_down)


@jax.custom_vjp
def low(v):
    return lax.optimization_barrier(v.astype(jnp.bfloat16)).astype(jnp.float32)

@jax.custom_vjp
def low_back(v):
    return v

def low_keep(v):
    return (low(v), None)

def low_pass(kept, grad):
    return (grad,)

def back_keep(v):
    return (v, None)

def back_low(kept, grad):
    return (low(grad),)
low.defvjp(low_keep, low_pass)
low_back.defvjp(back_keep, back_low)
HIGH = lax.Precision.HIGHEST
EPSILON = 1e-05

def rounded_both(v):
    return low_back(low(v))

def norm_rows(v, gain, shift):
    center = v - lax.optimization_barrier(jnp.mean(v, axis=-1, keepdims=True))
    spread = lax.optimization_barrier(jnp.mean(center * center, axis=-1, keepdims=True))
    return center * lax.rsqrt(spread + EPSILON) * gain + shift

def gelu_tanh(v):
    return jax.nn.gelu(v, approximate=True)

def attend(query, keys, values, doc_ids):
    rows = query.shape[0]
    block = min(512, rows)
    position = jnp.arange(rows, dtype=jnp.int32)
    scale = 1.0 / math.sqrt(HD)

    def one_block(index):
        start = index * block
        part_query = lax.dynamic_slice_in_dim(query, start, block, 0)
        part_pos = lax.dynamic_slice_in_dim(position, start, block, 0)
        part_doc = lax.dynamic_slice_in_dim(doc_ids, start, block, 0)
        scores = low_back(jnp.einsum('qhd,khd->hqk', part_query, keys, precision=HIGH) * scale)
        allowed = (part_pos[:, None] >= position[None, :]) & (part_doc[:, None] == doc_ids[None, :])
        scores = jnp.where(allowed[None], scores, -1e+30)
        peak = lax.optimization_barrier(jnp.max(scores, axis=-1, keepdims=True))
        weights = jnp.exp(scores - peak)
        probs = low(weights / lax.optimization_barrier(jnp.sum(weights, axis=-1, keepdims=True)))
        return jnp.einsum('hqk,khd->qhd', probs, values, precision=HIGH)
    mixed = lax.map(jax.checkpoint(one_block), jnp.arange(rows // block, dtype=jnp.int32))
    return mixed.reshape(rows, H * HD)

def layer(inputs, first, vecs, w_qkv, w_out, w_up, w_down, doc_ids):
    gain_one = vecs[0:D]
    shift_one = vecs[D:2 * D]
    bias_query = vecs[2 * D:3 * D]
    bias_value = vecs[3 * D:3 * D + VD]
    bias_out = vecs[3 * D + VD:4 * D + VD]
    gain_two = vecs[4 * D + VD:5 * D + VD]
    shift_two = vecs[5 * D + VD:6 * D + VD]
    bias_up = vecs[6 * D + VD:6 * D + VD + FF]
    bias_down = vecs[6 * D + VD + FF:]
    rows = inputs.shape[0]
    act_one = low(norm_rows(inputs, gain_one, shift_one))
    mixed = jnp.dot(act_one, w_qkv, precision=HIGH)
    query = rounded_both(mixed[:, 0:D] + bias_query)
    keys = rounded_both(mixed[:, D:2 * D])
    fresh = rounded_both(mixed[:, 2 * D:] + bias_value)
    values = jnp.concatenate([fresh, first], axis=1)
    attended = rounded_both(attend(query.reshape(rows, H, HD), keys.reshape(rows, H, HD), values.reshape(rows, H, HD), doc_ids))
    residual = inputs + low_back(jnp.dot(attended, w_out, precision=HIGH) + bias_out)
    act_two = low(norm_rows(residual, gain_two, shift_two))
    before = low_back(jnp.dot(act_two, w_up, precision=HIGH) + bias_up)
    hidden = low(gelu_tanh(before))
    return residual + jnp.dot(hidden, w_down, precision=HIGH) + bias_down

def reference(tokens, first_values, cotangent, lengths, vectors, w_qkv, w_out, w_up, w_down):
    params = (vectors.astype(jnp.float32), w_qkv.astype(jnp.float32), w_out.astype(jnp.float32), w_up.astype(jnp.float32), w_down.astype(jnp.float32))
    count = tokens.shape[0] // TOK_DEV
    position = jnp.arange(TOK_DEV, dtype=jnp.int32)

    def step(totals, index):
        start = (index * TOK_DEV).astype(jnp.int32)
        inputs = lax.dynamic_slice_in_dim(tokens, start, TOK_DEV, 0).astype(jnp.float32)
        first = lax.dynamic_slice_in_dim(first_values, start, TOK_DEV, 0).astype(jnp.float32)
        grad_in = lax.dynamic_slice_in_dim(cotangent, start, TOK_DEV, 0).astype(jnp.float32)
        first_len = lax.dynamic_index_in_dim(lengths, index, 0, keepdims=False)[0]
        doc_ids = (position >= first_len).astype(jnp.int32)

        def forward(inputs, first, vecs, wq, wo, wu, wd):
            return layer(inputs, first, vecs, wq, wo, wu, wd, doc_ids)
        result, pull = jax.vjp(forward, inputs, first, *params)
        grads = pull(grad_in)
        totals = tuple((total + grad for total, grad in zip(totals, grads[2:])))
        return (totals, (result.astype(jnp.bfloat16), grads[0].astype(jnp.bfloat16), grads[1].astype(jnp.bfloat16)))
    start_totals = tuple((jnp.zeros_like(param) for param in params))
    totals, (outputs, grad_tokens, grad_first) = lax.scan(step, start_totals, jnp.arange(count, dtype=jnp.int32))
    return (outputs.reshape(-1, D), grad_tokens.reshape(-1, D), grad_first.reshape(-1, VD), totals[0], totals[1], totals[2], totals[3], totals[4])
```

```python
import functools, math
import jax
import jax.numpy as jnp
from jax.sharding import PartitionSpec as P
from jax import lax
from jax.experimental import pallas as pl
from jax.experimental.pallas import tpu as pltpu
BF=jnp.bfloat16; F32=jnp.float32
HD=64
NEG=-1e30
def nt(a,b): return lax.dot_general(a,b,(((1,),(1,)),((),())),preferred_element_type=F32)
def nn(a,b): return jnp.dot(a,b,preferred_element_type=F32)

def half_mask(head, n=128):
    return (lax.broadcasted_iota(jnp.int32,(1,n),1)//HD)==head

def attend_forward_kernel(len_ref, q_ref, k_ref, v_ref, o_ref, lse_ref, ot_ref):
    rows=q_ref.shape[0]; blk=256; half=rows//2
    bias=jnp.where(len_ref[0,0]<rows, NEG, 0.0).astype(F32)
    vt=v_ref[...].T
    causal=lax.broadcasted_iota(jnp.int32,(blk,blk),0)<=lax.broadcasted_iota(jnp.int32,(blk,blk),1)
    for head in range(2):
        vth=vt[HD*head:HD*head+HD]
        for i in range(rows//blk):
            q=jnp.where(half_mask(head), q_ref[i*blk:(i+1)*blk], jnp.zeros((),BF))
            parts=[]
            for j in range(i+1):
                s=nt(k_ref[j*blk:(j+1)*blk], q)
                if j==i: s=jnp.where(causal,s,NEG)
                elif i*blk>=half and (j+1)*blk<=half: s=s+bias
                parts.append(s)
            m=parts[0].max(axis=0,keepdims=True)
            for s in parts[1:]: m=jnp.maximum(m,s.max(axis=0,keepdims=True))
            l=jnp.zeros((1,blk),F32); ot=jnp.zeros((HD,blk),F32)
            for j,s in enumerate(parts):
                p=jnp.exp(s-m)
                l=l+p.sum(axis=0,keepdims=True)
                ot=ot+nn(vth[:,j*blk:(j+1)*blk],p.astype(BF))
            ot_ref[HD*head:HD*head+HD,i*blk:(i+1)*blk]=ot/l
            lse_ref[0,head:head+1,i*blk:(i+1)*blk]=m+jnp.log(l)
    o_ref[...]=ot_ref[...].T.astype(BF)

def attend_forward(lengths,q,k,v):
    rows,width=q.shape
    pair=pl.BlockSpec((rows,128),lambda p:(0,p))
    n=width//128
    return pl.pallas_call(attend_forward_kernel,grid=(n,),
        in_specs=[pl.BlockSpec(memory_space=pltpu.SMEM),pair,pair,pair],
        out_specs=[pair,pl.BlockSpec((1,2,rows),lambda p:(p,0,0))],
        out_shape=[jax.ShapeDtypeStruct((rows,width),BF),jax.ShapeDtypeStruct((n,2,rows),F32)],
        scratch_shapes=[pltpu.VMEM((128,rows),F32)],
        compiler_params=pltpu.CompilerParams(vmem_limit_bytes=48<<20),
        cost_estimate=pl.CostEstimate(flops=4*rows*rows*width,bytes_accessed=8*rows*width,transcendentals=rows*rows*width//64),
        name="attend_forward")(lengths,q,k,v)

def attend_backward_kernel(len_ref,q_ref,k_ref,v_ref,o_ref,do_ref,lse_ref,dq_ref,dk_ref,df_ref,gf_ref,dqt_ref,dv_ref,dk_acc,nfresh=3):
    rows=q_ref.shape[0]; blk=256; half=rows//2
    pair=pl.program_id(0)
    bias=jnp.where(len_ref[0,0]<rows, NEG, 0.0).astype(F32)
    prod=(do_ref[...].astype(F32)*o_ref[...].astype(F32)).T
    kt=k_ref[...].T
    causal=lax.broadcasted_iota(jnp.int32,(blk,blk),0)<=lax.broadcasted_iota(jnp.int32,(blk,blk),1)
    nb=rows//blk
    for head in range(2):
        delta=prod[HD*head:HD*head+HD].sum(axis=0,keepdims=True)
        lse=lse_ref[0,head:head+1,:]
        qh=jnp.where(half_mask(head), q_ref[...], jnp.zeros((),BF))
        doh=jnp.where(half_mask(head), do_ref[...], jnp.zeros((),BF))
        for j in range(nb):
            kj=k_ref[j*blk:(j+1)*blk]; vj=v_ref[j*blk:(j+1)*blk]
            ktj=kt[HD*head:HD*head+HD,j*blk:(j+1)*blk]
            dv=jnp.zeros((blk,128),F32); dk=jnp.zeros((blk,128),F32)
            for i in range(j,nb):
                sl=slice(i*blk,(i+1)*blk)
                s=nt(kj,qh[sl])
                if i==j: s=jnp.where(causal,s,NEG)
                elif i*blk>=half and (j+1)*blk<=half: s=s+bias
                p=jnp.exp(s-lse[:,sl])
                dp=nt(vj,doh[sl])
                ds=(p*(dp-delta[:,sl])).astype(BF)
                dv=dv+nn(p.astype(BF),doh[sl])
                dk=dk+nn(ds,qh[sl])
                dqt=nn(ktj,ds)
                if j==0: dqt_ref[HD*head:HD*head+HD,sl]=dqt
                else: dqt_ref[HD*head:HD*head+HD,sl]+=dqt
            kr=slice(j*blk,(j+1)*blk)
            if head==0:
                dv_ref[kr]=dv; dk_acc[kr]=dk
            else:
                dv_ref[kr]+=dv; dk_acc[kr]+=dk
    dq_ref[...]=(dqt_ref[...].T*0.125).astype(BF)
    dk_ref[...]=dk_acc[...].astype(BF)
    dv=dv_ref[...].astype(BF)
    @pl.when(pair<nfresh)
    def _(): df_ref[...]=dv
    @pl.when(pair>=nfresh)
    def _(): gf_ref[...]=dv

def attend_backward(lengths,q,k,v,o,do,lse):
    rows,width=q.shape
    pair=pl.BlockSpec((rows,128),lambda p:(0,p))
    n=width//128; nf=n//2
    return pl.pallas_call(functools.partial(attend_backward_kernel,nfresh=nf),grid=(n,),
        in_specs=[pl.BlockSpec(memory_space=pltpu.SMEM)]+[pair]*5+[pl.BlockSpec((1,2,rows),lambda p:(p,0,0))],
        out_specs=[pair,pair,pl.BlockSpec((rows,128),lambda p:(0,jnp.minimum(p,nf-1))),pl.BlockSpec((rows,128),lambda p:(0,jnp.maximum(p-nf,0)))],
        out_shape=[jax.ShapeDtypeStruct((rows,width),BF)]*2+[jax.ShapeDtypeStruct((rows,width//2),BF)]*2,
        scratch_shapes=[pltpu.VMEM((128,rows),F32),pltpu.VMEM((rows,128),F32),pltpu.VMEM((rows,128),F32)],
        compiler_params=pltpu.CompilerParams(vmem_limit_bytes=48<<20),
        cost_estimate=pl.CostEstimate(flops=10*rows*rows*width,bytes_accessed=16*rows*width,transcendentals=rows*rows*width//64),
        name="attend_backward")(lengths,q,k,v,o,do,lse)

def row_stats(v):
    center=v-jnp.mean(v,axis=-1,keepdims=True)
    rstd=lax.rsqrt(jnp.mean(center*center,axis=-1,keepdims=True)+1e-5)
    return center*rstd, rstd

def project_kernel(x_ref,first_ref,g_ref,b_ref,bq_ref,bv_ref,w_ref,a_ref,q_ref,k_ref,v_ref):
    d=x_ref.shape[1]; vd=first_ref.shape[1]
    xh,_=row_stats(x_ref[...].astype(F32))
    a=(xh*g_ref[...]+b_ref[...]).astype(BF)
    a_ref[...]=a
    q=(nn(a,w_ref[:,0:d])+bq_ref[...]).astype(BF)
    q_ref[...]=(q.astype(F32)*0.125).astype(BF)
    k_ref[...]=nn(a,w_ref[:,d:2*d]).astype(BF)
    v_ref[:,0:vd]=(nn(a,w_ref[:,2*d:])+bv_ref[...]).astype(BF)
    v_ref[:,vd:]=first_ref[...]

def full(a):
    return pl.BlockSpec(a.shape,lambda i:(0,)*a.ndim,pipeline_mode=pl.Buffered(1))

def project(x,first,g,b,bq,bv,w,blk=256):
    rows,d=x.shape
    rb=lambda n: pl.BlockSpec((blk,n),lambda i:(i,0))
    return pl.pallas_call(project_kernel,grid=(rows//blk,),
        in_specs=[rb(d),rb(first.shape[1]),full(g),full(b),full(bq),full(bv),full(w)],
        out_specs=[rb(d)]*4,out_shape=[jax.ShapeDtypeStruct((rows,d),BF)]*4,
        compiler_params=pltpu.CompilerParams(vmem_limit_bytes=48<<20),
        cost_estimate=pl.CostEstimate(flops=2*rows*w.shape[0]*w.shape[1],bytes_accessed=2*rows*d*5+w.size*2,transcendentals=0),
        name="project")(x,first,g,b,bq,bv,w)

C0=math.sqrt(2/math.pi)
def mlp_kernel(o_ref,x_ref,c_ref,bo_ref,g_ref,b_ref,bu_ref,bd_ref,wo_ref,wu_ref,wd_ref,
               out_ref,a_ref,y_ref,du_ref,dx_ref,dz_ref,do_ref,dbo_ref,dg_ref,db_ref,dbu_ref,dbd_ref,chunk=512):
    step=pl.program_id(0)
    @pl.when(step==0)
    def _():
        for r in (dbo_ref,dg_ref,db_ref,dbu_ref,dbd_ref): r[...]=jnp.zeros(r.shape,F32)
    ff=wu_ref.shape[1]
    x1=x_ref[...].astype(F32)+(nn(o_ref[...],wo_ref[...])+bo_ref[...])
    xh,rstd=row_stats(x1)
    a=(xh*g_ref[...]+b_ref[...]).astype(BF)
    a_ref[...]=a
    c=c_ref[...]
    acc=x1+bd_ref[...]
    da=jnp.zeros(acc.shape,F32)
    for s in range(0,ff,chunk):
        sl=slice(s,s+chunk)
        u=nn(a,wu_ref[:,sl])+bu_ref[:,sl]
        dy=nt(c,wd_ref[sl])
        u2=u*u
        t=jnp.tanh(u*(C0+(C0*0.044715)*u2))
        h=0.5*t+0.5
        y=(u*h).astype(BF)
        y_ref[:,sl]=y
        acc=acc+nn(y,wd_ref[sl])
        gd=h+(0.5*u)*(1.0-t*t)*(C0+(3*C0*0.044715)*u2)
        du=(gd*dy).astype(BF)
        du_ref[:,sl]=du
        dbu_ref[:,sl]+=du.astype(F32).sum(axis=0,keepdims=True)
        da=da+nt(du,wu_ref[:,sl])
    out_ref[...]=acc.astype(BF)
    c32=c.astype(F32)
    dbd_ref[...]+=c32.sum(axis=0,keepdims=True)
    db_ref[...]+=da.sum(axis=0,keepdims=True)
    dg_ref[...]+=(da*xh).sum(axis=0,keepdims=True)
    dxh=da*g_ref[...]
    dx=c32+rstd*(dxh-jnp.mean(dxh,axis=-1,keepdims=True)-xh*jnp.mean(dxh*xh,axis=-1,keepdims=True))
    dx_ref[...]=dx
    dz=dx.astype(BF)
    dz_ref[...]=dz
    dbo_ref[...]+=dz.astype(F32).sum(axis=0,keepdims=True)
    do_ref[...]=nt(dz,wo_ref[...]).astype(BF)

def mlp(o,x,c,bo,g,b,bu,bd,wo,wu,wd,blk=256):
    rows,d=x.shape; ff=wu.shape[1]
    rb=lambda n: pl.BlockSpec((blk,n),lambda i:(i,0))
    vec=lambda n: pl.BlockSpec((1,n),lambda i:(0,0))
    S=jax.ShapeDtypeStruct
    return pl.pallas_call(mlp_kernel,grid=(rows//blk,),
        in_specs=[rb(d)]*3+[full(t) for t in (bo,g,b,bu,bd,wo,wu,wd)],
        out_specs=[rb(d),rb(d),rb(ff),rb(ff),rb(d),rb(d),rb(d),vec(d),vec(d),vec(d),vec(ff),vec(d)],
        out_shape=[S((rows,d),BF),S((rows,d),BF),S((rows,ff),BF),S((rows,ff),BF),S((rows,d),F32),S((rows,d),BF),S((rows,d),BF),
                   S((1,d),F32),S((1,d),F32),S((1,d),F32),S((1,ff),F32),S((1,d),F32)],
        compiler_params=pltpu.CompilerParams(vmem_limit_bytes=56<<20),
        cost_estimate=pl.CostEstimate(flops=4*rows*(wo.size+2*wu.size),bytes_accessed=rows*(d*18+ff*4)+2*(wo.size+2*wu.size),transcendentals=rows*ff),
        name="feed_forward")(o,x,c,bo,g,b,bu,bd,wo,wu,wd)

def grad_kernel(where_ref,l_ref,r_ref,own_ref,sib_ref,lt_ref,*,planes,zs,piece):
    z=where_ref[0]; pn=where_ref[1]; core=where_ref[2]
    @pl.when(pl.program_id(0)==0)
    def _(): lt_ref[...]=l_ref[...].T
    acc=nn(lt_ref[...],r_ref[...])
    for dz in range(zs):
        for dp in range(planes):
            base=(dz*planes+dp)*2*piece
            sz=lax.rem(dz-z+zs,zs); sp=jnp.bitwise_xor(dp,pn)
            lo=acc[base:base+piece].astype(BF); hi=acc[base+piece:base+2*piece].astype(BF)
            own_ref[sp,sz]=jnp.where(core==0,lo,hi)
            sib_ref[sp,sz]=jnp.where(core==0,hi,lo)

def weight_grad(where,left,right,planes,zs,nblk,name):
    rows,m=left.shape; n=right.shape[1]
    piece=m//(planes*zs*2)
    S=jax.ShapeDtypeStruct
    ob=pl.BlockSpec((planes,zs,piece,nblk),lambda i:(0,0,0,i))
    return pl.pallas_call(functools.partial(grad_kernel,planes=planes,zs=zs,piece=piece),grid=(n//nblk,),
        in_specs=[pl.BlockSpec(memory_space=pltpu.SMEM),full(left),pl.BlockSpec((rows,nblk),lambda i:(0,i))],
        out_specs=[ob,ob],out_shape=[S((planes,zs,piece,n),BF)]*2,
        scratch_shapes=[pltpu.VMEM((m,rows),BF)],
        compiler_params=pltpu.CompilerParams(vmem_limit_bytes=56<<20),
        cost_estimate=pl.CostEstimate(flops=2*rows*m*n,bytes_accessed=2*(left.size+right.size+m*n),transcendentals=0),
        name=name)(where,left,right)

def last_kernel(dq_ref,dk_ref,df_ref,w_ref,x_ref,dx_ref,g_ref,gt_ref,dg_ref,db_ref,dbq_ref,dbv_ref):
    d=x_ref.shape[1]
    @pl.when(pl.program_id(0)==0)
    def _():
        for r in (dg_ref,db_ref,dbq_ref,dbv_ref): r[...]=jnp.zeros(r.shape,F32)
    dq=dq_ref[...]; df=df_ref[...]
    da=nt(dq,w_ref[:,0:d])+nt(dk_ref[...],w_ref[:,d:2*d])+nt(df,w_ref[:,2*d:])
    dbq_ref[...]+=dq.astype(F32).sum(axis=0,keepdims=True)
    dbv_ref[...]+=df.astype(F32).sum(axis=0,keepdims=True)
    xh,rstd=row_stats(x_ref[...].astype(F32))
    db_ref[...]+=da.sum(axis=0,keepdims=True)
    dg_ref[...]+=(da*xh).sum(axis=0,keepdims=True)
    dxh=da*g_ref[...]
    gt_ref[...]=(dx_ref[...]+rstd*(dxh-jnp.mean(dxh,axis=-1,keepdims=True)-xh*jnp.mean(dxh*xh,axis=-1,keepdims=True))).astype(BF)

def last(dq,dk,df,w,x,dx,g,blk=256):
    rows,d=x.shape; vd=df.shape[1]
    rb=lambda n: pl.BlockSpec((blk,n),lambda i:(i,0))
    vec=lambda n: pl.BlockSpec((1,n),lambda i:(0,0))
    S=jax.ShapeDtypeStruct
    return pl.pallas_call(last_kernel,grid=(rows//blk,),
        in_specs=[rb(d),rb(d),rb(vd),full(w),rb(d),rb(d),full(g)],
        out_specs=[rb(d),vec(d),vec(d),vec(d),vec(vd)],
        out_shape=[S((rows,d),BF),S((1,d),F32),S((1,d),F32),S((1,d),F32),S((1,vd),F32)],
        compiler_params=pltpu.CompilerParams(vmem_limit_bytes=48<<20),
        cost_estimate=pl.CostEstimate(flops=2*rows*w.size,bytes_accessed=rows*d*14+2*w.size,transcendentals=0),
        name="input_grad")(dq,dk,df,w,x,dx,g)

AXES=("dp","fsdp")


def place(mesh):
    return mesh.shape["dp"], mesh.shape["fsdp"]//2

def shift_dp(v,k,zs):
    return lax.ppermute(v,"dp",[(i,(i+k)%zs) for i in range(zs)])

def swap_plane(v,k,planes):
    return lax.ppermute(v,"fsdp",[(i,i^(2*k)) for i in range(2*planes)])

def swap_core(v,planes):
    return lax.ppermute(v,"fsdp",[(i,i^1) for i in range(2*planes)])

def assemble_kernel(where_ref,*refs,planes,zs,piece):
    out=refs[-1]
    z=where_ref[0]; pn=where_ref[1]; core=where_ref[2]
    for p in range(planes):
        for k in range(zs):
            chip=lax.rem(z-k+zs,zs)*planes+jnp.bitwise_xor(pn,p)
            own=refs[p][k].astype(F32); sib=refs[planes+p][k].astype(F32)
            lo=jnp.where(core==0,own,sib); hi=jnp.where(core==0,sib,own)
            row=pl.multiple_of(chip*(2*piece),2*piece)
            out[pl.ds(row,2*piece),:]=jnp.concatenate([lo,hi],axis=0).astype(BF)

def assemble(where,pieces,planes,zs,name):
    _,piece,n=pieces[0].shape
    nblk=n//2 if (n//2)%128==0 else n
    if n%384==0: nblk=384
    return pl.pallas_call(functools.partial(assemble_kernel,planes=planes,zs=zs,piece=piece),grid=(n//nblk,),
        in_specs=[pl.BlockSpec(memory_space=pltpu.SMEM)]+[pl.BlockSpec((zs,piece,nblk),lambda i:(0,0,i))]*(2*planes),
        out_specs=pl.BlockSpec((2*planes*zs*piece,nblk),lambda i:(0,i)),
        out_shape=jax.ShapeDtypeStruct((2*planes*zs*piece,n),BF),
        compiler_params=pltpu.CompilerParams(vmem_limit_bytes=48<<20),
        cost_estimate=pl.CostEstimate(flops=0,bytes_accessed=8*planes*zs*piece*n,transcendentals=0),
        name=name)(where,*pieces)

def gather_pieces(w,zs,planes):
    mine=jnp.stack([w]+[shift_dp(w,k,zs) for k in range(1,zs)])
    own=[mine]+[swap_plane(mine,k,planes) for k in range(1,planes)]
    return own+[swap_core(t,planes) for t in own]

def scatter_sum(own,sib,zs,planes):
    got=swap_core(sib,planes)
    part=[(own[p].astype(F32)+got[p].astype(F32)).astype(BF) for p in range(planes)]
    total=part[0].astype(F32)
    for p in range(1,planes):
        total=total+swap_plane(part[p],p,planes).astype(F32)
    mine=total[0]
    rest=total.astype(BF)
    for k in range(1,zs):
        mine=mine+shift_dp(rest[k],k,zs).astype(F32)
    return mine

def swapped(v,flag,axis):
    return jnp.where(flag,jnp.flip(v,axis),v)

def gather_vectors(v,planes,plane,core):
    own=[v]+[swap_plane(v,k,planes) for k in range(1,planes)]
    own=jnp.stack(own)
    both=jnp.stack([own,swap_core(own,planes)],axis=1)
    both=swapped(both,core==1,1)
    bits=planes.bit_length()-1
    both=both.reshape((2,)*bits+both.shape[1:])
    for b in range(bits):
        both=swapped(both,((plane>>(bits-1-b))&1)==1,b)
    return both.reshape(-1)

def sum_vectors(v,zs,planes,plane,core):
    n=v.shape[0]//(2*planes)
    bits=planes.bit_length()-1
    v=v.reshape((2,)*(bits+1)+(n,))
    for b in range(bits):
        v=swapped(v,((plane>>(bits-1-b))&1)==1,b)
    v=swapped(v,core==1,bits)
    v=v.reshape(planes,2,n)
    part=v[:,0]+swap_core(v[:,1],planes)
    total=part[0]
    for p in range(1,planes):
        total=total+swap_plane(part[p],p,planes)
    mine=total
    for k in range(1,zs):
        mine=mine+shift_dp(total,k,zs)
    return mine

def local(zs,planes,tokens,first_values,cotangent,lengths,vectors,w_qkv,w_out,w_up,w_down):
    d=tokens.shape[1]; vd=first_values.shape[1]; ff=w_up.shape[1]
    fine=w_qkv.shape[0]%8==0 and w_down.shape[0]%8==0 and planes&(planes-1)==0
    index=lax.axis_index("fsdp")
    z=lax.axis_index("dp"); plane=index//2; core=index%2
    where=jnp.stack([z,plane,core]).astype(jnp.int32)
    def gather(w,name):
        if fine:
            return assemble(where,gather_pieces(w,zs,planes),planes,zs,name)
        return lax.all_gather(w,AXES,axis=0,tiled=True)
    def scatter(left,right,nblk,name):
        if fine:
            own,sib=weight_grad(where,left,right,planes,zs,nblk,name)
            return scatter_sum(own,sib,zs,planes)
        return lax.psum_scatter(lax.dot_general(left,right,(((0,),(0,)),((),())),preferred_element_type=F32),AXES,scatter_dimension=0,tiled=True)
    if fine: whole=gather_vectors(vectors,planes,plane,core)
    else: whole=lax.all_gather(vectors,"fsdp",axis=0,tiled=True)
    pieces=[]; at=0
    for n in (d,d,d,vd,d,d,d,ff,d):
        pieces.append(whole[at:at+n].reshape(1,n)); at+=n
    g1,b1,bq,bv,bo,g2,b2,bu,bd=pieces
    f_qkv=gather(w_qkv,"whole_qkv")
    f_down=gather(w_down,"whole_down")
    both=lax.all_gather(jnp.concatenate([w_up,w_out],axis=1),AXES,axis=0,tiled=True)
    f_up=both[:,:ff]; f_out=both[:,ff:]
    a1,q,k,v=project(tokens,first_values,g1,b1,bq,bv,f_qkv)
    o,lse=attend_forward(lengths,q,k,v)
    output,a2,y,du,dx1,dz,do,dbo,dg2,db2,dbu,dbd=mlp(o,tokens,cotangent,bo,g2,b2,bu,bd,f_out,f_up,f_down)
    grad_down=scatter(y,cotangent,768,"down_grad")
    grad_up=scatter(a2,du,1024,"up_grad")
    grad_out=scatter(o,dz,768,"out_grad")
    dq,dk,df,gf=attend_backward(lengths,q,k,v,o,do,lse)
    grad_qkv=scatter(a1,jnp.concatenate([dq,dk,df],axis=1),640,"qkv_grad")
    grad_tokens,dg1,db1,dbq,dbv=last(dq,dk,df,f_qkv,tokens,dx1,g1)
    vec=jnp.concatenate([t.reshape(-1) for t in (dg1,db1,dbq,dbv,dbo,dg2,db2,dbu,dbd)])
    if fine: grad_vectors=sum_vectors(vec,zs,planes,plane,core)
    else:
        n=vectors.shape[0]
        grad_vectors=lax.dynamic_slice_in_dim(lax.psum(vec,AXES),index*n,n,0)
    return output,grad_tokens,gf,grad_vectors,grad_qkv,grad_out,grad_up,grad_down

def solution(mesh):
    zs,planes=place(mesh)
    rows=P(AXES,None)
    return jax.shard_map(functools.partial(local,zs,planes),mesh=mesh,
        in_specs=(rows,rows,rows,rows,P("fsdp"),rows,rows,rows,rows),
        out_specs=(rows,rows,rows,P("fsdp"),rows,rows,rows,rows),check_vma=False)
```

```python
import functools
import math

import jax
import jax.numpy as jnp
from jax import lax
from jax.experimental import pallas as pl
from jax.experimental.pallas import tpu as pltpu
from jax.sharding import PartitionSpec as P

BF = jnp.bfloat16
F32 = jnp.float32
HD = 64
EPSILON = 1e-5
HIDDEN = -1e30
AXES = ("dp", "fsdp")
GELU = math.sqrt(2 / math.pi)
CUBE = 0.044715
MIB = 1 << 20
VMEM = 60
PACE = 0.01


def nn(a, b):
    return jnp.dot(a, b, preferred_element_type=F32)


def nt(a, b):
    return lax.dot_general(a, b, (((1,), (1,)), ((), ())), preferred_element_type=F32)


def tn(a, b):
    return lax.dot_general(a, b, (((0,), (0,)), ((), ())), preferred_element_type=F32)


def shape_of(shape, dtype=BF):
    return jax.ShapeDtypeStruct(shape, dtype)


def whole(a):
    return pl.BlockSpec(a.shape, lambda i: (0,) * a.ndim, pipeline_mode=pl.Buffered(1))


def kept(a):
    return pl.BlockSpec(a.shape, lambda *at: (0,) * a.ndim, pipeline_mode=pl.Buffered(1))


def rows_of(blk, n):
    return pl.BlockSpec((blk, n), lambda i: (i, 0))


def vector_of(n):
    return pl.BlockSpec((1, n), lambda i: (0, 0))


SCALARS = pl.BlockSpec(memory_space=pltpu.SMEM)


class Chain:
    def __init__(self):
        self.mark = None

    def call(
        self, kernel, args, *, grid, in_specs, out_specs, out_shape, vmem, cost, waits=(), scalars=0,
        scratch_shapes=(), name=None,
    ):
        several = isinstance(out_shape, (list, tuple))
        out_specs = list(out_specs) if several else [out_specs]
        out_shape = list(out_shape) if several else [out_shape]
        deps = ([] if self.mark is None else [self.mark]) + list(waits)
        used, extra, outs = len(args), len(deps), len(out_shape)

        def body(*refs):
            results = used + extra
            mark = refs[results + outs]
            mark[...] = jnp.zeros(mark.shape, mark.dtype)
            kernel(*refs[:used], *refs[results : results + outs], *refs[results + outs + 1 :])

        got = pl.pallas_call(
            body,
            grid_spec=pltpu.PrefetchScalarGridSpec(
                num_scalar_prefetch=scalars,
                grid=grid,
                in_specs=list(in_specs) + [pl.BlockSpec(memory_space=pl.ANY)] * extra,
                out_specs=out_specs + [pl.BlockSpec((8, 128), lambda *at: (0, 0))],
                scratch_shapes=list(scratch_shapes),
            ),
            out_shape=out_shape + [shape_of((8, 128), F32)],
            compiler_params=pltpu.CompilerParams(vmem_limit_bytes=vmem * MIB),
            cost_estimate=pl.CostEstimate(
                flops=int(cost * PACE * 1.15e9), bytes_accessed=int(cost * PACE * 3.69e6), transcendentals=0
            ),
            name=name,
        )(*args, *deps)
        self.mark = got[-1]
        return got[:-1] if several else got[0]


def half_mask(head):
    return (lax.broadcasted_iota(jnp.int32, (1, 2 * HD), 1) // HD) == head


def causal_tile(blk):
    key = lax.broadcasted_iota(jnp.int32, (blk, blk), 0)
    return key <= lax.broadcasted_iota(jnp.int32, (blk, blk), 1)


def attend_forward_kernel(len_ref, q_ref, k_ref, v_ref, o_ref, lse_ref, ot_ref):
    rows = q_ref.shape[0]
    blk, half = 256, rows // 2
    bias = jnp.where(len_ref[0, 0] < rows, HIDDEN, 0.0).astype(F32)
    vt = v_ref[...].T
    causal = causal_tile(blk)
    for head in range(2):
        hs = slice(HD * head, HD * head + HD)
        vth = vt[hs]
        for i in range(rows // blk):
            at = slice(i * blk, (i + 1) * blk)
            q = jnp.where(half_mask(head), q_ref[at], jnp.zeros((), BF))
            parts = []
            for j in range(i + 1):
                s = nt(k_ref[j * blk : (j + 1) * blk], q)
                if j == i:
                    s = jnp.where(causal, s, HIDDEN)
                elif i * blk >= half and (j + 1) * blk <= half:
                    s = s + bias
                parts.append(s)
            m = parts[0].max(axis=0, keepdims=True)
            for s in parts[1:]:
                m = jnp.maximum(m, s.max(axis=0, keepdims=True))
            total = jnp.zeros((1, blk), F32)
            mixed = jnp.zeros((HD, blk), F32)
            for j, s in enumerate(parts):
                p = jnp.exp(s - m)
                total = total + p.sum(axis=0, keepdims=True)
                mixed = mixed + nn(vth[:, j * blk : (j + 1) * blk], p.astype(BF))
            ot_ref[hs, at] = mixed / total
            lse_ref[0, head : head + 1, at] = m + jnp.log(total)
    o_ref[...] = ot_ref[...].T.astype(BF)


def attend_forward(chain, lengths, q, k, v, first, count):
    rows = q.shape[0]
    pair = pl.BlockSpec((rows, 2 * HD), lambda p: (0, p + first))
    out = pl.BlockSpec((rows, 2 * HD), lambda p: (0, p))
    return chain.call(
        attend_forward_kernel,
        (lengths, q, k, v),
        grid=(count,),
        in_specs=[SCALARS, pair, pair, pair],
        out_specs=[out, pl.BlockSpec((1, 2, rows), lambda p: (p, 0, 0))],
        out_shape=[shape_of((rows, count * 2 * HD)), shape_of((count, 2, rows), F32)],
        scratch_shapes=[pltpu.VMEM((2 * HD, rows), F32)],
        vmem=VMEM,
        cost=3.5 * count,
        name="attend_forward",
    )


def attend_backward_kernel(
    len_ref, q_ref, k_ref, v_ref, o_ref, do_ref, lse_ref,
    dq_ref, dk_ref, dv_ref, dqt_acc, dv_acc, dk_acc,
):
    rows = q_ref.shape[0]
    blk, half = 256, rows // 2
    nb = rows // blk
    bias = jnp.where(len_ref[0, 0] < rows, HIDDEN, 0.0).astype(F32)
    prod = (do_ref[...].astype(F32) * o_ref[...].astype(F32)).T
    kt = k_ref[...].T
    causal = causal_tile(blk)
    for head in range(2):
        hs = slice(HD * head, HD * head + HD)
        delta = prod[hs].sum(axis=0, keepdims=True)
        lse = lse_ref[0, head : head + 1, :]
        qh = jnp.where(half_mask(head), q_ref[...], jnp.zeros((), BF))
        doh = jnp.where(half_mask(head), do_ref[...], jnp.zeros((), BF))
        for j in range(nb):
            kr = slice(j * blk, (j + 1) * blk)
            kj, vj, ktj = k_ref[kr], v_ref[kr], kt[hs, kr]
            dv = jnp.zeros((blk, 2 * HD), F32)
            dk = jnp.zeros((blk, 2 * HD), F32)
            for i in range(j, nb):
                at = slice(i * blk, (i + 1) * blk)
                s = nt(kj, qh[at])
                if i == j:
                    s = jnp.where(causal, s, HIDDEN)
                elif i * blk >= half and (j + 1) * blk <= half:
                    s = s + bias
                p = jnp.exp(s - lse[:, at])
                dp = nt(vj, doh[at])
                ds = (p * (dp - delta[:, at])).astype(BF)
                dv = dv + nn(p.astype(BF), doh[at])
                dk = dk + nn(ds, qh[at])
                dqt = nn(ktj, ds)
                if j == 0:
                    dqt_acc[hs, at] = dqt
                else:
                    dqt_acc[hs, at] += dqt
            if head == 0:
                dv_acc[kr] = dv
                dk_acc[kr] = dk
            else:
                dv_acc[kr] += dv
                dk_acc[kr] += dk
    dq_ref[...] = (dqt_acc[...].T * 0.125).astype(BF)
    dk_ref[...] = dk_acc[...].astype(BF)
    dv_ref[...] = dv_acc[...].astype(BF)


def attend_backward(chain, lengths, q, k, v, o, do, lse, first, waits=()):
    rows, width = o.shape
    count = lse.shape[0]
    pair = pl.BlockSpec((rows, 2 * HD), lambda p: (0, p + first))
    part = pl.BlockSpec((rows, 2 * HD), lambda p: (0, p))
    return chain.call(
        attend_backward_kernel,
        (lengths, q, k, v, o, do, lse),
        grid=(count,),
        in_specs=[SCALARS, pair, pair, pair, part, pair, pl.BlockSpec((1, 2, rows), lambda p: (p, 0, 0))],
        out_specs=[part] * 3,
        out_shape=[shape_of((rows, width))] * 3,
        scratch_shapes=[
            pltpu.VMEM((2 * HD, rows), F32),
            pltpu.VMEM((rows, 2 * HD), F32),
            pltpu.VMEM((rows, 2 * HD), F32),
        ],
        vmem=VMEM,
        cost=6 * count,
        waits=waits,
        name="attend_backward",
    )


def row_stats(v):
    center = v - jnp.mean(v, axis=-1, keepdims=True)
    rstd = lax.rsqrt(jnp.mean(center * center, axis=-1, keepdims=True) + EPSILON)
    return center * rstd, rstd


def norm_back(grad, unit, rstd, gain):
    g = grad * gain
    return rstd * (
        g - jnp.mean(g, axis=-1, keepdims=True) - unit * jnp.mean(g * unit, axis=-1, keepdims=True)
    )


def column_sum(v):
    return v.astype(F32).sum(axis=0, keepdims=True)


def clear(*refs):
    @pl.when(pl.program_id(0) == 0)
    def _():
        for r in refs:
            r[...] = jnp.zeros(r.shape, r.dtype)


def vector_parts(ref, d, vd):
    ff = ref.shape[1] - 7 * d - vd
    parts, at = [], 0
    for n in (d, d, d, vd, d, d, d, ff, d):
        parts.append(ref.at[:, at : at + n])
        at += n
    return parts


def project_kernel(*refs, pieces, load):
    if load:
        where_ref, *side = refs[: 2 * pieces + 1]
        x_ref, first_ref, vec_ref, a_ref, q_ref, k_ref, v_ref, w_ref, acc_ref = refs[2 * pieces + 1 :]

        @pl.when(pl.program_id(0) == 0)
        def _():
            load(where_ref, side[:pieces], side[pieces:], (w_ref,), (acc_ref,))
    else:
        x_ref, first_ref, vec_ref, w_ref, a_ref, q_ref, k_ref, v_ref = refs
    d, vd = x_ref.shape[1], first_ref.shape[1]
    g_ref, b_ref, bq_ref, bv_ref = vector_parts(vec_ref, d, vd)[:4]
    unit, _ = row_stats(x_ref[...].astype(F32))
    a = (unit * g_ref[...] + b_ref[...]).astype(BF)
    a_ref[...] = a
    q = (nn(a, w_ref[:, 0:d]) + bq_ref[...]).astype(BF)
    q_ref[...] = (q.astype(F32) * 0.125).astype(BF)
    k_ref[...] = nn(a, w_ref[:, d : 2 * d]).astype(BF)
    v_ref[:, 0:vd] = (nn(a, w_ref[:, 2 * d :]) + bv_ref[...]).astype(BF)
    v_ref[:, vd:] = first_ref[...]


def project(chain, x, first, vec, w, where=None, blk=256):
    rows, d = x.shape
    pieces = w is not None and where is not None
    args, specs = (x, first, vec), [rows_of(blk, d), rows_of(blk, first.shape[1]), whole(vec)]
    outs, shapes, scratch = [rows_of(blk, d)] * 4, [shape_of((rows, d))] * 4, []
    count = 0
    if pieces:
        own, sib = w
        count = len(own)
        _, _, r, n = own[0].shape
        args = (where, *own, *sib) + args
        specs = [SCALARS] + [kept(t) for t in (*own, *sib)] + specs
        outs = outs + [pl.BlockSpec((32 * r, n), lambda i: (0, 0))]
        shapes = shapes + [shape_of((32 * r, n))]
        scratch = [pltpu.VMEM((32 * r, n), F32)]
    else:
        args, specs = args + (w,), specs + [whole(w)]
    return chain.call(
        functools.partial(project_kernel, pieces=count, load=load_weights if pieces else None),
        args,
        grid=(rows // blk,),
        in_specs=specs,
        out_specs=outs,
        out_shape=shapes,
        scratch_shapes=scratch,
        vmem=VMEM,
        cost=8,
        name="project",
    )


def feed_kernel(*refs, pieces, load, chunk=512):
    if load:
        where_ref, *side = refs[: 2 * pieces + 1]
        (
            oa_ref, ob_ref, x_ref, c_ref, vec_ref, wu_ref, x1_ref, a_ref, y_ref, du_ref, dx_ref, dz_ref, do_ref,
            dbo_ref, dg_ref, db_ref, dbu_ref, dbd_ref, wd_ref, wo_ref, acc_d, acc_o,
        ) = refs[2 * pieces + 1 :]

        @pl.when(pl.program_id(0) == 0)
        def _():
            load(where_ref, side[:pieces], side[pieces:], (wd_ref, wo_ref), (acc_d, acc_o))
    else:
        (
            oa_ref, ob_ref, x_ref, c_ref, vec_ref, wu_ref, wd_ref, wo_ref, x1_ref, a_ref, y_ref, du_ref, dx_ref,
            dz_ref, do_ref, dbo_ref, dg_ref, db_ref, dbu_ref, dbd_ref,
        ) = refs
    clear(dbo_ref, dg_ref, db_ref, dbu_ref, dbd_ref)
    d, ff = wu_ref.shape
    bo_ref, g_ref, b_ref, bu_ref = vector_parts(vec_ref, d, vec_ref.shape[1] - 7 * d - ff)[4:8]
    half = oa_ref.shape[1]
    mixed = nn(oa_ref[...], wo_ref[0:half]) + nn(ob_ref[...], wo_ref[half:])
    x1 = x_ref[...].astype(F32) + (mixed + bo_ref[...])
    x1_ref[...] = x1
    unit, rstd = row_stats(x1)
    a = (unit * g_ref[...] + b_ref[...]).astype(BF)
    a_ref[...] = a
    c = c_ref[...]
    da = jnp.zeros(x1.shape, F32)
    for s in range(0, wu_ref.shape[1], chunk):
        at = slice(s, s + chunk)
        u = nn(a, wu_ref[:, at]) + bu_ref[:, at]
        dy = nt(c, wd_ref[at])
        u2 = u * u
        t = jnp.tanh(u * (GELU + (GELU * CUBE) * u2))
        h = 0.5 * t + 0.5
        y_ref[:, at] = (u * h).astype(BF)
        slope = h + (0.5 * u) * (1.0 - t * t) * (GELU + (3 * GELU * CUBE) * u2)
        du = (slope * dy).astype(BF)
        du_ref[:, at] = du
        dbu_ref[:, at] += column_sum(du)
        da = da + nt(du, wu_ref[:, at])
    c32 = c.astype(F32)
    dbd_ref[...] += column_sum(c)
    db_ref[...] += column_sum(da)
    dg_ref[...] += column_sum(da * unit)
    dx = c32 + norm_back(da, unit, rstd, g_ref[...])
    dx_ref[...] = dx
    dz = dx.astype(BF)
    dz_ref[...] = dz
    dbo_ref[...] += column_sum(dz)
    do_ref[...] = nt(dz, wo_ref[...]).astype(BF)


def feed(chain, oa, ob, x, c, vec, wu, wd, wo, where=None, blk=256):
    rows, d = x.shape
    ff = wu.shape[1]
    args = (oa, ob, x, c, vec, wu)
    specs = [rows_of(blk, t.shape[1]) for t in args[:4]] + [whole(vec), whole(wu)]
    outs = [rows_of(blk, n) for n in (d, d, ff, ff, d, d, d)] + [vector_of(n) for n in (d, d, d, ff, d)]
    shapes = [
        shape_of((rows, d), F32), shape_of((rows, d)), shape_of((rows, ff)), shape_of((rows, ff)),
        shape_of((rows, d), F32), shape_of((rows, d)), shape_of((rows, d)),
    ] + [shape_of((1, n), F32) for n in (d, d, d, ff, d)]
    scratch, count = [], 0
    if where is not None:
        count = len(wd)
        args = (where, *wd, *wo) + args
        specs = [SCALARS] + [kept(t) for t in (*wd, *wo)] + specs
        outs = outs + [pl.BlockSpec((ff, d), lambda i: (0, 0))]
        shapes = shapes + [shape_of((ff, d))]
        scratch = [pltpu.VMEM((d, d), BF), pltpu.VMEM((ff, d), F32), pltpu.VMEM((d, d), F32)]
    else:
        args, specs = args + (wd, wo), specs + [whole(wd), whole(wo)]
    return chain.call(
        functools.partial(feed_kernel, pieces=count, load=load_weights if count else None),
        args,
        grid=(rows // blk,),
        in_specs=specs,
        out_specs=outs,
        out_shape=shapes,
        scratch_shapes=scratch,
        vmem=VMEM,
        cost=31,
        name="feed_forward",
    )


def output_kernel(y_ref, x1_ref, vec_ref, wd_ref, out_ref, acc_ref):
    step = pl.program_id(0)

    @pl.when(step == 0)
    def _():
        acc_ref[...] = x1_ref[...] + vec_ref[:, vec_ref.shape[1] - x1_ref.shape[1] :]

    acc_ref[...] += nn(y_ref[...], wd_ref[...])

    @pl.when(step == pl.num_programs(0) - 1)
    def _():
        out_ref[...] = acc_ref[...].astype(BF)


def final_output(chain, y, x1, vec, wd, waits=(), blk=768):
    rows, ff = y.shape
    d = x1.shape[1]
    return chain.call(
        output_kernel,
        (y, x1, vec, wd),
        grid=(ff // blk,),
        in_specs=[pl.BlockSpec((rows, blk), lambda i: (0, i)), whole(x1), whole(vec), rows_of(blk, d)],
        out_specs=pl.BlockSpec((rows, d), lambda i: (0, 0)),
        out_shape=shape_of((rows, d)),
        scratch_shapes=[pltpu.VMEM((rows, d), F32)],
        waits=waits,
        vmem=VMEM,
        cost=8,
        name="output",
    )


def input_kernel(
    where_ref, dqa_ref, dqb_ref, dka_ref, dkb_ref, df_ref, w_ref, x_ref, dx_ref, vec_ref,
    dbo_ref, dg2_ref, db2_ref, dbu_ref, dbd_ref, gt_ref, *rest, split,
):
    dvec_ref = rest[-1]
    clear(dvec_ref)
    half = dqa_ref.shape[1]
    d = x_ref.shape[1]
    dg, db, dbq, dbv, dbo, dg2, db2, dbu, dbd = vector_parts(dvec_ref, d, half)
    terms = (dqa_ref[...], dqb_ref[...], dka_ref[...], dkb_ref[...], df_ref[...])
    da = jnp.zeros(x_ref.shape, F32)
    for n, t in enumerate(terms):
        da = da + nt(t, w_ref[:, n * half : (n + 1) * half])
    dbq[:, 0:half] += column_sum(terms[0])
    dbq[:, half:] += column_sum(terms[1])
    dbv[...] += column_sum(terms[4])
    unit, rstd = row_stats(x_ref[...].astype(F32))
    db[...] += column_sum(da)
    dg[...] += column_sum(da * unit)
    gt_ref[...] = (dx_ref[...] + norm_back(da, unit, rstd, vec_ref[:, 0:d])).astype(BF)

    @pl.when(pl.program_id(0) == pl.num_programs(0) - 1)
    def _():
        for ref, known in ((dbo, dbo_ref), (dg2, dg2_ref), (db2, db2_ref), (dbu, dbu_ref), (dbd, dbd_ref)):
            ref[...] = known[...]
        if not split:
            rest[0][...] = dvec_ref[...]
            return
        plane, core = where_ref[1], where_ref[2]
        n = rest[0].shape[1]
        parts = [dvec_ref[:, f * n : (f + 1) * n] for f in range(8)]
        for side, out in enumerate(rest[:2]):
            for r in range(4):
                f = jnp.bitwise_xor(plane, r) * 2 + (core if side == 0 else 1 - core)
                v = parts[0]
                for g in range(1, 8):
                    v = jnp.where(f == g, parts[g], v)
                out[r : r + 1, :] = v


def input_grad(chain, where, terms, w, x, dx, vec, known, split, waits=(), blk=256):
    rows, d = x.shape
    half = terms[0].shape[1]
    n = vec.shape[1]
    vecs = [(4, n // 8)] * 2 if split else [(1, n)]
    return chain.call(
        functools.partial(input_kernel, split=split),
        (where, *terms, w, x, dx, vec, *known),
        grid=(rows // blk,),
        in_specs=[SCALARS] + [rows_of(blk, half)] * 5 + [whole(w), rows_of(blk, d), rows_of(blk, d)]
        + [whole(t) for t in (vec, *known)],
        out_specs=[rows_of(blk, d)] + [pl.BlockSpec(t, lambda i: (0, 0)) for t in vecs],
        out_shape=[shape_of((rows, d))] + [shape_of(t, F32) for t in vecs],
        scratch_shapes=[pltpu.VMEM((1, n), F32)],
        waits=waits,
        vmem=VMEM,
        cost=9,
        name="input_grad",
    )


def flipped(r):
    return 2 * lax.rem(r, 2) + lax.div(r, 2)


def gathered_slot(r, core):
    return jnp.where(core == 0, r, flipped(r))


def summed_slot(r, core):
    return jnp.where(core == 0, flipped(r), r)


def plane_step(v, step):
    return lax.ppermute(v, "fsdp", [(i, i ^ (2 if i % 2 == step else 4)) for i in range(8)])


def depth_step(v, step):
    pairs = [(i, i ^ (8 if i % 2 == step else 16)) for i in range(32)]
    return lax.ppermute(v, AXES, pairs)


def depth_swap(v, bits):
    return lax.ppermute(v, "dp", [(i, i ^ bits) for i in range(4)])


def fsdp_swap(v, bit):
    return lax.ppermute(v, "fsdp", [(i, i ^ bit) for i in range(8)])


def core_step(v):
    return fsdp_swap(v, 1)


def resident(a):
    return pl.BlockSpec(a.shape, lambda *at: (0,) * a.ndim)


def pack(chain, groups, waits=()):
    count = sum(len(g) for g in groups)

    def kernel(*refs):
        at = 0
        for g, out in zip(groups, refs[count:]):
            row = 0
            for part in g:
                out[row : row + part.shape[0]] = refs[at][...]
                row += part.shape[0]
                at += 1

    shapes = [shape_of((sum(p.shape[0] for p in g), *g[0].shape[1:]), g[0].dtype) for g in groups]
    return chain.call(
        kernel,
        [p for g in groups for p in g],
        grid=(1,),
        in_specs=[resident(p) for g in groups for p in g],
        out_specs=[resident(t) for t in shapes],
        out_shape=shapes,
        waits=waits,
        vmem=8,
        cost=1,
        name="pack",
    )


def load_weights(where_ref, own, sib, outs, accs):
    z, plane, core = where_ref[0], where_ref[1], where_ref[2]
    rows = own[0].shape[2]
    for side, group in enumerate((own, sib)):
        half = core if side == 0 else 1 - core
        for rp, ref in enumerate(group):
            for rz in range(ref.shape[0]):
                chip = jnp.bitwise_xor(z, rz) * 4 + jnp.bitwise_xor(plane, gathered_slot(rp, half))
                q = 0
                for acc in accs:
                    part = acc.shape[0] // (32 * rows)
                    base = (chip * 2 + half) * (part * rows)
                    for r in range(part):
                        acc[pl.ds(pl.multiple_of(base + r * rows, 8), rows), :] = ref[rz, q].astype(F32)
                        q += 1
    for out, acc in zip(outs, accs):
        out[...] = acc[...].astype(BF)


class Sum:
    def __init__(self, own):
        self.terms = [own]

    def upper(self, got):
        self.terms.append(got)
        n = got.shape[0]
        send = sum(t[n // 2 : n].astype(F32) for t in self.terms).astype(BF)
        return send

    def total(self, got):
        return sum(t[0].astype(F32) for t in self.terms + [got])


def hand_out(where_ref, acc, piece, own_ref, sib_ref):
    z, plane, core = where_ref[0], where_ref[1], where_ref[2]
    n = 0
    for zd in range(4):
        for pd in range(4):
            rz, rp = jnp.bitwise_xor(z, zd), jnp.bitwise_xor(plane, pd)
            lo, hi = acc[n : n + piece].astype(BF), acc[n + piece : n + 2 * piece].astype(BF)
            own_ref[summed_slot(rp, core) * 4 + summed_slot(rz, core), 0] = jnp.where(core == 0, lo, hi)
            sib_ref[summed_slot(rp, 1 - core) * 4 + summed_slot(rz, 1 - core), 0] = jnp.where(core == 0, hi, lo)
            n += 2 * piece


def wide_grad(chain, where, left, rights, blk, name, waits=()):
    rows, m = left.shape
    piece = m // 32
    each = rights[0].shape[1] // blk
    steps = each * len(rights)

    def kernel(where_ref, l_ref, *refs):
        r_refs, (own_ref, sib_ref, lt_ref, r_all) = refs[: len(rights)], refs[len(rights) :]
        step = pl.program_id(0)

        @pl.when(step == 0)
        def _():
            lt_ref[...] = l_ref[...].T

        if len(rights) == 1:
            right = r_refs[0][...]
        else:
            for n, ref in enumerate(r_refs):

                @pl.when(step == n)
                def _(ref=ref):
                    r_all[...] = ref[...]

            right = r_all[...]
        hand_out(where_ref, nn(lt_ref[...], right), piece, own_ref, sib_ref)

    right_spec = pl.BlockSpec((rows, blk), lambda i: (0, i)) if len(rights) == 1 else whole(rights[0])
    block = pl.BlockSpec((16, 1, piece, blk), lambda i: (0, i, 0, 0))
    return chain.call(
        kernel,
        (where, left, *rights),
        grid=(steps,),
        in_specs=[SCALARS, whole(left)] + [right_spec] * len(rights),
        out_specs=[block, block],
        out_shape=[shape_of((16, steps, piece, blk))] * 2,
        scratch_shapes=[pltpu.VMEM((m, rows), BF), pltpu.VMEM((rows, blk), BF)],
        waits=waits,
        vmem=VMEM,
        cost=9,
        name=name,
    )


def tall_grad_kernel(where_ref, y_ref, c_ref, oa_ref, ob_ref, dz_ref, own_ref, sib_ref, acc_ref, out_ref):
    step = pl.program_id(0)
    tall = y_ref.shape[1] // 8
    half = oa_ref.shape[1]
    flat = half // 16

    @pl.when(step == 0)
    def _():
        out_ref[0:half] = tn(oa_ref[...], dz_ref[...])
        out_ref[half:] = tn(ob_ref[...], dz_ref[...])

    acc_ref[...] = tn(y_ref[...], c_ref[...])
    plane, core = where_ref[1], where_ref[2]
    base = step * (8 * flat)
    for pd in range(4):
        rp = jnp.bitwise_xor(plane, pd)
        mine, other = summed_slot(rp, core), summed_slot(rp, 1 - core)

        def put(lo, hi, q):
            lo, hi = lo.astype(BF), hi.astype(BF)
            own_ref[mine, 0, q] = jnp.where(core == 0, lo, hi)
            sib_ref[other, 0, q] = jnp.where(core == 0, hi, lo)

        for q in range(tall // flat):
            n = 2 * tall * pd + flat * q
            put(acc_ref[n : n + flat], acc_ref[n + tall : n + tall + flat], q)
        n = pl.multiple_of(base + 2 * flat * pd, 8)
        put(out_ref[pl.ds(n, flat)], out_ref[pl.ds(n + flat, flat)], tall // flat)


def tall_grad(chain, where, y, c, oa, ob, dz):
    rows, ff = y.shape
    d = c.shape[1]
    piece = d // 32
    chunks = ff // d + 1

    def slot(flip):
        def index(i, where_ref):
            core = where_ref[2]
            return (0, summed_slot(jnp.bitwise_xor(i, where_ref[0]), 1 - core if flip else core), 0, 0, 0)

        return pl.BlockSpec((4, 1, chunks, piece, d), index)

    own, sib = chain.call(
        tall_grad_kernel,
        (where, y, c, oa, ob, dz),
        scalars=1,
        grid=(4,),
        in_specs=[pl.BlockSpec((rows, ff // 4), lambda i, w: (0, i)), kept(c), kept(oa), kept(ob), kept(dz)],
        out_specs=[slot(False), slot(True)],
        out_shape=[shape_of((4, 4, chunks, piece, d))] * 2,
        scratch_shapes=[pltpu.VMEM((ff // 4, d), F32), pltpu.VMEM((d, d), F32)],
        vmem=VMEM,
        cost=12.5,
        name="down_out_grad",
    )
    return own.reshape(16, chunks, piece, d), sib.reshape(16, chunks, piece, d)


def arrange_vectors(chain, where, parts):
    n = parts.shape[1]

    def kernel(where_ref, p_ref, out_ref):
        me = where_ref[1] * 2 + where_ref[2]
        for f in range(8):
            rel = jnp.bitwise_xor(me, f)
            v = p_ref[0:1, :]
            for r in range(1, 8):
                row = (r % 2) * 4 + (r // 4) * 2 + (r // 2) % 2
                v = jnp.where(rel == r, p_ref[row : row + 1, :], v)
            out_ref[:, f * n : (f + 1) * n] = v

    return chain.call(
        kernel,
        (where, parts),
        grid=(1,),
        in_specs=[SCALARS, resident(parts)],
        out_specs=vector_of(8 * n),
        out_shape=shape_of((1, 8 * n), F32),
        vmem=8,
        cost=1,
        name="arrange_vectors",
    )


def after(values, *deps):
    return lax.optimization_barrier((values, deps))[0]


def whole_gather(w, axes=AXES):
    return lax.all_gather(w, axes, axis=0, tiled=True)


def general(tokens, first_values, cotangent, lengths, vectors, w_qkv, w_out, w_up, w_down):
    d = tokens.shape[1]
    chain = Chain()
    scatter = lambda g: lax.psum_scatter(g, AXES, scatter_dimension=0, tiled=True)
    vec = whole_gather(vectors, "fsdp").reshape(1, -1)
    f_qkv, f_out, f_up, f_down = (whole_gather(w) for w in (w_qkv, w_out, w_up, w_down))
    where = jnp.zeros((3,), jnp.int32)
    a1, q, k, v = project(chain, tokens, first_values, vec, f_qkv)
    n = d // (4 * HD)
    oa, la = attend_forward(chain, lengths, q, k, v, 0, n)
    ob, lb = attend_forward(chain, lengths, q, k, v, n, n)
    x1, a2, y, du, dx1, dz, do, *known = feed(chain, oa, ob, tokens, cotangent, vec, f_up, f_down, f_out)
    output = final_output(chain, y, x1, vec, f_down)
    dqa, dka, df = attend_backward(chain, lengths, q, k, v, oa, do, la, 0)
    dqb, dkb, dfirst = attend_backward(chain, lengths, q, k, v, ob, do, lb, n)
    terms = (dqa, dqb, dka, dkb, df)
    grad_tokens, dvec = input_grad(chain, where, terms, f_qkv, tokens, dx1, vec, known, False)
    n = vectors.shape[0]
    grad_vectors = lax.dynamic_slice_in_dim(lax.psum(dvec[0], AXES), lax.axis_index("fsdp") * n, n, 0)
    return (
        output, grad_tokens, dfirst, grad_vectors,
        scatter(tn(a1, jnp.concatenate(terms, axis=1))), scatter(jnp.concatenate([tn(oa, dz), tn(ob, dz)], axis=0)), scatter(tn(a2, du)), scatter(tn(y, cotangent)),
    )


def local(tokens, first_values, cotangent, lengths, vectors, w_qkv, w_out, w_up, w_down):
    d = tokens.shape[1]
    index = lax.axis_index("fsdp")
    plane, core = lax.div(index, 2), lax.rem(index, 2)
    where = jnp.stack([lax.axis_index("dp"), plane, core]).astype(jnp.int32)
    piece = w_qkv.shape[0]
    tall = w_down.shape[0] // piece
    chain = Chain()

    f_up = whole_gather(w_up)
    m = w_qkv[None, None]
    m = jnp.concatenate([m] + [depth_swap(m, bits) for bits in (1, 2, 3)], axis=0)
    near, side = plane_step(m, 0), plane_step(m, 1)
    md = jnp.concatenate([w_down.reshape(tall, piece, d), w_out[None]], axis=0)[None]
    md, vec = after((md, vectors[None]), m)
    got_vec = fsdp_swap(vec, 2)
    deep = [depth_swap(md, 1), depth_swap(md, 3)]
    m, near, side, got_vec, md, deep = after((m, near, side, got_vec, md, deep))
    far = plane_step(near, 1)
    sib = [core_step(t) for t in (m, near, side)]
    vec = jnp.concatenate([vec, got_vec], axis=0)
    got_vec = fsdp_swap(vec, 4)
    deep = [md, deep[0], depth_swap(md, 2), deep[1]]
    far, sib, got_vec, deep = after((far, sib, got_vec, deep))
    sib = sib + [core_step(far)]
    md = jnp.concatenate(deep, axis=0)
    near_d, side_d = plane_step(md, 0), plane_step(md, 1)
    vec = jnp.concatenate([vec, got_vec], axis=0)
    vec = arrange_vectors(chain, where, jnp.concatenate([vec, core_step(vec)], axis=0))
    a1, q, k, v, f_qkv = project(chain, tokens, first_values, vec, ([m, near, side, far], sib), where)
    n = d // (4 * HD)
    oa, la = attend_forward(chain, lengths, q, k, v, 0, n)
    md, near_d, side_d = after((md, near_d, side_d), oa)
    far_d = plane_step(near_d, 1)
    sib_d = [core_step(t) for t in (md, near_d, side_d)]
    ob, lb = attend_forward(chain, lengths, q, k, v, n, n)
    far_d, sib_d = after((far_d, sib_d), ob)
    sib_d = sib_d + [core_step(far_d)]
    f_up, sib_d = after((f_up, sib_d))
    x1, a2, y, du, dx1, dz, do, *known, f_down = feed(
        chain, oa, ob, tokens, cotangent, vec, f_up, [md, near_d, side_d, far_d], sib_d, where
    )

    own_d, sib_d = tall_grad(chain, where, y, cotangent, oa, ob, dz)
    got_d = core_step(sib_d)
    own_u, sib_u = wide_grad(chain, where, a2, [du], d, "up_grad")
    got_u = core_step(sib_u)
    sum_d, sum_u = Sum(own_d), Sum(own_u)
    send_d = sum_d.upper(after(got_d, own_u))
    got_d = plane_step(send_d, 0)
    dqa, dka, df = attend_backward(chain, lengths, q, k, v, oa, do, la, 0, (send_d,))
    got_d, got_u = after((got_d, got_u), dqa)
    send_d, send_u = sum_d.upper(got_d), sum_u.upper(got_u)
    got_d, got_u = plane_step(send_d, 1), plane_step(send_u, 0)
    dqb, dkb, dfirst = attend_backward(chain, lengths, q, k, v, ob, do, lb, n, (send_d, send_u))
    got_d, got_u = after((got_d, got_u), dqb)
    send_d, send_u = sum_d.upper(got_d), sum_u.upper(got_u)
    got_d, got_u = depth_step(send_d, 0), plane_step(send_u, 1)
    terms = (dqa, dqb, dka, dkb, df)
    own_q, sib_q = wide_grad(chain, where, a1, terms, terms[0].shape[1], "qkv_grad", (send_d, send_u))
    got_q = core_step(sib_q)
    output = final_output(chain, y, x1, vec, f_down)
    got_q, got_d, got_u = after((got_q, got_d, got_u), output)
    sum_q = Sum(own_q)
    send_q, send_d, send_u = sum_q.upper(got_q), sum_d.upper(got_d), sum_u.upper(got_u)
    got_q, got_d, got_u = plane_step(send_q, 0), depth_step(send_d, 1), depth_step(send_u, 0)
    grad_tokens, vec_own, vec_sib = input_grad(
        chain, where, terms, f_qkv, tokens, dx1, vec, known, True, (send_q, send_d, send_u)
    )
    got_q, got_d, got_u, vec_own, vec_sib = after((got_q, got_d, got_u, vec_own, vec_sib))
    send_q, send_u = sum_q.upper(got_q), sum_u.upper(got_u)
    got_q, got_vec, got_u = plane_step(send_q, 1), core_step(vec_sib), depth_step(send_u, 1)
    got_q = after(got_q, got_d)
    send_q = sum_q.upper(got_q)
    got_vec, got_u = after((got_vec, got_u), send_q)
    got_q = depth_step(send_q, 0)
    v = vec_own + got_vec
    got_vec = [fsdp_swap(v[bits], 2 * bits) for bits in (1, 2, 3)]
    send_q = sum_q.upper(got_q)
    got_vec, total_d, total_u = after((got_vec, sum_d.total(got_d), sum_u.total(got_u)), send_q)
    got_q = depth_step(send_q, 1)
    v = v[0] + sum(got_vec)
    got_vec = [depth_swap(v, bits) for bits in (1, 2, 3)]
    total_q = sum_q.total(got_q)
    grad_vectors = v + sum(after(got_vec, total_q))
    wide = lambda t: t.transpose(1, 0, 2).reshape(piece, -1)
    return (
        output, grad_tokens, dfirst, grad_vectors,
        wide(total_q), total_d[tall], wide(total_u), total_d[:tall].reshape(tall * piece, d),
    )


def solution(mesh):
    rows = P(AXES, None)
    small = mesh.shape["dp"] == 4 and mesh.shape["fsdp"] == 8
    return jax.shard_map(
        local if small else general,
        mesh=mesh,
        in_specs=(rows, rows, rows, rows, P("fsdp"), rows, rows, rows, rows),
        out_specs=(rows, rows, rows, P("fsdp"), rows, rows, rows, rows),
        check_vma=False,
    )
```

```python
import functools
import math

import jax
import jax.numpy as jnp
from jax import lax
from jax.experimental import pallas as pl
from jax.experimental.pallas import tpu as pltpu
from jax.sharding import PartitionSpec as P

BF = jnp.bfloat16
F32 = jnp.float32
HD = 64
EPSILON = 1e-5
HIDDEN = -1e30
AXES = ("dp", "fsdp")
GELU = math.sqrt(2 / math.pi)
CUBE = 0.044715
MIB = 1 << 20
VMEM = 60
PACE = 0.01


def nn(a, b):
    return jnp.dot(a, b, preferred_element_type=F32)


def nt(a, b):
    return lax.dot_general(a, b, (((1,), (1,)), ((), ())), preferred_element_type=F32)


def tn(a, b):
    return lax.dot_general(a, b, (((0,), (0,)), ((), ())), preferred_element_type=F32)


def shape_of(shape, dtype=BF):
    return jax.ShapeDtypeStruct(shape, dtype)


def whole(a):
    return pl.BlockSpec(a.shape, lambda i: (0,) * a.ndim, pipeline_mode=pl.Buffered(1))


def kept(a):
    return pl.BlockSpec(a.shape, lambda *at: (0,) * a.ndim, pipeline_mode=pl.Buffered(1))


def rows_of(blk, n):
    return pl.BlockSpec((blk, n), lambda i: (i, 0))


def vector_of(n):
    return pl.BlockSpec((1, n), lambda i: (0, 0))


SCALARS = pl.BlockSpec(memory_space=pltpu.SMEM)


class Chain:
    def __init__(self):
        self.mark = None

    def call(
        self, kernel, args, *, grid, in_specs, out_specs, out_shape, vmem, cost, waits=(), into=None, scalars=0,
        scratch_shapes=(), name=None,
    ):
        several = isinstance(out_shape, (list, tuple))
        out_specs = list(out_specs) if several else [out_specs]
        out_shape = list(out_shape) if several else [out_shape]
        into = list(into or ())
        deps = into + ([] if self.mark is None else [self.mark]) + list(waits)
        used, extra, outs = len(args), len(deps), len(out_shape)

        def body(*refs):
            results = used + extra
            mark = refs[results + outs]
            mark[...] = jnp.zeros(mark.shape, mark.dtype)
            kernel(*refs[:used], *refs[results : results + outs], *refs[results + outs + 1 :])

        got = pl.pallas_call(
            body,
            grid_spec=pltpu.PrefetchScalarGridSpec(
                num_scalar_prefetch=scalars,
                grid=grid,
                in_specs=list(in_specs) + [pl.BlockSpec(memory_space=pl.ANY)] * extra,
                out_specs=out_specs + [pl.BlockSpec((8, 128), lambda *at: (0, 0))],
                scratch_shapes=list(scratch_shapes),
            ),
            out_shape=out_shape + [shape_of((8, 128), F32)],
            compiler_params=pltpu.CompilerParams(vmem_limit_bytes=vmem * MIB),
            cost_estimate=pl.CostEstimate(
                flops=int(cost * PACE * 1.15e9), bytes_accessed=int(cost * PACE * 3.69e6), transcendentals=0
            ),
            input_output_aliases={used + i: i for i in range(len(into))},
            name=name,
        )(*args, *deps)
        self.mark = got[-1]
        return got[:-1] if several else got[0]


def half_mask(head):
    return (lax.broadcasted_iota(jnp.int32, (1, 2 * HD), 1) // HD) == head


def causal_tile(blk):
    key = lax.broadcasted_iota(jnp.int32, (blk, blk), 0)
    return key <= lax.broadcasted_iota(jnp.int32, (blk, blk), 1)


def attend_forward_kernel(len_ref, q_ref, k_ref, v_ref, o_ref, lse_ref, ot_ref):
    rows = q_ref.shape[0]
    blk, half = 256, rows // 2
    bias = jnp.where(len_ref[0, 0] < rows, HIDDEN, 0.0).astype(F32)
    vt = v_ref[...].T
    causal = causal_tile(blk)
    for head in range(2):
        hs = slice(HD * head, HD * head + HD)
        vth = vt[hs]
        for i in range(rows // blk):
            at = slice(i * blk, (i + 1) * blk)
            q = jnp.where(half_mask(head), q_ref[at], jnp.zeros((), BF))
            parts = []
            for j in range(i + 1):
                s = nt(k_ref[j * blk : (j + 1) * blk], q)
                if j == i:
                    s = jnp.where(causal, s, HIDDEN)
                elif i * blk >= half and (j + 1) * blk <= half:
                    s = s + bias
                parts.append(s)
            m = parts[0].max(axis=0, keepdims=True)
            for s in parts[1:]:
                m = jnp.maximum(m, s.max(axis=0, keepdims=True))
            total = jnp.zeros((1, blk), F32)
            mixed = jnp.zeros((HD, blk), F32)
            for j, s in enumerate(parts):
                p = jnp.exp(s - m)
                total = total + p.sum(axis=0, keepdims=True)
                mixed = mixed + nn(vth[:, j * blk : (j + 1) * blk], p.astype(BF))
            ot_ref[hs, at] = mixed / total
            lse_ref[0, head : head + 1, at] = m + jnp.log(total)
    o_ref[...] = ot_ref[...].T.astype(BF)


def attend_forward(chain, lengths, q, k, v, first, count, into=None):
    rows, width = q.shape
    pair = pl.BlockSpec((rows, 2 * HD), lambda p: (0, p + first))
    return chain.call(
        attend_forward_kernel,
        (lengths, q, k, v),
        grid=(count,),
        in_specs=[SCALARS, pair, pair, pair],
        out_specs=[pair, pl.BlockSpec((1, 2, rows), lambda p: (p + first, 0, 0))],
        out_shape=[shape_of((rows, width)), shape_of((width // (2 * HD), 2, rows), F32)],
        scratch_shapes=[pltpu.VMEM((2 * HD, rows), F32)],
        into=into,
        vmem=VMEM,
        cost=3.5 * count,
        name="attend_forward",
    )


def attend_backward_kernel(
    len_ref, q_ref, k_ref, v_ref, o_ref, do_ref, lse_ref, dq_ref, dk_ref, *rest, first, fresh, parts
):
    dv_refs, (dqt_acc, dv_acc, dk_acc) = rest[:parts], rest[parts:]
    rows = q_ref.shape[0]
    blk, half = 256, rows // 2
    nb = rows // blk
    bias = jnp.where(len_ref[0, 0] < rows, HIDDEN, 0.0).astype(F32)
    prod = (do_ref[...].astype(F32) * o_ref[...].astype(F32)).T
    kt = k_ref[...].T
    causal = causal_tile(blk)
    for head in range(2):
        hs = slice(HD * head, HD * head + HD)
        delta = prod[hs].sum(axis=0, keepdims=True)
        lse = lse_ref[0, head : head + 1, :]
        qh = jnp.where(half_mask(head), q_ref[...], jnp.zeros((), BF))
        doh = jnp.where(half_mask(head), do_ref[...], jnp.zeros((), BF))
        for j in range(nb):
            kr = slice(j * blk, (j + 1) * blk)
            kj, vj, ktj = k_ref[kr], v_ref[kr], kt[hs, kr]
            dv = jnp.zeros((blk, 2 * HD), F32)
            dk = jnp.zeros((blk, 2 * HD), F32)
            for i in range(j, nb):
                at = slice(i * blk, (i + 1) * blk)
                s = nt(kj, qh[at])
                if i == j:
                    s = jnp.where(causal, s, HIDDEN)
                elif i * blk >= half and (j + 1) * blk <= half:
                    s = s + bias
                p = jnp.exp(s - lse[:, at])
                dp = nt(vj, doh[at])
                ds = (p * (dp - delta[:, at])).astype(BF)
                dv = dv + nn(p.astype(BF), doh[at])
                dk = dk + nn(ds, qh[at])
                dqt = nn(ktj, ds)
                if j == 0:
                    dqt_acc[hs, at] = dqt
                else:
                    dqt_acc[hs, at] += dqt
            if head == 0:
                dv_acc[kr] = dv
                dk_acc[kr] = dk
            else:
                dv_acc[kr] += dv
                dk_acc[kr] += dk
    dq_ref[...] = (dqt_acc[...].T * 0.125).astype(BF)
    dk_ref[...] = dk_acc[...].astype(BF)
    dv = dv_acc[...].astype(BF)
    if len(dv_refs) == 1:
        dv_refs[0][...] = dv
        return
    pair = pl.program_id(0) + first

    @pl.when(pair < fresh)
    def _():
        dv_refs[0][...] = dv

    @pl.when(pair >= fresh)
    def _():
        dv_refs[1][...] = dv


def attend_backward(chain, lengths, q, k, v, o, do, lse, first, count, into=None, waits=()):
    rows, width = q.shape
    fresh = width // (4 * HD)
    pair = pl.BlockSpec((rows, 2 * HD), lambda p: (0, p + first))
    new = pl.BlockSpec((rows, 2 * HD), lambda p: (0, jnp.minimum(p + first, fresh - 1)))
    old = pl.BlockSpec((rows, 2 * HD), lambda p: (0, jnp.maximum(p + first - fresh, 0)))
    dvs = [new] * (first < fresh) + [old] * (first + count > fresh)
    return chain.call(
        functools.partial(attend_backward_kernel, first=first, fresh=fresh, parts=len(dvs)),
        (lengths, q, k, v, o, do, lse),
        grid=(count,),
        in_specs=[SCALARS] + [pair] * 5 + [pl.BlockSpec((1, 2, rows), lambda p: (p + first, 0, 0))],
        out_specs=[pair, pair] + dvs,
        out_shape=[shape_of((rows, width))] * 2 + [shape_of((rows, width // 2))] * len(dvs),
        scratch_shapes=[
            pltpu.VMEM((2 * HD, rows), F32),
            pltpu.VMEM((rows, 2 * HD), F32),
            pltpu.VMEM((rows, 2 * HD), F32),
        ],
        vmem=VMEM,
        cost=6 * count,
        into=into,
        waits=waits,
        name="attend_backward",
    )


def row_stats(v):
    center = v - jnp.mean(v, axis=-1, keepdims=True)
    rstd = lax.rsqrt(jnp.mean(center * center, axis=-1, keepdims=True) + EPSILON)
    return center * rstd, rstd


def norm_back(grad, unit, rstd, gain):
    g = grad * gain
    return rstd * (
        g - jnp.mean(g, axis=-1, keepdims=True) - unit * jnp.mean(g * unit, axis=-1, keepdims=True)
    )


def column_sum(v):
    return v.astype(F32).sum(axis=0, keepdims=True)


def clear(*refs):
    @pl.when(pl.program_id(0) == 0)
    def _():
        for r in refs:
            r[...] = jnp.zeros(r.shape, r.dtype)


def vector_parts(ref, d, vd):
    ff = ref.shape[1] - 7 * d - vd
    parts, at = [], 0
    for n in (d, d, d, vd, d, d, d, ff, d):
        parts.append(ref.at[:, at : at + n])
        at += n
    return parts


def project_kernel(*refs, pieces):
    if pieces:
        where_ref, *side = refs[: 2 * pieces + 1]
        x_ref, first_ref, vec_ref, a_ref, q_ref, k_ref, v_ref, w_ref, acc_ref = refs[2 * pieces + 1 :]

        @pl.when(pl.program_id(0) == 0)
        def _():
            load_side(where_ref, side[:pieces], side[pieces:], w_ref, acc_ref)
    else:
        x_ref, first_ref, vec_ref, w_ref, a_ref, q_ref, k_ref, v_ref = refs
    d, vd = x_ref.shape[1], first_ref.shape[1]
    g_ref, b_ref, bq_ref, bv_ref = vector_parts(vec_ref, d, vd)[:4]
    unit, _ = row_stats(x_ref[...].astype(F32))
    a = (unit * g_ref[...] + b_ref[...]).astype(BF)
    a_ref[...] = a
    q = (nn(a, w_ref[:, 0:d]) + bq_ref[...]).astype(BF)
    q_ref[...] = (q.astype(F32) * 0.125).astype(BF)
    k_ref[...] = nn(a, w_ref[:, d : 2 * d]).astype(BF)
    v_ref[:, 0:vd] = (nn(a, w_ref[:, 2 * d :]) + bv_ref[...]).astype(BF)
    v_ref[:, vd:] = first_ref[...]


def project(chain, x, first, vec, w, where=None, blk=256):
    rows, d = x.shape
    pieces = w is not None and where is not None
    args, specs = (x, first, vec), [rows_of(blk, d), rows_of(blk, first.shape[1]), whole(vec)]
    outs, shapes, scratch = [rows_of(blk, d)] * 4, [shape_of((rows, d))] * 4, []
    count = 0
    if pieces:
        own, sib = w
        count = len(own)
        _, r, n = own[0].shape
        n = n * (own[0].shape[0] // 4)
        args = (where, *own, *sib) + args
        specs = [SCALARS] + [kept(t) for t in (*own, *sib)] + specs
        outs = outs + [pl.BlockSpec((32 * r, n), lambda i: (0, 0))]
        shapes = shapes + [shape_of((32 * r, n))]
        scratch = [pltpu.VMEM((32 * r, n), F32)]
    else:
        args, specs = args + (w,), specs + [whole(w)]
    return chain.call(
        functools.partial(project_kernel, pieces=count),
        args,
        grid=(rows // blk,),
        in_specs=specs,
        out_specs=outs,
        out_shape=shapes,
        scratch_shapes=scratch,
        vmem=VMEM,
        cost=8,
        name="project",
    )


def feed_kernel(*refs, pieces, chunk=512):
    if pieces:
        where_ref, *side = refs[: pieces + 1]
        (
            o_ref, x_ref, c_ref, vec_ref, x1_ref, a_ref, y_ref, du_ref, dx_ref, dz_ref, do_ref,
            dbo_ref, dg_ref, db_ref, dbu_ref, dbd_ref, wd_ref, wo_ref, wu_ref, acc,
        ) = refs[pieces + 1 :]

        @pl.when(pl.program_id(0) == 0)
        def _():
            load_wide(where_ref, side[:4], side[4:8], wu_ref, acc)
            load_tall(where_ref, side[8:12], side[12:], wd_ref, wo_ref, acc)
    else:
        (
            o_ref, x_ref, c_ref, vec_ref, wu_ref, wd_ref, wo_ref, x1_ref, a_ref, y_ref, du_ref, dx_ref,
            dz_ref, do_ref, dbo_ref, dg_ref, db_ref, dbu_ref, dbd_ref,
        ) = refs
    clear(dbo_ref, dg_ref, db_ref, dbu_ref, dbd_ref)
    d, ff = wu_ref.shape
    bo_ref, g_ref, b_ref, bu_ref = vector_parts(vec_ref, d, vec_ref.shape[1] - 7 * d - ff)[4:8]
    x1 = x_ref[...].astype(F32) + (nn(o_ref[...], wo_ref[...]) + bo_ref[...])
    x1_ref[...] = x1
    unit, rstd = row_stats(x1)
    a = (unit * g_ref[...] + b_ref[...]).astype(BF)
    a_ref[...] = a
    c = c_ref[...]
    da = jnp.zeros(x1.shape, F32)
    for s in range(0, wu_ref.shape[1], chunk):
        at = slice(s, s + chunk)
        u = nn(a, wu_ref[:, at]) + bu_ref[:, at]
        dy = nt(c, wd_ref[at])
        u2 = u * u
        t = jnp.tanh(u * (GELU + (GELU * CUBE) * u2))
        h = 0.5 * t + 0.5
        y_ref[:, at] = (u * h).astype(BF)
        slope = h + (0.5 * u) * (1.0 - t * t) * (GELU + (3 * GELU * CUBE) * u2)
        du = (slope * dy).astype(BF)
        du_ref[:, at] = du
        dbu_ref[:, at] += column_sum(du)
        da = da + nt(du, wu_ref[:, at])
    c32 = c.astype(F32)
    dbd_ref[...] += column_sum(c)
    db_ref[...] += column_sum(da)
    dg_ref[...] += column_sum(da * unit)
    dx = c32 + norm_back(da, unit, rstd, g_ref[...])
    dx_ref[...] = dx
    dz = dx.astype(BF)
    dz_ref[...] = dz
    dbo_ref[...] += column_sum(dz)
    do_ref[...] = nt(dz, wo_ref[...]).astype(BF)


def feed(chain, o, x, c, vec, weights, where=None, blk=256):
    rows, d = x.shape
    ff = vec.shape[1] - 7 * d - d // 2
    args = (o, x, c, vec)
    specs = [rows_of(blk, d)] * 3 + [whole(vec)]
    outs = [rows_of(blk, n) for n in (d, d, ff, ff, d, d, d)] + [vector_of(n) for n in (d, d, d, ff, d)]
    shapes = [
        shape_of((rows, d), F32), shape_of((rows, d)), shape_of((rows, ff)), shape_of((rows, ff)),
        shape_of((rows, d), F32), shape_of((rows, d)), shape_of((rows, d)),
    ] + [shape_of((1, n), F32) for n in (d, d, d, ff, d)]
    scratch, count = [], 0
    if where is not None:
        count = len(weights)
        args = (where, *weights) + args
        specs = [SCALARS] + [kept(t) for t in weights] + specs
        outs = outs + [pl.BlockSpec((ff, d), lambda i: (0, 0))]
        shapes = shapes + [shape_of((ff, d))]
        scratch = [pltpu.VMEM((d, d), BF), pltpu.VMEM((d, ff), BF), pltpu.VMEM((d, d), F32)]
    else:
        args, specs = args + tuple(weights), specs + [whole(t) for t in weights]
    return chain.call(
        functools.partial(feed_kernel, pieces=count),
        args,
        grid=(rows // blk,),
        in_specs=specs,
        out_specs=outs,
        out_shape=shapes,
        scratch_shapes=scratch,
        vmem=VMEM,
        cost=31,
        name="feed_forward",
    )


def output_kernel(y_ref, x1_ref, vec_ref, wd_ref, out_ref, acc_ref):
    step = pl.program_id(0)

    @pl.when(step == 0)
    def _():
        acc_ref[...] = x1_ref[...] + vec_ref[:, vec_ref.shape[1] - x1_ref.shape[1] :]

    acc_ref[...] += nn(y_ref[...], wd_ref[...])

    @pl.when(step == pl.num_programs(0) - 1)
    def _():
        out_ref[...] = acc_ref[...].astype(BF)


def final_output(chain, y, x1, vec, wd, part=0, parts=1, into=None, waits=(), blk=768):
    rows, ff = y.shape[0] // parts, y.shape[1]
    d = x1.shape[1]
    return chain.call(
        output_kernel,
        (y, x1, vec, wd),
        grid=(ff // blk,),
        in_specs=[
            pl.BlockSpec((rows, blk), lambda i: (part, i)),
            pl.BlockSpec((rows, d), lambda i: (part, 0), pipeline_mode=pl.Buffered(1)),
            whole(vec),
            rows_of(blk, d),
        ],
        out_specs=pl.BlockSpec((rows, d), lambda i: (part, 0)),
        out_shape=shape_of(x1.shape),
        into=into,
        scratch_shapes=[pltpu.VMEM((rows, d), F32)],
        waits=waits,
        vmem=VMEM,
        cost=8,
        name="output",
    )


def input_kernel(
    where_ref, dq_ref, dk_ref, df_ref, w_ref, x_ref, dx_ref, vec_ref,
    dbo_ref, dg2_ref, db2_ref, dbu_ref, dbd_ref, gt_ref, *rest, split,
):
    dvec_ref = rest[-1]
    clear(dvec_ref)
    half = df_ref.shape[1]
    d = x_ref.shape[1]
    dg, db, dbq, dbv, dbo, dg2, db2, dbu, dbd = vector_parts(dvec_ref, d, half)
    dq, dk, df = dq_ref[...], dk_ref[...], df_ref[...]
    da = nt(dq, w_ref[:, 0:d]) + nt(dk, w_ref[:, d : 2 * d]) + nt(df, w_ref[:, 2 * d :])
    dbq[...] += column_sum(dq)
    dbv[...] += column_sum(df)
    unit, rstd = row_stats(x_ref[...].astype(F32))
    db[...] += column_sum(da)
    dg[...] += column_sum(da * unit)
    gt_ref[...] = (dx_ref[...] + norm_back(da, unit, rstd, vec_ref[:, 0:d])).astype(BF)

    @pl.when(pl.program_id(0) == pl.num_programs(0) - 1)
    def _():
        for ref, known in ((dbo, dbo_ref), (dg2, dg2_ref), (db2, db2_ref), (dbu, dbu_ref), (dbd, dbd_ref)):
            ref[...] = known[...]
        if not split:
            rest[0][...] = dvec_ref[...]
            return
        plane, core = where_ref[1], where_ref[2]
        n = rest[0].shape[1]
        parts = [dvec_ref[:, f * n : (f + 1) * n] for f in range(8)]
        for side, out in enumerate(rest[:2]):
            for r in range(4):
                f = jnp.bitwise_xor(plane, r) * 2 + (core if side == 0 else 1 - core)
                v = parts[0]
                for g in range(1, 8):
                    v = jnp.where(f == g, parts[g], v)
                out[r : r + 1, :] = v


def input_grad(chain, where, terms, w, x, dx, vec, known, split, waits=(), blk=256):
    rows, d = x.shape
    n = vec.shape[1]
    vecs = [(4, n // 8)] * 2 if split else [(1, n)]
    return chain.call(
        functools.partial(input_kernel, split=split),
        (where, *terms, w, x, dx, vec, *known),
        grid=(rows // blk,),
        in_specs=[SCALARS] + [rows_of(blk, t.shape[1]) for t in terms] + [whole(w), rows_of(blk, d), rows_of(blk, d)]
        + [whole(t) for t in (vec, *known)],
        out_specs=[rows_of(blk, d)] + [pl.BlockSpec(t, lambda i: (0, 0)) for t in vecs],
        out_shape=[shape_of((rows, d))] + [shape_of(t, F32) for t in vecs],
        scratch_shapes=[pltpu.VMEM((1, n), F32)],
        waits=waits,
        vmem=VMEM,
        cost=9,
        name="input_grad",
    )


def flipped(r):
    return 2 * lax.rem(r, 2) + lax.div(r, 2)


def gathered_slot(r, core):
    return jnp.where(core == 0, r, flipped(r))


def summed_slot(r, core):
    return jnp.where(core == 0, flipped(r), r)


def plane_step(v, step):
    return lax.ppermute(v, "fsdp", [(i, i ^ (2 if i % 2 == step else 4)) for i in range(8)])


def depth_step(v, step):
    pairs = [(i, i ^ (8 if i % 2 == step else 16)) for i in range(32)]
    return lax.ppermute(v, AXES, pairs)


def depth_swap(v, bits):
    return lax.ppermute(v, "dp", [(i, i ^ bits) for i in range(4)])


def fsdp_swap(v, bit):
    return lax.ppermute(v, "fsdp", [(i, i ^ bit) for i in range(8)])


def core_step(v):
    return fsdp_swap(v, 1)


def resident(a):
    return pl.BlockSpec(a.shape, lambda *at: (0,) * a.ndim)


def pack(chain, parts, vec, n):
    rows, columns = parts[0].shape[1:]
    each = columns // n
    m = vec.shape[1]

    def kernel(*refs):
        v_ref, out, acc = refs[len(parts) :]
        for i in range(len(parts)):
            for c in range(each):
                out[i * each + c] = refs[i][0, :, c * n : (c + 1) * n]
        acc[...] = jnp.zeros(acc.shape, F32)
        for row, at in enumerate(range(0, m, n)):
            rest = v_ref[:, at : min(at + n, m)]
            for term in range(3):
                part = rest.astype(BF).astype(F32)
                acc[3 * term + row : 3 * term + row + 1, 0 : part.shape[1]] = part
                rest = rest - part
        out[each * len(parts)] = acc[...].astype(BF)

    shape = shape_of((each * len(parts) + 1, rows, n))
    return chain.call(
        kernel,
        (*parts, vec),
        grid=(1,),
        in_specs=[resident(p) for p in (*parts, vec)],
        out_specs=resident(shape),
        out_shape=shape,
        scratch_shapes=[pltpu.VMEM((rows, n), F32)],
        vmem=8,
        cost=1,
        name="pack",
    )


def places(where_ref, own, sib, straight):
    z, plane, core = where_ref[0], where_ref[1], where_ref[2]
    for side, group in enumerate((own, sib)):
        half = core if side == 0 else 1 - core
        for rp, ref in enumerate(group):
            for t in range(4):
                rz = t if straight else gathered_slot(t, half)
                chip = jnp.bitwise_xor(z, rz) * 4 + jnp.bitwise_xor(plane, gathered_slot(rp, half))
                yield ref, t, chip * 2 + half


def load_side(where_ref, own, sib, out, acc):
    rows, n = own[0].shape[1:]
    for ref, t, device in places(where_ref, own, sib, True):
        at = pl.ds(pl.multiple_of(device * rows, 8), rows)
        for c in range(out.shape[1] // n):
            acc[at, c * n : (c + 1) * n] = ref[t * (out.shape[1] // n) + c].astype(F32)
    out[...] = acc[...].astype(BF)


def load_wide(where_ref, own, sib, out, acc):
    rows = own[0].shape[1]
    n = acc.shape[1]
    for c in range(0, out.shape[1], n):
        for ref, t, device in places(where_ref, own, sib, False):
            acc[pl.ds(pl.multiple_of(device * rows, 8), rows), :] = ref[t, :, c : c + n].astype(F32)
        out[:, c : c + n] = acc[...].astype(BF)


def load_tall(where_ref, own, sib, tall, flat, acc):
    chunks, rows = own[0].shape[1:3]
    for ref, t, device in places(where_ref, own, sib, False):
        part = jnp.concatenate([ref[t, q].astype(F32) for q in range(chunks - 1)], axis=0)
        n = (chunks - 1) * rows
        tall[pl.ds(pl.multiple_of(device * n, n), n), :] = part.astype(BF)
        acc[pl.ds(pl.multiple_of(device * rows, 8), rows), :] = ref[t, chunks - 1].astype(F32)
    flat[...] = acc[...].astype(BF)


class Sum:
    def __init__(self, own):
        self.terms = [own]

    def upper(self, got):
        self.terms.append(got)
        n = got.shape[0]
        send = sum(t[n // 2 : n].astype(F32) for t in self.terms).astype(BF)
        return send

    def total(self, got):
        return sum(t[0].astype(F32) for t in self.terms + [got])


def hand_out(where_ref, acc, piece, own_ref, sib_ref):
    z, plane, core = where_ref[0], where_ref[1], where_ref[2]
    n = 0
    for zd in range(4):
        for pd in range(4):
            rz, rp = jnp.bitwise_xor(z, zd), jnp.bitwise_xor(plane, pd)
            lo, hi = acc[n : n + piece].astype(BF), acc[n + piece : n + 2 * piece].astype(BF)
            own_ref[summed_slot(rp, core) * 4 + summed_slot(rz, core), 0] = jnp.where(core == 0, lo, hi)
            sib_ref[summed_slot(rp, 1 - core) * 4 + summed_slot(rz, 1 - core), 0] = jnp.where(core == 0, hi, lo)
            n += 2 * piece


def wide_grad(chain, where, left, rights, blk, name, waits=()):
    rows, m = left.shape
    piece = m // 32
    starts, steps = [], 0
    for r in rights:
        starts.append(steps)
        steps += r.shape[1] // blk

    def kernel(where_ref, l_ref, *refs):
        r_refs, (own_ref, sib_ref, lt_ref, r_all) = refs[: len(rights)], refs[len(rights) :]
        step = pl.program_id(0)

        @pl.when(step == 0)
        def _():
            lt_ref[...] = l_ref[...].T

        for ref, start, end in zip(r_refs, starts, starts[1:] + [steps]):

            @pl.when((step >= start) & (step < end))
            def _(ref=ref):
                r_all[...] = ref[...]

        hand_out(where_ref, nn(lt_ref[...], r_all[...]), piece, own_ref, sib_ref)

    def chunk(r, start):
        n = r.shape[1] // blk
        return pl.BlockSpec((rows, blk), lambda i: (0, jnp.clip(i - start, 0, n - 1)))

    block = pl.BlockSpec((16, 1, piece, blk), lambda i: (0, i, 0, 0))
    return chain.call(
        kernel,
        (where, left, *rights),
        grid=(steps,),
        in_specs=[SCALARS, whole(left)] + [chunk(r, start) for r, start in zip(rights, starts)],
        out_specs=[block, block],
        out_shape=[shape_of((16, steps, piece, blk))] * 2,
        scratch_shapes=[pltpu.VMEM((m, rows), BF), pltpu.VMEM((rows, blk), BF)],
        waits=waits,
        vmem=VMEM,
        cost=9,
        name=name,
    )


def tall_grad_kernel(where_ref, y_ref, c_ref, o_ref, dz_ref, own_ref, sib_ref, acc_ref, out_ref):
    step = pl.program_id(0)
    tall = y_ref.shape[1] // 8
    flat = o_ref.shape[1] // 32

    @pl.when(step == 0)
    def _():
        out_ref[...] = tn(o_ref[...], dz_ref[...])

    acc_ref[...] = tn(y_ref[...], c_ref[...])
    plane, core = where_ref[1], where_ref[2]
    base = step * (8 * flat)
    for pd in range(4):
        rp = jnp.bitwise_xor(plane, pd)
        mine, other = summed_slot(rp, core), summed_slot(rp, 1 - core)

        def put(lo, hi, q):
            lo, hi = lo.astype(BF), hi.astype(BF)
            own_ref[mine, 0, q] = jnp.where(core == 0, lo, hi)
            sib_ref[other, 0, q] = jnp.where(core == 0, hi, lo)

        for q in range(tall // flat):
            n = 2 * tall * pd + flat * q
            put(acc_ref[n : n + flat], acc_ref[n + tall : n + tall + flat], q)
        n = pl.multiple_of(base + 2 * flat * pd, 8)
        put(out_ref[pl.ds(n, flat)], out_ref[pl.ds(n + flat, flat)], tall // flat)


def tall_grad(chain, where, y, c, o, dz):
    rows, ff = y.shape
    d = c.shape[1]
    piece = d // 32
    chunks = ff // d + 1

    def slot(flip):
        def index(i, where_ref):
            core = where_ref[2]
            return (0, summed_slot(jnp.bitwise_xor(i, where_ref[0]), 1 - core if flip else core), 0, 0, 0)

        return pl.BlockSpec((4, 1, chunks, piece, d), index)

    own, sib = chain.call(
        tall_grad_kernel,
        (where, y, c, o, dz),
        scalars=1,
        grid=(4,),
        in_specs=[pl.BlockSpec((rows, ff // 4), lambda i, w: (0, i)), kept(c), kept(o), kept(dz)],
        out_specs=[slot(False), slot(True)],
        out_shape=[shape_of((4, 4, chunks, piece, d))] * 2,
        scratch_shapes=[pltpu.VMEM((ff // 4, d), F32), pltpu.VMEM((d, d), F32)],
        vmem=VMEM,
        cost=12.5,
        name="down_out_grad",
    )
    return own.reshape(16, chunks, piece, d), sib.reshape(16, chunks, piece, d)


def arrange_vectors(chain, where, own, sib, m):
    last, rows, n = own[0].shape

    def kernel(where_ref, *refs):
        plane, core = where_ref[1], where_ref[2]
        out = refs[8]
        found = []
        for ref in refs[:8]:
            t = ref[0].astype(F32)
            found.append(t[0:3] + t[3:6] + t[6:9])
        for f in range(8):
            mine = core == f % 2
            slot = gathered_slot(jnp.bitwise_xor(plane, f // 2), f % 2)
            v = jnp.where(mine, found[0], found[4])
            for r in range(1, 4):
                v = jnp.where(slot == r, jnp.where(mine, found[r], found[4 + r]), v)
            for row, at in enumerate(range(0, m, n)):
                w = min(n, m - at)
                out[:, f * m + at : f * m + at + w] = v[row : row + 1, 0:w]

    block = pl.BlockSpec((1, rows, n), lambda i: (last - 1, 0, 0))
    return chain.call(
        kernel,
        (where, *own, *sib),
        grid=(1,),
        in_specs=[SCALARS] + [block] * 8,
        out_specs=vector_of(8 * m),
        out_shape=shape_of((1, 8 * m), F32),
        vmem=8,
        cost=1,
        name="arrange_vectors",
    )


def after(values, *deps):
    return lax.optimization_barrier((values, deps))[0]


def whole_gather(w, axes=AXES):
    return lax.all_gather(w, axes, axis=0, tiled=True)


def general(tokens, first_values, cotangent, lengths, vectors, w_qkv, w_out, w_up, w_down):
    d = tokens.shape[1]
    chain = Chain()
    scatter = lambda g: lax.psum_scatter(g, AXES, scatter_dimension=0, tiled=True)
    vec = whole_gather(vectors, "fsdp").reshape(1, -1)
    f_qkv, f_out, f_up, f_down = (whole_gather(w) for w in (w_qkv, w_out, w_up, w_down))
    where = jnp.zeros((3,), jnp.int32)
    a1, q, k, v = project(chain, tokens, first_values, vec, f_qkv)
    n = d // (4 * HD)
    o, lse = attend_forward(chain, lengths, q, k, v, 0, 2 * n)
    x1, a2, y, du, dx1, dz, do, *known = feed(chain, o, tokens, cotangent, vec, (f_up, f_down, f_out))
    output = final_output(chain, y, x1, vec, f_down)
    dq, dk, df, dfirst = attend_backward(chain, lengths, q, k, v, o, do, lse, 0, 2 * n)
    terms = (dq, dk, df)
    grad_tokens, dvec = input_grad(chain, where, terms, f_qkv, tokens, dx1, vec, known, False)
    n = vectors.shape[0]
    grad_vectors = lax.dynamic_slice_in_dim(lax.psum(dvec[0], AXES), lax.axis_index("fsdp") * n, n, 0)
    return (
        output, grad_tokens, dfirst, grad_vectors,
        scatter(tn(a1, jnp.concatenate(terms, axis=1))), scatter(tn(o, dz)), scatter(tn(a2, du)), scatter(tn(y, cotangent)),
    )


def local(tokens, first_values, cotangent, lengths, vectors, w_qkv, w_out, w_up, w_down):
    d = tokens.shape[1]
    index = lax.axis_index("fsdp")
    plane, core = lax.div(index, 2), lax.rem(index, 2)
    where = jnp.stack([lax.axis_index("dp"), plane, core]).astype(jnp.int32)
    piece = w_qkv.shape[0]
    tall = w_down.shape[0] // piece
    chain = Chain()

    grow = lambda a, b: jnp.concatenate([a, b], axis=0)
    up = w_up[None]
    down = jnp.concatenate([w_down.reshape(tall, piece, d), w_out[None]], axis=0)[None]
    m = [w_qkv[None]] + [depth_swap(w_qkv[None], bits) for bits in (1, 2, 3)]
    m, got_u, down = after((m, depth_step(up, 0), down))

    m = pack(chain, m, vectors[None], d // 2)
    up = grow(up, got_u)
    near, side = plane_step(m, 0), plane_step(m, 1)
    m, near, side, got_u = after((m, near, side, depth_step(up, 1)))

    up = grow(up, got_u)
    far = plane_step(near, 1)
    near_u, side_u = plane_step(up, 0), plane_step(up, 1)
    near, side, far, sib, got_d = after((near, side, far, core_step(m), depth_step(down, 0)))

    down = grow(down, got_d)
    got_d = depth_step(down, 1)
    sib = [sib] + [core_step(t) for t in (near, side, far)]
    sib, up, near_u, side_u = after((sib, up, near_u, side_u))

    own = [m, near, side, far]
    far_u = plane_step(near_u, 1)
    sib_u = [core_step(up), core_step(near_u)]
    vec = arrange_vectors(chain, where, own, sib, vectors.shape[0])
    a1, q, k, v, f_qkv = project(chain, tokens, first_values, vec, (own, sib), where)
    far_u, sib_u, side_u, down, got_d = after((far_u, sib_u, side_u, down, got_d), a1)

    down = grow(down, got_d)
    near_d, side_d = plane_step(down, 0), plane_step(down, 1)
    sib_u += [core_step(side_u), core_step(far_u)]
    o, lse = attend_forward(chain, lengths, q, k, v, 0, 2)
    o, lse = attend_forward(chain, lengths, q, k, v, 2, 2, (o, lse))
    near_d, side_d, sib_u, down = after((near_d, side_d, sib_u, down), o)

    far_d = plane_step(near_d, 1)
    sib_d = [core_step(t) for t in (down, near_d, side_d)]
    o, lse = attend_forward(chain, lengths, q, k, v, 4, 2, (o, lse))
    far_d, sib_d = after((far_d, sib_d), o)
    sib_d += [core_step(far_d)]
    x1, a2, y, du, dx1, dz, do, *known, f_down = feed(
        chain, o, tokens, cotangent, vec,
        (up, near_u, side_u, far_u, *sib_u, down, near_d, side_d, far_d, *sib_d), where,
    )

    own_d, sib_d = tall_grad(chain, where, y, cotangent, o, dz)
    got_d = core_step(sib_d)
    own_u, sib_u = wide_grad(chain, where, a2, [du], d, "up_grad")
    got_u = core_step(sib_u)
    sum_d, sum_u = Sum(own_d), Sum(own_u)
    send_d = sum_d.upper(after(got_d, own_u))
    got_d = plane_step(send_d, 0)
    n = d // (4 * HD)
    parts = attend_backward(chain, lengths, q, k, v, o, do, lse, 0, n, None, (send_d,))
    got_d, got_u = after((got_d, got_u), parts)
    send_d, send_u = sum_d.upper(got_d), sum_u.upper(got_u)
    got_d, got_u = plane_step(send_d, 1), plane_step(send_u, 0)
    dq, dk, dfirst = attend_backward(chain, lengths, q, k, v, o, do, lse, n, n, parts[:2], (send_d, send_u))
    got_d, got_u = after((got_d, got_u), dq)
    send_d, send_u = sum_d.upper(got_d), sum_u.upper(got_u)
    got_d, got_u = depth_step(send_d, 0), plane_step(send_u, 1)
    terms = (dq, dk, parts[2])
    own_q, sib_q = wide_grad(chain, where, a1, terms, d // 2, "qkv_grad", (send_d, send_u))
    got_q = core_step(sib_q)
    grad_tokens, vec_own, vec_sib = input_grad(chain, where, terms, f_qkv, tokens, dx1, vec, known, True)
    got_q, got_d, got_u, vec_sib = after((got_q, got_d, got_u, vec_sib))
    sum_q = Sum(own_q)
    send_q, send_d, send_u = sum_q.upper(got_q), sum_d.upper(got_d), sum_u.upper(got_u)
    got_q, got_d, got_u = plane_step(send_q, 0), depth_step(send_d, 1), depth_step(send_u, 0)
    got_vec = core_step(vec_sib)
    output = final_output(chain, y, x1, vec, f_down, 0, 1, None, (send_q, send_d, send_u))
    got_q, got_d, got_u, got_vec = after((got_q, got_d, got_u, got_vec), output)
    send_q, send_u = sum_q.upper(got_q), sum_u.upper(got_u)
    got_q, got_u = plane_step(send_q, 1), depth_step(send_u, 1)
    v = vec_own + got_vec
    got_vec = [fsdp_swap(v[bits], 2 * bits) for bits in (1, 2, 3)]
    send_q = sum_q.upper(got_q)
    got_vec, total_d, total_u = after((got_vec, sum_d.total(got_d), sum_u.total(got_u)), send_q)
    got_q = depth_step(send_q, 0)
    v = v[0] + sum(got_vec)
    got_vec = [depth_swap(v, bits) for bits in (1, 2, 3)]
    send_q = sum_q.upper(got_q)
    grad_vectors = v + sum(after(got_vec, send_q))
    total_q = sum_q.total(depth_step(send_q, 1))
    wide = lambda t: t.transpose(1, 0, 2).reshape(piece, -1)
    return (
        output, grad_tokens, dfirst, grad_vectors,
        wide(total_q), total_d[tall], wide(total_u), total_d[:tall].reshape(tall * piece, d),
    )


def solution(mesh):
    rows = P(AXES, None)
    small = mesh.shape["dp"] == 4 and mesh.shape["fsdp"] == 8
    return jax.shard_map(
        local if small else general,
        mesh=mesh,
        in_specs=(rows, rows, rows, rows, P("fsdp"), rows, rows, rows, rows),
        out_specs=(rows, rows, rows, P("fsdp"), rows, rows, rows, rows),
        check_vma=False,
    )
```

```python
import functools
import math

import jax
import jax.numpy as jnp
from jax import lax
from jax.experimental import pallas as pl
from jax.experimental.pallas import tpu as pltpu
from jax.sharding import PartitionSpec as P

BF = jnp.bfloat16
F32 = jnp.float32
HD = 64
EPSILON = 1e-5
HIDDEN = -1e30
AXES = ("dp", "fsdp")
GELU = math.sqrt(2 / math.pi)
CUBE = 0.044715
MIB = 1 << 20
VMEM = 60
PACE = 0.01


def nn(a, b):
    return jnp.dot(a, b, preferred_element_type=F32)


def nt(a, b):
    return lax.dot_general(a, b, (((1,), (1,)), ((), ())), preferred_element_type=F32)


def tn(a, b):
    return lax.dot_general(a, b, (((0,), (0,)), ((), ())), preferred_element_type=F32)


def shape_of(shape, dtype=BF):
    return jax.ShapeDtypeStruct(shape, dtype)


def whole(a):
    return pl.BlockSpec(a.shape, lambda i: (0,) * a.ndim, pipeline_mode=pl.Buffered(1))


def kept(a):
    return pl.BlockSpec(a.shape, lambda *at: (0,) * a.ndim, pipeline_mode=pl.Buffered(1))


def rows_of(blk, n):
    return pl.BlockSpec((blk, n), lambda i: (i, 0))


def vector_of(n):
    return pl.BlockSpec((1, n), lambda i: (0, 0))


SCALARS = pl.BlockSpec(memory_space=pltpu.SMEM)


class Chain:
    def __init__(self):
        self.mark = None

    def call(
        self, kernel, args, *, grid, in_specs, out_specs, out_shape, vmem, cost, waits=(), into=None, scalars=0,
        scratch_shapes=(), name=None,
    ):
        several = isinstance(out_shape, (list, tuple))
        out_specs = list(out_specs) if several else [out_specs]
        out_shape = list(out_shape) if several else [out_shape]
        into = list(into or ())
        deps = into + ([] if self.mark is None else [self.mark]) + list(waits)
        used, extra, outs = len(args), len(deps), len(out_shape)

        def body(*refs):
            results = used + extra
            mark = refs[results + outs]
            mark[...] = jnp.zeros(mark.shape, mark.dtype)
            kernel(*refs[:used], *refs[results : results + outs], *refs[results + outs + 1 :])

        got = pl.pallas_call(
            body,
            grid_spec=pltpu.PrefetchScalarGridSpec(
                num_scalar_prefetch=scalars,
                grid=grid,
                in_specs=list(in_specs) + [pl.BlockSpec(memory_space=pl.ANY)] * extra,
                out_specs=out_specs + [pl.BlockSpec((8, 128), lambda *at: (0, 0))],
                scratch_shapes=list(scratch_shapes),
            ),
            out_shape=out_shape + [shape_of((8, 128), F32)],
            compiler_params=pltpu.CompilerParams(vmem_limit_bytes=vmem * MIB),
            cost_estimate=pl.CostEstimate(
                flops=int(cost * PACE * 1.15e9), bytes_accessed=int(cost * PACE * 3.69e6), transcendentals=0
            ),
            input_output_aliases={used + i: i for i in range(len(into))},
            name=name,
        )(*args, *deps)
        self.mark = got[-1]
        return got[:-1] if several else got[0]


def half_mask(head):
    return (lax.broadcasted_iota(jnp.int32, (1, 2 * HD), 1) // HD) == head


def causal_tile(blk):
    key = lax.broadcasted_iota(jnp.int32, (blk, blk), 0)
    return key <= lax.broadcasted_iota(jnp.int32, (blk, blk), 1)


def staged(work, *stages):
    first, second, third = stages
    ahead, behind = first(*work[0]), None
    for t in range(len(work) + 1):
        coming = first(*work[t + 1]) if t + 1 < len(work) else None
        now = second(*work[t], *ahead) if t < len(work) else None
        if behind is not None:
            third(*work[t - 1], *behind)
        ahead, behind = coming, now


def attend_forward_kernel(len_ref, q_ref, k_ref, v_ref, o_ref, lse_ref, ot_ref):
    rows = q_ref.shape[0]
    blk, half = 256, rows // 2
    bias = jnp.where(len_ref[0, 0] < rows, HIDDEN, 0.0).astype(F32)
    vt = v_ref[...].T
    causal = causal_tile(blk)

    def scores(head, i):
        q = jnp.where(half_mask(head), q_ref[i * blk : (i + 1) * blk], jnp.zeros((), BF))
        parts = []
        for j in range(i + 1):
            s = nt(k_ref[j * blk : (j + 1) * blk], q)
            if j == i:
                s = jnp.where(causal, s, HIDDEN)
            elif i * blk >= half and (j + 1) * blk <= half:
                s = s + bias
            parts.append(s)
        return (parts,)

    def weights(head, i, parts):
        m = functools.reduce(jnp.maximum, [s.max(axis=0, keepdims=True) for s in parts])
        total = jnp.zeros((1, blk), F32)
        probs = []
        for s in parts:
            p = jnp.exp(s - m)
            total = total + p.sum(axis=0, keepdims=True)
            probs.append(p.astype(BF))
        lse_ref[0, head : head + 1, i * blk : (i + 1) * blk] = m + jnp.log(total)
        return probs, total

    def mix(head, i, probs, total):
        hs = slice(HD * head, HD * head + HD)
        mixed = sum(nn(vt[hs, j * blk : (j + 1) * blk], p) for j, p in enumerate(probs))
        ot_ref[hs, i * blk : (i + 1) * blk] = mixed / total

    staged([(head, i) for i in range(rows // blk) for head in range(2)], scores, weights, mix)
    o_ref[...] = ot_ref[...].T.astype(BF)


def attend_forward(chain, lengths, q, k, v, first, count, into=None):
    rows, width = q.shape
    pair = pl.BlockSpec((rows, 2 * HD), lambda p: (0, p + first))
    return chain.call(
        attend_forward_kernel,
        (lengths, q, k, v),
        grid=(count,),
        in_specs=[SCALARS, pair, pair, pair],
        out_specs=[pair, pl.BlockSpec((1, 2, rows), lambda p: (p + first, 0, 0))],
        out_shape=[shape_of((rows, width)), shape_of((width // (2 * HD), 2, rows), F32)],
        scratch_shapes=[pltpu.VMEM((2 * HD, rows), F32)],
        into=into,
        vmem=VMEM,
        cost=3.5 * count,
        name="attend_forward",
    )


def attend_backward_kernel(
    len_ref, q_ref, k_ref, v_ref, o_ref, do_ref, lse_ref, dq_ref, dk_ref, *rest, first, fresh, parts
):
    dv_refs, (dqt_acc, dv_acc, dk_acc) = rest[:parts], rest[parts:]
    rows = q_ref.shape[0]
    blk, half = 256, rows // 2
    nb = rows // blk
    bias = jnp.where(len_ref[0, 0] < rows, HIDDEN, 0.0).astype(F32)
    prod = (do_ref[...].astype(F32) * o_ref[...].astype(F32)).T
    kt = k_ref[...].T
    causal = causal_tile(blk)
    delta = [prod[HD * h : HD * h + HD].sum(axis=0, keepdims=True) for h in range(2)]
    qh = [jnp.where(half_mask(h), q_ref[...], jnp.zeros((), BF)) for h in range(2)]
    doh = [jnp.where(half_mask(h), do_ref[...], jnp.zeros((), BF)) for h in range(2)]
    block = lambda i: slice(i * blk, (i + 1) * blk)
    sums = {}

    def scores(head, j, i):
        return nt(k_ref[block(j)], qh[head][block(i)]), nt(v_ref[block(j)], doh[head][block(i)])

    def weights(head, j, i, s, dp):
        if i == j:
            s = jnp.where(causal, s, HIDDEN)
        elif i * blk >= half and (j + 1) * blk <= half:
            s = s + bias
        p = jnp.exp(s - lse_ref[0, head : head + 1, block(i)])
        return p.astype(BF), (p * (dp - delta[head][:, block(i)])).astype(BF)

    def mix(head, j, i, p, ds):
        hs, at, kr = slice(HD * head, HD * head + HD), block(i), block(j)
        dv, dk = nn(p, doh[head][at]), nn(ds, qh[head][at])
        if i > j:
            dv, dk = sums[head, j][0] + dv, sums[head, j][1] + dk
        sums[head, j] = dv, dk
        dqt = nn(kt[hs, kr], ds)
        if j == 0:
            dqt_acc[hs, at] = dqt
        else:
            dqt_acc[hs, at] += dqt
        if i == nb - 1:
            dv, dk = sums.pop((head, j))
            if head == 0:
                dv_acc[kr] = dv
                dk_acc[kr] = dk
            else:
                dv_acc[kr] += dv
                dk_acc[kr] += dk

    staged([(h, j, i) for h in range(2) for j in range(nb) for i in range(j, nb)], scores, weights, mix)
    dq_ref[...] = (dqt_acc[...].T * 0.125).astype(BF)
    dk_ref[...] = dk_acc[...].astype(BF)
    dv = dv_acc[...].astype(BF)
    if len(dv_refs) == 1:
        dv_refs[0][...] = dv
        return
    pair = pl.program_id(0) + first

    @pl.when(pair < fresh)
    def _():
        dv_refs[0][...] = dv

    @pl.when(pair >= fresh)
    def _():
        dv_refs[1][...] = dv


def attend_backward(chain, lengths, q, k, v, o, do, lse, first, count, into=None, waits=()):
    rows, width = q.shape
    fresh = width // (4 * HD)
    pair = pl.BlockSpec((rows, 2 * HD), lambda p: (0, p + first))
    new = pl.BlockSpec((rows, 2 * HD), lambda p: (0, jnp.minimum(p + first, fresh - 1)))
    old = pl.BlockSpec((rows, 2 * HD), lambda p: (0, jnp.maximum(p + first - fresh, 0)))
    dvs = [new] * (first < fresh) + [old] * (first + count > fresh)
    return chain.call(
        functools.partial(attend_backward_kernel, first=first, fresh=fresh, parts=len(dvs)),
        (lengths, q, k, v, o, do, lse),
        grid=(count,),
        in_specs=[SCALARS] + [pair] * 5 + [pl.BlockSpec((1, 2, rows), lambda p: (p + first, 0, 0))],
        out_specs=[pair, pair] + dvs,
        out_shape=[shape_of((rows, width))] * 2 + [shape_of((rows, width // 2))] * len(dvs),
        scratch_shapes=[
            pltpu.VMEM((2 * HD, rows), F32),
            pltpu.VMEM((rows, 2 * HD), F32),
            pltpu.VMEM((rows, 2 * HD), F32),
        ],
        vmem=VMEM,
        cost=6 * count,
        into=into,
        waits=waits,
        name="attend_backward",
    )


def row_stats(v):
    center = v - jnp.mean(v, axis=-1, keepdims=True)
    rstd = lax.rsqrt(jnp.mean(center * center, axis=-1, keepdims=True) + EPSILON)
    return center * rstd, rstd


def norm_back(grad, unit, rstd, gain):
    g = grad * gain
    return rstd * (
        g - jnp.mean(g, axis=-1, keepdims=True) - unit * jnp.mean(g * unit, axis=-1, keepdims=True)
    )


def column_sum(v):
    return v.astype(F32).sum(axis=0, keepdims=True)


def clear(*refs):
    @pl.when(pl.program_id(0) == 0)
    def _():
        for r in refs:
            r[...] = jnp.zeros(r.shape, r.dtype)


def vector_parts(ref, d, vd):
    ff = ref.shape[1] - 7 * d - vd
    parts, at = [], 0
    for n in (d, d, d, vd, d, d, d, ff, d):
        parts.append(ref.at[:, at : at + n])
        at += n
    return parts


def project_kernel(*refs, pieces):
    if pieces:
        where_ref, *side = refs[: 2 * pieces + 1]
        x_ref, first_ref, vec_ref, a_ref, q_ref, k_ref, v_ref, w_ref, acc_ref = refs[2 * pieces + 1 :]

        @pl.when(pl.program_id(0) == 0)
        def _():
            load_side(where_ref, side[:pieces], side[pieces:], w_ref, acc_ref)
    else:
        x_ref, first_ref, vec_ref, w_ref, a_ref, q_ref, k_ref, v_ref = refs
    d, vd = x_ref.shape[1], first_ref.shape[1]
    g_ref, b_ref, bq_ref, bv_ref = vector_parts(vec_ref, d, vd)[:4]
    unit, _ = row_stats(x_ref[...].astype(F32))
    a = (unit * g_ref[...] + b_ref[...]).astype(BF)
    a_ref[...] = a
    q = (nn(a, w_ref[:, 0:d]) + bq_ref[...]).astype(BF)
    q_ref[...] = (q.astype(F32) * 0.125).astype(BF)
    k_ref[...] = nn(a, w_ref[:, d : 2 * d]).astype(BF)
    v_ref[:, 0:vd] = (nn(a, w_ref[:, 2 * d :]) + bv_ref[...]).astype(BF)
    v_ref[:, vd:] = first_ref[...]


def project(chain, x, first, vec, w, where=None, blk=256):
    rows, d = x.shape
    pieces = w is not None and where is not None
    args, specs = (x, first, vec), [rows_of(blk, d), rows_of(blk, first.shape[1]), whole(vec)]
    outs, shapes, scratch = [rows_of(blk, d)] * 4, [shape_of((rows, d))] * 4, []
    count = 0
    if pieces:
        own, sib = w
        count = len(own)
        _, r, n = own[0].shape
        n = n * (own[0].shape[0] // 4)
        args = (where, *own, *sib) + args
        specs = [SCALARS] + [kept(t) for t in (*own, *sib)] + specs
        outs = outs + [pl.BlockSpec((32 * r, n), lambda i: (0, 0))]
        shapes = shapes + [shape_of((32 * r, n))]
        scratch = [pltpu.VMEM((32 * r, n), F32)]
    else:
        args, specs = args + (w,), specs + [whole(w)]
    return chain.call(
        functools.partial(project_kernel, pieces=count),
        args,
        grid=(rows // blk,),
        in_specs=specs,
        out_specs=outs,
        out_shape=shapes,
        scratch_shapes=scratch,
        vmem=VMEM,
        cost=8,
        name="project",
    )


def feed_kernel(*refs, pieces, chunk=512):
    if pieces:
        where_ref, *side = refs[: pieces + 1]
        (
            o_ref, x_ref, c_ref, vec_ref, x1_ref, a_ref, y_ref, du_ref, dx_ref, dz_ref, do_ref,
            dbo_ref, dg_ref, db_ref, dbu_ref, dbd_ref, wd_ref, wo_ref, wu_ref, acc,
        ) = refs[pieces + 1 :]

        @pl.when(pl.program_id(0) == 0)
        def _():
            load_wide(where_ref, side[:4], side[4:8], wu_ref, acc)
            load_tall(where_ref, side[8:12], side[12:], wd_ref, wo_ref, acc)
    else:
        (
            o_ref, x_ref, c_ref, vec_ref, wu_ref, wd_ref, wo_ref, x1_ref, a_ref, y_ref, du_ref, dx_ref,
            dz_ref, do_ref, dbo_ref, dg_ref, db_ref, dbu_ref, dbd_ref,
        ) = refs
    clear(dbo_ref, dg_ref, db_ref, dbu_ref, dbd_ref)
    d, ff = wu_ref.shape
    bo_ref, g_ref, b_ref, bu_ref = vector_parts(vec_ref, d, vec_ref.shape[1] - 7 * d - ff)[4:8]
    x1 = x_ref[...].astype(F32) + (nn(o_ref[...], wo_ref[...]) + bo_ref[...])
    x1_ref[...] = x1
    unit, rstd = row_stats(x1)
    a = (unit * g_ref[...] + b_ref[...]).astype(BF)
    a_ref[...] = a
    c = c_ref[...]
    da = jnp.zeros(x1.shape, F32)
    for s in range(0, wu_ref.shape[1], chunk):
        at = slice(s, s + chunk)
        u = nn(a, wu_ref[:, at]) + bu_ref[:, at]
        dy = nt(c, wd_ref[at])
        u2 = u * u
        t = jnp.tanh(u * (GELU + (GELU * CUBE) * u2))
        h = 0.5 * t + 0.5
        y_ref[:, at] = (u * h).astype(BF)
        slope = h + (0.5 * u) * (1.0 - t * t) * (GELU + (3 * GELU * CUBE) * u2)
        du = (slope * dy).astype(BF)
        du_ref[:, at] = du
        dbu_ref[:, at] += column_sum(du)
        da = da + nt(du, wu_ref[:, at])
    c32 = c.astype(F32)
    dbd_ref[...] += column_sum(c)
    db_ref[...] += column_sum(da)
    dg_ref[...] += column_sum(da * unit)
    dx = c32 + norm_back(da, unit, rstd, g_ref[...])
    dx_ref[...] = dx
    dz = dx.astype(BF)
    dz_ref[...] = dz
    dbo_ref[...] += column_sum(dz)
    do_ref[...] = nt(dz, wo_ref[...]).astype(BF)


def feed(chain, o, x, c, vec, weights, where=None, blk=256):
    rows, d = x.shape
    ff = vec.shape[1] - 7 * d - d // 2
    args = (o, x, c, vec)
    specs = [rows_of(blk, d)] * 3 + [whole(vec)]
    outs = [rows_of(blk, n) for n in (d, d, ff, ff, d, d, d)] + [vector_of(n) for n in (d, d, d, ff, d)]
    shapes = [
        shape_of((rows, d), F32), shape_of((rows, d)), shape_of((rows, ff)), shape_of((rows, ff)),
        shape_of((rows, d), F32), shape_of((rows, d)), shape_of((rows, d)),
    ] + [shape_of((1, n), F32) for n in (d, d, d, ff, d)]
    scratch, count = [], 0
    if where is not None:
        count = len(weights)
        args = (where, *weights) + args
        specs = [SCALARS] + [kept(t) for t in weights] + specs
        outs = outs + [pl.BlockSpec((ff, d), lambda i: (0, 0))]
        shapes = shapes + [shape_of((ff, d))]
        scratch = [pltpu.VMEM((d, d), BF), pltpu.VMEM((d, ff), BF), pltpu.VMEM((d, d), F32)]
    else:
        args, specs = args + tuple(weights), specs + [whole(t) for t in weights]
    return chain.call(
        functools.partial(feed_kernel, pieces=count),
        args,
        grid=(rows // blk,),
        in_specs=specs,
        out_specs=outs,
        out_shape=shapes,
        scratch_shapes=scratch,
        vmem=VMEM,
        cost=31,
        name="feed_forward",
    )


def output_kernel(y_ref, x1_ref, vec_ref, wd_ref, out_ref, acc_ref):
    step = pl.program_id(0)

    @pl.when(step == 0)
    def _():
        acc_ref[...] = x1_ref[...] + vec_ref[:, vec_ref.shape[1] - x1_ref.shape[1] :]

    acc_ref[...] += nn(y_ref[...], wd_ref[...])

    @pl.when(step == pl.num_programs(0) - 1)
    def _():
        out_ref[...] = acc_ref[...].astype(BF)


def final_output(chain, y, x1, vec, wd, part=0, parts=1, into=None, waits=(), blk=768):
    rows, ff = y.shape[0] // parts, y.shape[1]
    d = x1.shape[1]
    return chain.call(
        output_kernel,
        (y, x1, vec, wd),
        grid=(ff // blk,),
        in_specs=[
            pl.BlockSpec((rows, blk), lambda i: (part, i)),
            pl.BlockSpec((rows, d), lambda i: (part, 0), pipeline_mode=pl.Buffered(1)),
            whole(vec),
            rows_of(blk, d),
        ],
        out_specs=pl.BlockSpec((rows, d), lambda i: (part, 0)),
        out_shape=shape_of(x1.shape),
        into=into,
        scratch_shapes=[pltpu.VMEM((rows, d), F32)],
        waits=waits,
        vmem=VMEM,
        cost=8,
        name="output",
    )


def input_kernel(
    where_ref, dq_ref, dk_ref, df_ref, w_ref, x_ref, dx_ref, vec_ref,
    dbo_ref, dg2_ref, db2_ref, dbu_ref, dbd_ref, gt_ref, *rest, split,
):
    dvec_ref = rest[-1]
    clear(dvec_ref)
    half = df_ref.shape[1]
    d = x_ref.shape[1]
    dg, db, dbq, dbv, dbo, dg2, db2, dbu, dbd = vector_parts(dvec_ref, d, half)
    dq, dk, df = dq_ref[...], dk_ref[...], df_ref[...]
    da = nt(dq, w_ref[:, 0:d]) + nt(dk, w_ref[:, d : 2 * d]) + nt(df, w_ref[:, 2 * d :])
    dbq[...] += column_sum(dq)
    dbv[...] += column_sum(df)
    unit, rstd = row_stats(x_ref[...].astype(F32))
    db[...] += column_sum(da)
    dg[...] += column_sum(da * unit)
    gt_ref[...] = (dx_ref[...] + norm_back(da, unit, rstd, vec_ref[:, 0:d])).astype(BF)

    @pl.when(pl.program_id(0) == pl.num_programs(0) - 1)
    def _():
        for ref, known in ((dbo, dbo_ref), (dg2, dg2_ref), (db2, db2_ref), (dbu, dbu_ref), (dbd, dbd_ref)):
            ref[...] = known[...]
        if not split:
            rest[0][...] = dvec_ref[...]
            return
        plane, core = where_ref[1], where_ref[2]
        n = rest[0].shape[1]
        parts = [dvec_ref[:, f * n : (f + 1) * n] for f in range(8)]
        for side, out in enumerate(rest[:2]):
            for r in range(4):
                f = jnp.bitwise_xor(plane, r) * 2 + (core if side == 0 else 1 - core)
                v = parts[0]
                for g in range(1, 8):
                    v = jnp.where(f == g, parts[g], v)
                out[r : r + 1, :] = v


def input_grad(chain, where, terms, w, x, dx, vec, known, split, waits=(), blk=256):
    rows, d = x.shape
    n = vec.shape[1]
    vecs = [(4, n // 8)] * 2 if split else [(1, n)]
    return chain.call(
        functools.partial(input_kernel, split=split),
        (where, *terms, w, x, dx, vec, *known),
        grid=(rows // blk,),
        in_specs=[SCALARS] + [rows_of(blk, t.shape[1]) for t in terms] + [whole(w), rows_of(blk, d), rows_of(blk, d)]
        + [whole(t) for t in (vec, *known)],
        out_specs=[rows_of(blk, d)] + [pl.BlockSpec(t, lambda i: (0, 0)) for t in vecs],
        out_shape=[shape_of((rows, d))] + [shape_of(t, F32) for t in vecs],
        scratch_shapes=[pltpu.VMEM((1, n), F32)],
        waits=waits,
        vmem=VMEM,
        cost=9,
        name="input_grad",
    )


def flipped(r):
    return 2 * lax.rem(r, 2) + lax.div(r, 2)


def gathered_slot(r, core):
    return jnp.where(core == 0, r, flipped(r))


def summed_slot(r, core):
    return jnp.where(core == 0, flipped(r), r)


def plane_step(v, step):
    return lax.ppermute(v, "fsdp", [(i, i ^ (2 if i % 2 == step else 4)) for i in range(8)])


def depth_step(v, step):
    pairs = [(i, i ^ (8 if i % 2 == step else 16)) for i in range(32)]
    return lax.ppermute(v, AXES, pairs)


def depth_swap(v, bits):
    return lax.ppermute(v, "dp", [(i, i ^ bits) for i in range(4)])


def fsdp_swap(v, bit):
    return lax.ppermute(v, "fsdp", [(i, i ^ bit) for i in range(8)])


def core_step(v):
    return fsdp_swap(v, 1)


def resident(a):
    return pl.BlockSpec(a.shape, lambda *at: (0,) * a.ndim)


def pack(chain, parts, vec, n):
    rows, columns = parts[0].shape[1:]
    each = columns // n
    m = vec.shape[1]

    def kernel(*refs):
        v_ref, out, acc = refs[len(parts) :]
        at = 0
        for ref in refs[: len(parts)]:
            for i in range(ref.shape[0]):
                for c in range(each):
                    out[at] = ref[i, :, c * n : (c + 1) * n]
                    at += 1
        acc[...] = jnp.zeros(acc.shape, F32)
        for row, lane in enumerate(range(0, m, n)):
            rest = v_ref[:, lane : min(lane + n, m)]
            for term in range(3):
                part = rest.astype(BF).astype(F32)
                acc[3 * term + row : 3 * term + row + 1, 0 : part.shape[1]] = part
                rest = rest - part
        out[at] = acc[...].astype(BF)

    shape = shape_of((each * sum(p.shape[0] for p in parts) + 1, rows, n))
    return chain.call(
        kernel,
        (*parts, vec),
        grid=(1,),
        in_specs=[resident(p) for p in (*parts, vec)],
        out_specs=resident(shape),
        out_shape=shape,
        scratch_shapes=[pltpu.VMEM((rows, n), F32)],
        vmem=8,
        cost=1,
        name="pack",
    )


def places(where_ref, own, sib):
    z, plane, core = where_ref[0], where_ref[1], where_ref[2]
    for side, group in enumerate((own, sib)):
        half = core if side == 0 else 1 - core
        for rp, ref in enumerate(group):
            for t in range(4):
                chip = jnp.bitwise_xor(z, gathered_slot(t, half)) * 4 + jnp.bitwise_xor(plane, gathered_slot(rp, half))
                yield ref, t, chip * 2 + half


def load_side(where_ref, own, sib, out, acc):
    rows, n = own[0].shape[1:]
    for ref, t, device in places(where_ref, own, sib):
        at = pl.ds(pl.multiple_of(device * rows, 8), rows)
        for c in range(out.shape[1] // n):
            acc[at, c * n : (c + 1) * n] = ref[t * (out.shape[1] // n) + c].astype(F32)
    out[...] = acc[...].astype(BF)


def load_wide(where_ref, own, sib, out, acc):
    rows = own[0].shape[1]
    n = acc.shape[1]
    for c in range(0, out.shape[1], n):
        for ref, t, device in places(where_ref, own, sib):
            acc[pl.ds(pl.multiple_of(device * rows, 8), rows), :] = ref[t, :, c : c + n].astype(F32)
        out[:, c : c + n] = acc[...].astype(BF)


def load_tall(where_ref, own, sib, tall, flat, acc):
    chunks, rows = own[0].shape[1:3]
    for ref, t, device in places(where_ref, own, sib):
        part = jnp.concatenate([ref[t, q].astype(F32) for q in range(chunks - 1)], axis=0)
        n = (chunks - 1) * rows
        tall[pl.ds(pl.multiple_of(device * n, n), n), :] = part.astype(BF)
        acc[pl.ds(pl.multiple_of(device * rows, 8), rows), :] = ref[t, chunks - 1].astype(F32)
    flat[...] = acc[...].astype(BF)


class Sum:
    def __init__(self, own):
        self.terms = [own]

    def upper(self, got):
        self.terms.append(got)
        n = got.shape[0]
        send = sum(t[n // 2 : n].astype(F32) for t in self.terms).astype(BF)
        return send

    def total(self, got):
        return sum(t[0].astype(F32) for t in self.terms + [got])


def hand_out(where_ref, acc, piece, own_ref, sib_ref):
    z, plane, core = where_ref[0], where_ref[1], where_ref[2]
    n = 0
    for zd in range(4):
        for pd in range(4):
            rz, rp = jnp.bitwise_xor(z, zd), jnp.bitwise_xor(plane, pd)
            lo, hi = acc[n : n + piece].astype(BF), acc[n + piece : n + 2 * piece].astype(BF)
            own_ref[summed_slot(rp, core) * 4 + summed_slot(rz, core), 0] = jnp.where(core == 0, lo, hi)
            sib_ref[summed_slot(rp, 1 - core) * 4 + summed_slot(rz, 1 - core), 0] = jnp.where(core == 0, hi, lo)
            n += 2 * piece


def wide_grad(chain, where, left, rights, blk, name, waits=()):
    rows, m = left.shape
    piece = m // 32
    starts, steps = [], 0
    for r in rights:
        starts.append(steps)
        steps += r.shape[1] // blk

    def kernel(where_ref, l_ref, *refs):
        r_refs, (own_ref, sib_ref, lt_ref, r_all) = refs[: len(rights)], refs[len(rights) :]
        step = pl.program_id(0)

        @pl.when(step == 0)
        def _():
            lt_ref[...] = l_ref[...].T

        for ref, start, end in zip(r_refs, starts, starts[1:] + [steps]):

            @pl.when((step >= start) & (step < end))
            def _(ref=ref):
                r_all[...] = ref[...]

        hand_out(where_ref, nn(lt_ref[...], r_all[...]), piece, own_ref, sib_ref)

    def chunk(r, start):
        n = r.shape[1] // blk
        return pl.BlockSpec((rows, blk), lambda i: (0, jnp.clip(i - start, 0, n - 1)))

    block = pl.BlockSpec((16, 1, piece, blk), lambda i: (0, i, 0, 0))
    return chain.call(
        kernel,
        (where, left, *rights),
        grid=(steps,),
        in_specs=[SCALARS, whole(left)] + [chunk(r, start) for r, start in zip(rights, starts)],
        out_specs=[block, block],
        out_shape=[shape_of((16, steps, piece, blk))] * 2,
        scratch_shapes=[pltpu.VMEM((m, rows), BF), pltpu.VMEM((rows, blk), BF)],
        waits=waits,
        vmem=VMEM,
        cost=9,
        name=name,
    )


def tall_grad_kernel(where_ref, y_ref, c_ref, o_ref, dz_ref, own_ref, sib_ref, acc_ref, out_ref):
    step = pl.program_id(0)
    tall = y_ref.shape[1] // 8
    flat = o_ref.shape[1] // 32

    @pl.when(step == 0)
    def _():
        out_ref[...] = tn(o_ref[...], dz_ref[...])

    acc_ref[...] = tn(y_ref[...], c_ref[...])
    plane, core = where_ref[1], where_ref[2]
    base = step * (8 * flat)
    for pd in range(4):
        rp = jnp.bitwise_xor(plane, pd)
        mine, other = summed_slot(rp, core), summed_slot(rp, 1 - core)

        def put(lo, hi, q):
            lo, hi = lo.astype(BF), hi.astype(BF)
            own_ref[mine, 0, q] = jnp.where(core == 0, lo, hi)
            sib_ref[other, 0, q] = jnp.where(core == 0, hi, lo)

        for q in range(tall // flat):
            n = 2 * tall * pd + flat * q
            put(acc_ref[n : n + flat], acc_ref[n + tall : n + tall + flat], q)
        n = pl.multiple_of(base + 2 * flat * pd, 8)
        put(out_ref[pl.ds(n, flat)], out_ref[pl.ds(n + flat, flat)], tall // flat)


def tall_grad(chain, where, y, c, o, dz):
    rows, ff = y.shape
    d = c.shape[1]
    piece = d // 32
    chunks = ff // d + 1

    def slot(flip):
        def index(i, where_ref):
            core = where_ref[2]
            return (0, summed_slot(jnp.bitwise_xor(i, where_ref[0]), 1 - core if flip else core), 0, 0, 0)

        return pl.BlockSpec((4, 1, chunks, piece, d), index)

    own, sib = chain.call(
        tall_grad_kernel,
        (where, y, c, o, dz),
        scalars=1,
        grid=(4,),
        in_specs=[pl.BlockSpec((rows, ff // 4), lambda i, w: (0, i)), kept(c), kept(o), kept(dz)],
        out_specs=[slot(False), slot(True)],
        out_shape=[shape_of((4, 4, chunks, piece, d))] * 2,
        scratch_shapes=[pltpu.VMEM((ff // 4, d), F32), pltpu.VMEM((d, d), F32)],
        vmem=VMEM,
        cost=12.5,
        name="down_out_grad",
    )
    return own.reshape(16, chunks, piece, d), sib.reshape(16, chunks, piece, d)


def arrange_vectors(chain, where, own, sib, m):
    last, rows, n = own[0].shape

    def kernel(where_ref, *refs):
        plane, core = where_ref[1], where_ref[2]
        out = refs[8]
        found = []
        for ref in refs[:8]:
            t = ref[0].astype(F32)
            found.append(t[0:3] + t[3:6] + t[6:9])
        for f in range(8):
            mine = core == f % 2
            slot = gathered_slot(jnp.bitwise_xor(plane, f // 2), f % 2)
            v = jnp.where(mine, found[0], found[4])
            for r in range(1, 4):
                v = jnp.where(slot == r, jnp.where(mine, found[r], found[4 + r]), v)
            for row, at in enumerate(range(0, m, n)):
                w = min(n, m - at)
                out[:, f * m + at : f * m + at + w] = v[row : row + 1, 0:w]

    block = pl.BlockSpec((1, rows, n), lambda i: (last - 1, 0, 0))
    return chain.call(
        kernel,
        (where, *own, *sib),
        grid=(1,),
        in_specs=[SCALARS] + [block] * 8,
        out_specs=vector_of(8 * m),
        out_shape=shape_of((1, 8 * m), F32),
        vmem=8,
        cost=1,
        name="arrange_vectors",
    )


def after(values, *deps):
    return lax.optimization_barrier((values, deps))[0]


def whole_gather(w, axes=AXES):
    return lax.all_gather(w, axes, axis=0, tiled=True)


def general(tokens, first_values, cotangent, lengths, vectors, w_qkv, w_out, w_up, w_down):
    d = tokens.shape[1]
    chain = Chain()
    scatter = lambda g: lax.psum_scatter(g, AXES, scatter_dimension=0, tiled=True)
    vec = whole_gather(vectors, "fsdp").reshape(1, -1)
    f_qkv, f_out, f_up, f_down = (whole_gather(w) for w in (w_qkv, w_out, w_up, w_down))
    where = jnp.zeros((3,), jnp.int32)
    a1, q, k, v = project(chain, tokens, first_values, vec, f_qkv)
    n = d // (4 * HD)
    o, lse = attend_forward(chain, lengths, q, k, v, 0, 2 * n)
    x1, a2, y, du, dx1, dz, do, *known = feed(chain, o, tokens, cotangent, vec, (f_up, f_down, f_out))
    output = final_output(chain, y, x1, vec, f_down)
    dq, dk, df, dfirst = attend_backward(chain, lengths, q, k, v, o, do, lse, 0, 2 * n)
    terms = (dq, dk, df)
    grad_tokens, dvec = input_grad(chain, where, terms, f_qkv, tokens, dx1, vec, known, False)
    n = vectors.shape[0]
    grad_vectors = lax.dynamic_slice_in_dim(lax.psum(dvec[0], AXES), lax.axis_index("fsdp") * n, n, 0)
    return (
        output, grad_tokens, dfirst, grad_vectors,
        scatter(tn(a1, jnp.concatenate(terms, axis=1))), scatter(tn(o, dz)), scatter(tn(a2, du)), scatter(tn(y, cotangent)),
    )


def local(tokens, first_values, cotangent, lengths, vectors, w_qkv, w_out, w_up, w_down):
    d = tokens.shape[1]
    index = lax.axis_index("fsdp")
    plane, core = lax.div(index, 2), lax.rem(index, 2)
    where = jnp.stack([lax.axis_index("dp"), plane, core]).astype(jnp.int32)
    piece = w_qkv.shape[0]
    tall = w_down.shape[0] // piece
    chain = Chain()

    grow = lambda a, b: jnp.concatenate([a, b], axis=0)
    m, up = w_qkv[None], w_up[None]
    m, up, got, got_u = after((m, up, depth_step(m, 0), depth_step(up, 0)))

    m, up = grow(m, got), grow(up, got_u)
    down = jnp.concatenate([w_down.reshape(tall, piece, d), w_out[None]], axis=0)[None]
    m, up, got, got_u, down = after((m, up, depth_step(m, 1), depth_step(up, 1), down))

    m = pack(chain, [m, got], vectors[None], d // 2)
    up = grow(up, got_u)
    near, side = plane_step(m, 0), plane_step(m, 1)
    near_u, side_u = plane_step(up, 0), plane_step(up, 1)
    m, up, near, side, near_u, side_u, down, got_d = after((m, up, near, side, near_u, side_u, down, depth_step(down, 0)))

    down = grow(down, got_d)
    far, far_u = plane_step(near, 1), plane_step(near_u, 1)
    sib, far, far_u, down, got_d = after((core_step(m), far, far_u, down, depth_step(down, 1)))

    down = grow(down, got_d)
    own, sib = [m, near, side, far], [sib] + [core_step(t) for t in (near, side, far)]
    near_d, side_d = plane_step(down, 0), plane_step(down, 1)
    vec = arrange_vectors(chain, where, own, sib, vectors.shape[0])
    a1, q, k, v, f_qkv = project(chain, tokens, first_values, vec, (own, sib), where)
    up, near_u, side_u, far_u = after((up, near_u, side_u, far_u), a1)
    sib_u = [core_step(up), core_step(near_u), core_step(side_u)]
    o, lse = attend_forward(chain, lengths, q, k, v, 0, 2)
    near_d, side_d, sib_u, far_u, down = after((near_d, side_d, sib_u, far_u, down), o)

    far_d = plane_step(near_d, 1)
    sib_u += [core_step(far_u)]
    sib_d = [core_step(t) for t in (down, near_d, side_d)]
    o, lse = attend_forward(chain, lengths, q, k, v, 2, 4, (o, lse))
    far_d, sib_u, sib_d = after((far_d, sib_u, sib_d), o)
    sib_d += [core_step(far_d)]
    x1, a2, y, du, dx1, dz, do, *known, f_down = feed(
        chain, o, tokens, cotangent, vec,
        (up, near_u, side_u, far_u, *sib_u, down, near_d, side_d, far_d, *sib_d), where,
    )

    own_d, sib_d = tall_grad(chain, where, y, cotangent, o, dz)
    got_d = core_step(sib_d)
    own_u, sib_u = wide_grad(chain, where, a2, [du], d, "up_grad")
    got_u = core_step(sib_u)
    sum_d, sum_u = Sum(own_d), Sum(own_u)
    send_d = sum_d.upper(after(got_d, own_u))
    got_d = plane_step(send_d, 0)
    n = d // (2 * HD)
    parts = attend_backward(chain, lengths, q, k, v, o, do, lse, 0, 4, None, (send_d,))
    got_d, got_u = after((got_d, got_u), parts)
    send_d, send_u = sum_d.upper(got_d), sum_u.upper(got_u)
    got_d, got_u = plane_step(send_d, 1), plane_step(send_u, 0)
    dq, dk, dfirst = attend_backward(chain, lengths, q, k, v, o, do, lse, 4, n - 4, (parts[0], parts[1], parts[3]), (send_d, send_u))
    terms = (dq, dk, parts[2])
    own_q, sib_q = wide_grad(chain, where, a1, terms, d // 2, "qkv_grad")
    got_d, got_u = after((got_d, got_u), own_q)
    send_d, send_u = sum_d.upper(got_d), sum_u.upper(got_u)
    got_d, got_u = depth_step(send_d, 0), plane_step(send_u, 1)
    got_q = core_step(sib_q)
    grad_tokens, vec_own, vec_sib = input_grad(chain, where, terms, f_qkv, tokens, dx1, vec, known, True, (send_d, send_u))
    got_q, got_d, got_u, vec_sib = after((got_q, got_d, got_u, vec_sib))
    sum_q = Sum(own_q)
    send_q, send_d, send_u = sum_q.upper(got_q), sum_d.upper(got_d), sum_u.upper(got_u)
    got_q, got_d, got_u = plane_step(send_q, 0), depth_step(send_d, 1), depth_step(send_u, 0)
    got_vec = core_step(vec_sib)
    output = final_output(chain, y, x1, vec, f_down, 0, 1, None, (send_q, send_d, send_u))
    got_q, got_d, got_u, got_vec = after((got_q, got_d, got_u, got_vec), output)
    send_q, send_u = sum_q.upper(got_q), sum_u.upper(got_u)
    got_q, got_u = plane_step(send_q, 1), depth_step(send_u, 1)
    v = vec_own + got_vec
    got_vec = [fsdp_swap(v[bits], 2 * bits) for bits in (1, 2, 3)]
    send_q = sum_q.upper(got_q)
    got_vec, total_d, total_u = after((got_vec, sum_d.total(got_d), sum_u.total(got_u)), send_q)
    got_q = depth_step(send_q, 0)
    v = v[0] + sum(got_vec)
    got_vec = [depth_swap(v, bits) for bits in (1, 2, 3)]
    send_q = sum_q.upper(got_q)
    grad_vectors = v + sum(after(got_vec, send_q))
    total_q = sum_q.total(depth_step(send_q, 1))
    wide = lambda t: t.transpose(1, 0, 2).reshape(piece, -1)
    return (
        output, grad_tokens, dfirst, grad_vectors,
        wide(total_q), total_d[tall], wide(total_u), total_d[:tall].reshape(tall * piece, d),
    )


def solution(mesh):
    rows = P(AXES, None)
    small = mesh.shape["dp"] == 4 and mesh.shape["fsdp"] == 8
    return jax.shard_map(
        local if small else general,
        mesh=mesh,
        in_specs=(rows, rows, rows, rows, P("fsdp"), rows, rows, rows, rows),
        out_specs=(rows, rows, rows, P("fsdp"), rows, rows, rows, rows),
        check_vma=False,
    )
```

```python
import functools
import math

import jax
import jax.numpy as jnp
from jax import lax
from jax.experimental import pallas as pl
from jax.experimental.pallas import tpu as pltpu
from jax.sharding import PartitionSpec as P

BF = jnp.bfloat16
F32 = jnp.float32
HD = 64
EPSILON = 1e-5
HIDDEN = -1e30
AXES = ("dp", "fsdp")
GELU = math.sqrt(2 / math.pi)
CUBE = 0.044715
MIB = 1 << 20
VMEM = 60
PACE = 0.01


def nn(a, b):
    return jnp.dot(a, b, preferred_element_type=F32)


def nt(a, b):
    return lax.dot_general(a, b, (((1,), (1,)), ((), ())), preferred_element_type=F32)


def tn(a, b):
    return lax.dot_general(a, b, (((0,), (0,)), ((), ())), preferred_element_type=F32)


def shape_of(shape, dtype=BF):
    return jax.ShapeDtypeStruct(shape, dtype)


def whole(a):
    return pl.BlockSpec(a.shape, lambda i: (0,) * a.ndim, pipeline_mode=pl.Buffered(1))


def kept(a):
    return pl.BlockSpec(a.shape, lambda *at: (0,) * a.ndim, pipeline_mode=pl.Buffered(1))


def rows_of(blk, n):
    return pl.BlockSpec((blk, n), lambda i: (i, 0))


def vector_of(n):
    return pl.BlockSpec((1, n), lambda i: (0, 0))


SCALARS = pl.BlockSpec(memory_space=pltpu.SMEM)


class Chain:
    def __init__(self):
        self.mark = None

    def call(
        self, kernel, args, *, grid, in_specs, out_specs, out_shape, vmem, cost, waits=(), into=None, scalars=0,
        scratch_shapes=(), name=None,
    ):
        several = isinstance(out_shape, (list, tuple))
        out_specs = list(out_specs) if several else [out_specs]
        out_shape = list(out_shape) if several else [out_shape]
        into = list(into or ())
        deps = into + ([] if self.mark is None else [self.mark]) + list(waits)
        used, extra, outs = len(args), len(deps), len(out_shape)

        def body(*refs):
            results = used + extra
            mark = refs[results + outs]
            mark[...] = jnp.zeros(mark.shape, mark.dtype)
            kernel(*refs[:used], *refs[results : results + outs], *refs[results + outs + 1 :])

        got = pl.pallas_call(
            body,
            grid_spec=pltpu.PrefetchScalarGridSpec(
                num_scalar_prefetch=scalars,
                grid=grid,
                in_specs=list(in_specs) + [pl.BlockSpec(memory_space=pl.ANY)] * extra,
                out_specs=out_specs + [pl.BlockSpec((8, 128), lambda *at: (0, 0))],
                scratch_shapes=list(scratch_shapes),
            ),
            out_shape=out_shape + [shape_of((8, 128), F32)],
            compiler_params=pltpu.CompilerParams(vmem_limit_bytes=vmem * MIB),
            cost_estimate=pl.CostEstimate(
                flops=int(cost * PACE * 1.15e9), bytes_accessed=int(cost * PACE * 3.69e6), transcendentals=0
            ),
            input_output_aliases={used + i: i for i in range(len(into))},
            name=name,
        )(*args, *deps)
        self.mark = got[-1]
        return got[:-1] if several else got[0]


def half_mask(head):
    return (lax.broadcasted_iota(jnp.int32, (1, 2 * HD), 1) // HD) == head


def causal_tile(blk):
    key = lax.broadcasted_iota(jnp.int32, (blk, blk), 0)
    return key <= lax.broadcasted_iota(jnp.int32, (blk, blk), 1)


def staged(work, *stages):
    first, second, third = stages
    ahead, behind = first(*work[0]), None
    for t in range(len(work) + 1):
        coming = first(*work[t + 1]) if t + 1 < len(work) else None
        now = second(*work[t], *ahead) if t < len(work) else None
        if behind is not None:
            third(*work[t - 1], *behind)
        ahead, behind = coming, now


def attend_forward_kernel(len_ref, q_ref, k_ref, v_ref, o_ref, lse_ref, ot_ref):
    rows = q_ref.shape[0]
    blk, half = 256, rows // 2
    bias = jnp.where(len_ref[0, 0] < rows, HIDDEN, 0.0).astype(F32)
    vt = v_ref[...].T
    causal = causal_tile(blk)

    def scores(head, i):
        q = jnp.where(half_mask(head), q_ref[i * blk : (i + 1) * blk], jnp.zeros((), BF))
        parts = []
        for j in range(i + 1):
            s = nt(k_ref[j * blk : (j + 1) * blk], q)
            if j == i:
                s = jnp.where(causal, s, HIDDEN)
            elif i * blk >= half and (j + 1) * blk <= half:
                s = s + bias
            parts.append(s)
        return (parts,)

    def weights(head, i, parts):
        m = functools.reduce(jnp.maximum, [s.max(axis=0, keepdims=True) for s in parts])
        total = jnp.zeros((1, blk), F32)
        probs = []
        for s in parts:
            p = jnp.exp(s - m)
            total = total + p.sum(axis=0, keepdims=True)
            probs.append(p.astype(BF))
        lse_ref[0, head : head + 1, i * blk : (i + 1) * blk] = m + jnp.log(total)
        return probs, total

    def mix(head, i, probs, total):
        hs = slice(HD * head, HD * head + HD)
        mixed = sum(nn(vt[hs, j * blk : (j + 1) * blk], p) for j, p in enumerate(probs))
        ot_ref[hs, i * blk : (i + 1) * blk] = mixed / total

    staged([(head, i) for i in range(rows // blk) for head in range(2)], scores, weights, mix)
    o_ref[...] = ot_ref[...].T.astype(BF)


def attend_forward(chain, lengths, q, k, v, first, count, into=None):
    rows, width = q.shape
    pair = pl.BlockSpec((rows, 2 * HD), lambda p: (0, p + first))
    return chain.call(
        attend_forward_kernel,
        (lengths, q, k, v),
        grid=(count,),
        in_specs=[SCALARS, pair, pair, pair],
        out_specs=[pair, pl.BlockSpec((1, 2, rows), lambda p: (p + first, 0, 0))],
        out_shape=[shape_of((rows, width)), shape_of((width // (2 * HD), 2, rows), F32)],
        scratch_shapes=[pltpu.VMEM((2 * HD, rows), F32)],
        into=into,
        vmem=VMEM,
        cost=3.5 * count,
        name="attend_forward",
    )


def attend_backward_kernel(
    len_ref, q_ref, k_ref, v_ref, o_ref, do_ref, lse_ref, dq_ref, dk_ref, *rest, first, fresh, parts
):
    dv_refs, (dqt_acc, dv_acc, dk_acc) = rest[:parts], rest[parts:]
    rows = q_ref.shape[0]
    blk, half = 256, rows // 2
    nb = rows // blk
    bias = jnp.where(len_ref[0, 0] < rows, HIDDEN, 0.0).astype(F32)
    prod = (do_ref[...].astype(F32) * o_ref[...].astype(F32)).T
    kt = k_ref[...].T
    causal = causal_tile(blk)
    delta = [prod[HD * h : HD * h + HD].sum(axis=0, keepdims=True) for h in range(2)]
    qh = [jnp.where(half_mask(h), q_ref[...], jnp.zeros((), BF)) for h in range(2)]
    doh = [jnp.where(half_mask(h), do_ref[...], jnp.zeros((), BF)) for h in range(2)]
    block = lambda i: slice(i * blk, (i + 1) * blk)
    sums = {}

    def scores(head, j, i):
        return nt(k_ref[block(j)], qh[head][block(i)]), nt(v_ref[block(j)], doh[head][block(i)])

    def weights(head, j, i, s, dp):
        if i == j:
            s = jnp.where(causal, s, HIDDEN)
        elif i * blk >= half and (j + 1) * blk <= half:
            s = s + bias
        p = jnp.exp(s - lse_ref[0, head : head + 1, block(i)])
        return p.astype(BF), (p * (dp - delta[head][:, block(i)])).astype(BF)

    def mix(head, j, i, p, ds):
        hs, at, kr = slice(HD * head, HD * head + HD), block(i), block(j)
        dv, dk = nn(p, doh[head][at]), nn(ds, qh[head][at])
        if i > j:
            dv, dk = sums[head, j][0] + dv, sums[head, j][1] + dk
        sums[head, j] = dv, dk
        dqt = nn(kt[hs, kr], ds)
        if j == 0:
            dqt_acc[hs, at] = dqt
        else:
            dqt_acc[hs, at] += dqt
        if i == nb - 1:
            dv, dk = sums.pop((head, j))
            if head == 0:
                dv_acc[kr] = dv
                dk_acc[kr] = dk
            else:
                dv_acc[kr] += dv
                dk_acc[kr] += dk

    staged([(h, j, i) for h in range(2) for j in range(nb) for i in range(j, nb)], scores, weights, mix)
    dq_ref[...] = (dqt_acc[...].T * 0.125).astype(BF)
    dk_ref[...] = dk_acc[...].astype(BF)
    dv = dv_acc[...].astype(BF)
    if len(dv_refs) == 1:
        dv_refs[0][...] = dv
        return
    pair = pl.program_id(0) + first

    @pl.when(pair < fresh)
    def _():
        dv_refs[0][...] = dv

    @pl.when(pair >= fresh)
    def _():
        dv_refs[1][...] = dv


def attend_backward(chain, lengths, q, k, v, o, do, lse, first, count, into=None, waits=()):
    rows, width = q.shape
    fresh = width // (4 * HD)
    pair = pl.BlockSpec((rows, 2 * HD), lambda p: (0, p + first))
    new = pl.BlockSpec((rows, 2 * HD), lambda p: (0, jnp.minimum(p + first, fresh - 1)))
    old = pl.BlockSpec((rows, 2 * HD), lambda p: (0, jnp.maximum(p + first - fresh, 0)))
    dvs = [new] * (first < fresh) + [old] * (first + count > fresh)
    return chain.call(
        functools.partial(attend_backward_kernel, first=first, fresh=fresh, parts=len(dvs)),
        (lengths, q, k, v, o, do, lse),
        grid=(count,),
        in_specs=[SCALARS] + [pair] * 5 + [pl.BlockSpec((1, 2, rows), lambda p: (p + first, 0, 0))],
        out_specs=[pair, pair] + dvs,
        out_shape=[shape_of((rows, width))] * 2 + [shape_of((rows, width // 2))] * len(dvs),
        scratch_shapes=[
            pltpu.VMEM((2 * HD, rows), F32),
            pltpu.VMEM((rows, 2 * HD), F32),
            pltpu.VMEM((rows, 2 * HD), F32),
        ],
        vmem=VMEM,
        cost=6 * count,
        into=into,
        waits=waits,
        name="attend_backward",
    )


def row_stats(v):
    center = v - jnp.mean(v, axis=-1, keepdims=True)
    rstd = lax.rsqrt(jnp.mean(center * center, axis=-1, keepdims=True) + EPSILON)
    return center * rstd, rstd


def norm_back(grad, unit, rstd, gain):
    g = grad * gain
    return rstd * (
        g - jnp.mean(g, axis=-1, keepdims=True) - unit * jnp.mean(g * unit, axis=-1, keepdims=True)
    )


def column_sum(v):
    return v.astype(F32).sum(axis=0, keepdims=True)


def clear(*refs):
    @pl.when(pl.program_id(0) == 0)
    def _():
        for r in refs:
            r[...] = jnp.zeros(r.shape, r.dtype)


def vector_parts(ref, d, vd):
    ff = ref.shape[1] - 7 * d - vd
    parts, at = [], 0
    for n in (d, d, d, vd, d, d, d, ff, d):
        parts.append(ref.at[:, at : at + n])
        at += n
    return parts


def project_kernel(*refs, pieces):
    if pieces:
        where_ref, *side = refs[: 2 * pieces + 1]
        x_ref, first_ref, vec_ref, a_ref, q_ref, k_ref, v_ref, w_ref, acc_ref = refs[2 * pieces + 1 :]

        @pl.when(pl.program_id(0) == 0)
        def _():
            load_side(where_ref, side[:pieces], side[pieces:], w_ref, acc_ref)
    else:
        x_ref, first_ref, vec_ref, w_ref, a_ref, q_ref, k_ref, v_ref = refs
    d, vd = x_ref.shape[1], first_ref.shape[1]
    g_ref, b_ref, bq_ref, bv_ref = vector_parts(vec_ref, d, vd)[:4]
    unit, _ = row_stats(x_ref[...].astype(F32))
    a = (unit * g_ref[...] + b_ref[...]).astype(BF)
    a_ref[...] = a
    q = (nn(a, w_ref[:, 0:d]) + bq_ref[...]).astype(BF)
    q_ref[...] = (q.astype(F32) * 0.125).astype(BF)
    k_ref[...] = nn(a, w_ref[:, d : 2 * d]).astype(BF)
    v_ref[:, 0:vd] = (nn(a, w_ref[:, 2 * d :]) + bv_ref[...]).astype(BF)
    v_ref[:, vd:] = first_ref[...]


def project(chain, x, first, vec, w, where=None, blk=256):
    rows, d = x.shape
    pieces = w is not None and where is not None
    args, specs = (x, first, vec), [rows_of(blk, d), rows_of(blk, first.shape[1]), whole(vec)]
    outs, shapes, scratch = [rows_of(blk, d)] * 4, [shape_of((rows, d))] * 4, []
    count = 0
    if pieces:
        own, sib = w
        count = len(own)
        _, r, n = own[0].shape
        n = n * (own[0].shape[0] // 4)
        args = (where, *own, *sib) + args
        specs = [SCALARS] + [kept(t) for t in (*own, *sib)] + specs
        outs = outs + [pl.BlockSpec((32 * r, n), lambda i: (0, 0))]
        shapes = shapes + [shape_of((32 * r, n))]
        scratch = [pltpu.VMEM((32 * r, n), F32)]
    else:
        args, specs = args + (w,), specs + [whole(w)]
    return chain.call(
        functools.partial(project_kernel, pieces=count),
        args,
        grid=(rows // blk,),
        in_specs=specs,
        out_specs=outs,
        out_shape=shapes,
        scratch_shapes=scratch,
        vmem=VMEM,
        cost=8,
        name="project",
    )


def feed_kernel(*refs, pieces, chunk=512):
    if pieces:
        where_ref, *side = refs[: pieces + 1]
        (
            o_ref, x_ref, c_ref, vec_ref, x1_ref, a_ref, y_ref, du_ref, dx_ref, dz_ref, do_ref,
            dbo_ref, dg_ref, db_ref, dbu_ref, dbd_ref, wd_ref, wo_ref, wu_ref, acc,
        ) = refs[pieces + 1 :]

        @pl.when(pl.program_id(0) == 0)
        def _():
            load_feed(where_ref, side[:4], side[4:8], side[8:10], side[10:], wu_ref, wd_ref, wo_ref, acc)
    else:
        (
            o_ref, x_ref, c_ref, vec_ref, wu_ref, wd_ref, wo_ref, x1_ref, a_ref, y_ref, du_ref, dx_ref,
            dz_ref, do_ref, dbo_ref, dg_ref, db_ref, dbu_ref, dbd_ref,
        ) = refs
    clear(dbo_ref, dg_ref, db_ref, dbu_ref, dbd_ref)
    d, ff = wu_ref.shape
    bo_ref, g_ref, b_ref, bu_ref = vector_parts(vec_ref, d, vec_ref.shape[1] - 7 * d - ff)[4:8]
    x1 = x_ref[...].astype(F32) + (nn(o_ref[...], wo_ref[...]) + bo_ref[...])
    x1_ref[...] = x1
    unit, rstd = row_stats(x1)
    a = (unit * g_ref[...] + b_ref[...]).astype(BF)
    a_ref[...] = a
    c = c_ref[...]
    da = jnp.zeros(x1.shape, F32)
    for s in range(0, wu_ref.shape[1], chunk):
        at = slice(s, s + chunk)
        u = nn(a, wu_ref[:, at]) + bu_ref[:, at]
        dy = nt(c, wd_ref[at])
        u2 = u * u
        t = jnp.tanh(u * (GELU + (GELU * CUBE) * u2))
        h = 0.5 * t + 0.5
        y_ref[:, at] = (u * h).astype(BF)
        slope = h + (0.5 * u) * (1.0 - t * t) * (GELU + (3 * GELU * CUBE) * u2)
        du = (slope * dy).astype(BF)
        du_ref[:, at] = du
        dbu_ref[:, at] += column_sum(du)
        da = da + nt(du, wu_ref[:, at])
    c32 = c.astype(F32)
    dbd_ref[...] += column_sum(c)
    db_ref[...] += column_sum(da)
    dg_ref[...] += column_sum(da * unit)
    dx = c32 + norm_back(da, unit, rstd, g_ref[...])
    dx_ref[...] = dx
    dz = dx.astype(BF)
    dz_ref[...] = dz
    dbo_ref[...] += column_sum(dz)
    do_ref[...] = nt(dz, wo_ref[...]).astype(BF)


def feed(chain, o, x, c, vec, weights, where=None, blk=256):
    rows, d = x.shape
    ff = vec.shape[1] - 7 * d - d // 2
    args = (o, x, c, vec)
    specs = [rows_of(blk, d)] * 3 + [whole(vec)]
    outs = [rows_of(blk, n) for n in (d, d, ff, ff, d, d, d)] + [vector_of(n) for n in (d, d, d, ff, d)]
    shapes = [
        shape_of((rows, d), F32), shape_of((rows, d)), shape_of((rows, ff)), shape_of((rows, ff)),
        shape_of((rows, d), F32), shape_of((rows, d)), shape_of((rows, d)),
    ] + [shape_of((1, n), F32) for n in (d, d, d, ff, d)]
    scratch, count = [], 0
    if where is not None:
        count = len(weights)
        args = (where, *weights) + args
        specs = [SCALARS] + [kept(t) for t in weights] + specs
        outs = outs + [pl.BlockSpec((ff, d), lambda i: (0, 0))]
        shapes = shapes + [shape_of((ff, d))]
        scratch = [pltpu.VMEM((d, d), BF), pltpu.VMEM((d, ff), BF), pltpu.VMEM((d, d), F32)]
    else:
        args, specs = args + tuple(weights), specs + [whole(t) for t in weights]
    return chain.call(
        functools.partial(feed_kernel, pieces=count),
        args,
        grid=(rows // blk,),
        in_specs=specs,
        out_specs=outs,
        out_shape=shapes,
        scratch_shapes=scratch,
        vmem=VMEM,
        cost=31,
        name="feed_forward",
    )


def output_kernel(y_ref, x1_ref, vec_ref, wd_ref, out_ref, acc_ref):
    step = pl.program_id(0)

    @pl.when(step == 0)
    def _():
        acc_ref[...] = x1_ref[...] + vec_ref[:, vec_ref.shape[1] - x1_ref.shape[1] :]

    acc_ref[...] += nn(y_ref[...], wd_ref[...])

    @pl.when(step == pl.num_programs(0) - 1)
    def _():
        out_ref[...] = acc_ref[...].astype(BF)


def final_output(chain, y, x1, vec, wd, part=0, parts=1, into=None, waits=(), blk=768):
    rows, ff = y.shape[0] // parts, y.shape[1]
    d = x1.shape[1]
    return chain.call(
        output_kernel,
        (y, x1, vec, wd),
        grid=(ff // blk,),
        in_specs=[
            pl.BlockSpec((rows, blk), lambda i: (part, i)),
            pl.BlockSpec((rows, d), lambda i: (part, 0), pipeline_mode=pl.Buffered(1)),
            whole(vec),
            rows_of(blk, d),
        ],
        out_specs=pl.BlockSpec((rows, d), lambda i: (part, 0)),
        out_shape=shape_of(x1.shape),
        into=into,
        scratch_shapes=[pltpu.VMEM((rows, d), F32)],
        waits=waits,
        vmem=VMEM,
        cost=8,
        name="output",
    )


def input_kernel(
    where_ref, dq_ref, dk_ref, df_ref, w_ref, x_ref, dx_ref, vec_ref,
    dbo_ref, dg2_ref, db2_ref, dbu_ref, dbd_ref, gt_ref, *rest, split,
):
    dvec_ref = rest[-1]
    clear(dvec_ref)
    half = df_ref.shape[1]
    d = x_ref.shape[1]
    dg, db, dbq, dbv, dbo, dg2, db2, dbu, dbd = vector_parts(dvec_ref, d, half)
    dq, dk, df = dq_ref[...], dk_ref[...], df_ref[...]
    da = nt(dq, w_ref[:, 0:d]) + nt(dk, w_ref[:, d : 2 * d]) + nt(df, w_ref[:, 2 * d :])
    dbq[...] += column_sum(dq)
    dbv[...] += column_sum(df)
    unit, rstd = row_stats(x_ref[...].astype(F32))
    db[...] += column_sum(da)
    dg[...] += column_sum(da * unit)
    gt_ref[...] = (dx_ref[...] + norm_back(da, unit, rstd, vec_ref[:, 0:d])).astype(BF)

    @pl.when(pl.program_id(0) == pl.num_programs(0) - 1)
    def _():
        for ref, known in ((dbo, dbo_ref), (dg2, dg2_ref), (db2, db2_ref), (dbu, dbu_ref), (dbd, dbd_ref)):
            ref[...] = known[...]
        if not split:
            rest[0][...] = dvec_ref[...]
            return
        plane, core = where_ref[1], where_ref[2]
        n = rest[0].shape[1]
        parts = [dvec_ref[:, f * n : (f + 1) * n] for f in range(8)]
        for side, out in enumerate(rest[:2]):
            for r in range(4):
                f = jnp.bitwise_xor(plane, r) * 2 + (core if side == 0 else 1 - core)
                v = parts[0]
                for g in range(1, 8):
                    v = jnp.where(f == g, parts[g], v)
                out[r : r + 1, :] = v


def input_grad(chain, where, terms, w, x, dx, vec, known, split, waits=(), blk=256):
    rows, d = x.shape
    n = vec.shape[1]
    vecs = [(4, n // 8)] * 2 if split else [(1, n)]
    return chain.call(
        functools.partial(input_kernel, split=split),
        (where, *terms, w, x, dx, vec, *known),
        grid=(rows // blk,),
        in_specs=[SCALARS] + [rows_of(blk, t.shape[1]) for t in terms] + [whole(w), rows_of(blk, d), rows_of(blk, d)]
        + [whole(t) for t in (vec, *known)],
        out_specs=[rows_of(blk, d)] + [pl.BlockSpec(t, lambda i: (0, 0)) for t in vecs],
        out_shape=[shape_of((rows, d))] + [shape_of(t, F32) for t in vecs],
        scratch_shapes=[pltpu.VMEM((1, n), F32)],
        waits=waits,
        vmem=VMEM,
        cost=9,
        name="input_grad",
    )


def flipped(r):
    return 2 * lax.rem(r, 2) + lax.div(r, 2)


def gathered_slot(r, core):
    return jnp.where(core == 0, r, flipped(r))


def summed_slot(r, core):
    return jnp.where(core == 0, flipped(r), r)


def plane_step(v, step):
    return lax.ppermute(v, "fsdp", [(i, i ^ (2 if i % 2 == step else 4)) for i in range(8)])


def depth_step(v, step):
    pairs = [(i, i ^ (8 if i % 2 == step else 16)) for i in range(32)]
    return lax.ppermute(v, AXES, pairs)


def depth_swap(v, bits):
    return lax.ppermute(v, "dp", [(i, i ^ bits) for i in range(4)])


def fsdp_swap(v, bit):
    return lax.ppermute(v, "fsdp", [(i, i ^ bit) for i in range(8)])


def core_step(v):
    return fsdp_swap(v, 1)


def resident(a):
    return pl.BlockSpec(a.shape, lambda *at: (0,) * a.ndim)


def pack(chain, parts, vec, n):
    rows, columns = parts[0].shape[1:]
    each = columns // n
    m = vec.shape[1]

    def kernel(*refs):
        v_ref, out, acc = refs[len(parts) :]
        at = 0
        for ref in refs[: len(parts)]:
            for i in range(ref.shape[0]):
                for c in range(each):
                    out[at] = ref[i, :, c * n : (c + 1) * n]
                    at += 1
        acc[...] = jnp.zeros(acc.shape, F32)
        for row, lane in enumerate(range(0, m, n)):
            rest = v_ref[:, lane : min(lane + n, m)]
            for term in range(3):
                part = rest.astype(BF).astype(F32)
                acc[3 * term + row : 3 * term + row + 1, 0 : part.shape[1]] = part
                rest = rest - part
        out[at] = acc[...].astype(BF)

    shape = shape_of((each * sum(p.shape[0] for p in parts) + 1, rows, n))
    return chain.call(
        kernel,
        (*parts, vec),
        grid=(1,),
        in_specs=[resident(p) for p in (*parts, vec)],
        out_specs=resident(shape),
        out_shape=shape,
        scratch_shapes=[pltpu.VMEM((rows, n), F32)],
        vmem=8,
        cost=1,
        name="pack",
    )


def places(where_ref, own, sib, straight=False):
    z, plane, core = where_ref[0], where_ref[1], where_ref[2]
    for side, group in enumerate((own, sib)):
        half = core if side == 0 else 1 - core
        for rp, ref in enumerate(group):
            for t in range(4):
                rz = t if straight else gathered_slot(t, half)
                chip = jnp.bitwise_xor(z, rz) * 4 + jnp.bitwise_xor(plane, gathered_slot(rp, half))
                yield ref, t, chip * 2 + half


def load_side(where_ref, own, sib, out, acc):
    rows, n = own[0].shape[1:]
    each = out.shape[1] // n
    for ref, t, device in places(where_ref, own, sib, True):
        at = pl.ds(pl.multiple_of(device * rows, 8), rows)
        for c in range(each):
            acc[at, c * n : (c + 1) * n] = ref[t * each + c].astype(F32)
    out[...] = acc[...].astype(BF)


def load_feed(where_ref, own, sib, own_d, sib_d, wu, wd, wo, acc):
    rows, n = own[0].shape[2:]
    wide = wu.shape[1] // n
    tall = wd.shape[0] // 32
    at = lambda device: pl.ds(pl.multiple_of(device * rows, 8), rows)
    before = {id(ref): d for ref, d in zip((*own, *sib), [(own_d, r) for r in range(4)] + [(sib_d, r) for r in range(4)])}
    for ref, t, device in places(where_ref, own, sib):
        group, rp = before[id(ref)]
        early = group[t // 2]
        parts = [early[t % 2, rp, q] for q in range(early.shape[2])]
        parts += [ref[t, q] for q in range(wide + 1, ref.shape[1])]
        part = jnp.concatenate([p.astype(F32) for p in parts], axis=0)
        wd[pl.ds(pl.multiple_of(device * tall, tall), tall), :] = part.astype(BF)
        acc[at(device), :] = ref[t, wide].astype(F32)
    wo[...] = acc[...].astype(BF)
    for c in range(wide):
        for ref, t, device in places(where_ref, own, sib):
            acc[at(device), :] = ref[t, c].astype(F32)
        wu[:, c * n : (c + 1) * n] = acc[...].astype(BF)


class Sum:
    def __init__(self, own, sib):
        self.own = own
        self.got = tuple(core_step(t) for t in sib)

    def start(self):
        self.terms = [self.own[0], self.got[0]]
        return (self.own[1].astype(F32) + self.got[1].astype(F32)).astype(BF)

    def upper(self, got):
        self.terms.append(got)
        n = got.shape[0]
        return sum(t[n // 2 : n].astype(F32) for t in self.terms).astype(BF)

    def total(self, got, part):
        return sum(t[0, part].astype(F32) for t in self.terms + [got])


def hand_out(where_ref, acc, piece, own, sib, depth_first):
    z, plane, core = where_ref[0], where_ref[1], where_ref[2]
    for refs, half in ((own, core), (sib, 1 - core)):
        for slot in range(16):
            z_slot, p_slot = (slot // 4, slot % 4) if depth_first else (slot % 4, slot // 4)
            pd = jnp.bitwise_xor(plane, summed_slot(p_slot, half))
            zd = jnp.bitwise_xor(z, summed_slot(z_slot, half))
            row = pl.multiple_of(((zd * 4 + pd) * 2 + half) * piece, 8)
            refs[slot // 8][slot % 8, 0] = acc[pl.ds(row, piece)].astype(BF)


def wide_grad(chain, where, left, rights, blk, name, depth_first=False, waits=()):
    rows, m = left.shape
    piece = m // 32
    starts, steps = [], 0
    for r in rights:
        starts.append(steps)
        steps += r.shape[1] // blk

    def kernel(where_ref, l_ref, *refs):
        r_refs, (own_lo, own_hi, sib_lo, sib_hi, lt_ref, r_all, acc) = refs[: len(rights)], refs[len(rights) :]
        step = pl.program_id(0)

        @pl.when(step == 0)
        def _():
            lt_ref[...] = l_ref[...].T

        if len(rights) == 1:
            right = r_refs[0][...]
        else:
            for ref, start, end in zip(r_refs, starts, starts[1:] + [steps]):

                @pl.when((step >= start) & (step < end))
                def _(ref=ref):
                    r_all[...] = ref[...]

            right = r_all[...]
        acc[...] = nn(lt_ref[...], right)
        hand_out(where_ref, acc, piece, (own_lo, own_hi), (sib_lo, sib_hi), depth_first)

    def chunk(r, start):
        n = r.shape[1] // blk
        return pl.BlockSpec((rows, blk), lambda i: (0, jnp.clip(i - start, 0, n - 1)))

    block = pl.BlockSpec((8, 1, piece, blk), lambda i: (0, i, 0, 0))
    own_lo, own_hi, sib_lo, sib_hi = chain.call(
        kernel,
        (where, left, *rights),
        grid=(steps,),
        in_specs=[SCALARS, whole(left)] + [chunk(r, start) for r, start in zip(rights, starts)],
        out_specs=[block] * 4,
        out_shape=[shape_of((8, steps, piece, blk))] * 4,
        scratch_shapes=[pltpu.VMEM((m, rows), BF), pltpu.VMEM((rows, blk), BF), pltpu.VMEM((m, blk), F32)],
        waits=waits,
        vmem=VMEM,
        cost=9,
        name=name,
    )
    return (own_lo, own_hi), (sib_lo, sib_hi)


def tall_grad_kernel(
    where_ref, y_ref, c_ref, o_ref, dz_ref, own_lo, own_hi, sib_lo, sib_hi, acc_ref, out_ref
):
    step = pl.program_id(0)
    tall = y_ref.shape[1] // 8
    flat = o_ref.shape[1] // 32

    @pl.when(step == 0)
    def _():
        out_ref[...] = tn(o_ref[...], dz_ref[...])

    acc_ref[...] = tn(y_ref[...], c_ref[...])
    plane, core = where_ref[1], where_ref[2]
    for refs, half in (((own_lo, own_hi), core), ((sib_lo, sib_hi), 1 - core)):
        for slot in range(4):
            near = jnp.bitwise_xor(plane, summed_slot(slot, half)) * 2 + half
            out = refs[slot // 2]
            for q in range(tall // flat):
                row = pl.multiple_of(near * tall + q * flat, 8)
                out[slot % 2, 0, q] = acc_ref[pl.ds(row, flat)].astype(BF)
            row = pl.multiple_of((step * 8 + near) * flat, 8)
            out[slot % 2, 0, tall // flat] = out_ref[pl.ds(row, flat)].astype(BF)


def tall_grad(chain, where, y, c, o, dz):
    rows, ff = y.shape
    d = c.shape[1]
    piece = d // 32
    chunks = ff // d + 1

    def slot(flip):
        def index(i, where_ref):
            core = where_ref[2]
            return (0, summed_slot(jnp.bitwise_xor(i, where_ref[0]), 1 - core if flip else core), 0, 0, 0)

        return pl.BlockSpec((2, 1, chunks, piece, d), index)

    got = chain.call(
        tall_grad_kernel,
        (where, y, c, o, dz),
        scalars=1,
        grid=(4,),
        in_specs=[pl.BlockSpec((rows, ff // 4), lambda i, w: (0, i)), kept(c), kept(o), kept(dz)],
        out_specs=[slot(False), slot(False), slot(True), slot(True)],
        out_shape=[shape_of((2, 4, chunks, piece, d))] * 4,
        scratch_shapes=[pltpu.VMEM((ff // 4, d), F32), pltpu.VMEM((d, d), F32)],
        vmem=VMEM,
        cost=12.5,
        name="down_out_grad",
    )
    own_lo, own_hi, sib_lo, sib_hi = (t.reshape(8, chunks, piece, d) for t in got)
    return (own_lo, own_hi), (sib_lo, sib_hi)


def arrange_vectors(chain, where, own, sib, m):
    last, rows, n = own[0].shape

    def kernel(where_ref, *refs):
        plane, core = where_ref[1], where_ref[2]
        out = refs[8]
        found = []
        for ref in refs[:8]:
            t = ref[0].astype(F32)
            found.append(t[0:3] + t[3:6] + t[6:9])
        for f in range(8):
            mine = core == f % 2
            slot = gathered_slot(jnp.bitwise_xor(plane, f // 2), f % 2)
            v = jnp.where(mine, found[0], found[4])
            for r in range(1, 4):
                v = jnp.where(slot == r, jnp.where(mine, found[r], found[4 + r]), v)
            for row, at in enumerate(range(0, m, n)):
                w = min(n, m - at)
                out[:, f * m + at : f * m + at + w] = v[row : row + 1, 0:w]

    block = pl.BlockSpec((1, rows, n), lambda i: (last - 1, 0, 0))
    return chain.call(
        kernel,
        (where, *own, *sib),
        grid=(1,),
        in_specs=[SCALARS] + [block] * 8,
        out_specs=vector_of(8 * m),
        out_shape=shape_of((1, 8 * m), F32),
        vmem=8,
        cost=1,
        name="arrange_vectors",
    )


def after(values, *deps):
    return lax.optimization_barrier((values, deps))[0]


def whole_gather(w, axes=AXES):
    return lax.all_gather(w, axes, axis=0, tiled=True)


def general(tokens, first_values, cotangent, lengths, vectors, w_qkv, w_out, w_up, w_down):
    d = tokens.shape[1]
    chain = Chain()
    scatter = lambda g: lax.psum_scatter(g, AXES, scatter_dimension=0, tiled=True)
    vec = whole_gather(vectors, "fsdp").reshape(1, -1)
    f_qkv, f_out, f_up, f_down = (whole_gather(w) for w in (w_qkv, w_out, w_up, w_down))
    where = jnp.zeros((3,), jnp.int32)
    a1, q, k, v = project(chain, tokens, first_values, vec, f_qkv)
    n = d // (4 * HD)
    o, lse = attend_forward(chain, lengths, q, k, v, 0, 2 * n)
    x1, a2, y, du, dx1, dz, do, *known = feed(chain, o, tokens, cotangent, vec, (f_up, f_down, f_out))
    output = final_output(chain, y, x1, vec, f_down)
    dq, dk, df, dfirst = attend_backward(chain, lengths, q, k, v, o, do, lse, 0, 2 * n)
    terms = (dq, dk, df)
    grad_tokens, dvec = input_grad(chain, where, terms, f_qkv, tokens, dx1, vec, known, False)
    n = vectors.shape[0]
    grad_vectors = lax.dynamic_slice_in_dim(lax.psum(dvec[0], AXES), lax.axis_index("fsdp") * n, n, 0)
    return (
        output, grad_tokens, dfirst, grad_vectors,
        scatter(tn(a1, jnp.concatenate(terms, axis=1))), scatter(tn(o, dz)), scatter(tn(a2, du)), scatter(tn(y, cotangent)),
    )


def local(tokens, first_values, cotangent, lengths, vectors, w_qkv, w_out, w_up, w_down):
    d = tokens.shape[1]
    index = lax.axis_index("fsdp")
    plane, core = lax.div(index, 2), lax.rem(index, 2)
    where = jnp.stack([lax.axis_index("dp"), plane, core]).astype(jnp.int32)
    piece = w_qkv.shape[0]
    tall = w_down.shape[0] // piece
    chain = Chain()

    grow = lambda a, b: jnp.concatenate([a, b], axis=0)
    chunks = w_down.reshape(tall, piece, d)
    early = chunks[: tall // 2][None]
    late = jnp.concatenate([w_up.reshape(piece, -1, d).transpose(1, 0, 2), w_out[None], chunks[tall // 2 :]], axis=0)[None]
    m = [w_qkv[None]] + [depth_swap(w_qkv[None], bits) for bits in (1, 2, 3)]
    m, near_e, side_e, early, late = after((m, plane_step(early, 0), plane_step(early, 1), early, late))

    m = pack(chain, m, vectors[None], d // 2)
    near, side = plane_step(m, 0), plane_step(m, 1)
    far_e, got = plane_step(near_e, 1), depth_step(late, 0)
    m, near, side, far_e, late, got = after((m, near, side, far_e, late, got))

    late = grow(late, got)
    early = jnp.concatenate([early, near_e, side_e, far_e], axis=0)[None]
    far, sib, got = plane_step(near, 1), core_step(m), depth_step(late, 1)
    far, sib, got, late, early = after((far, sib, got, late, early))

    late = grow(late, got)
    own, sib = [m, near, side, far], [sib] + [core_step(t) for t in (near, side, far)]
    near_l, side_l, got = plane_step(late, 0), plane_step(late, 1), depth_step(early, 0)
    vec = arrange_vectors(chain, where, own, sib, vectors.shape[0])
    a1, q, k, v, f_qkv = project(chain, tokens, first_values, vec, (own, sib), where)
    early, got, late, near_l, side_l = after((early, got, late, near_l, side_l), a1)

    early = grow(early, got)
    got, sib_e = depth_step(early, 1), [core_step(early)]
    far_l = plane_step(near_l, 1)
    sib_l = [core_step(t) for t in (late, near_l, side_l)]
    o, lse = attend_forward(chain, lengths, q, k, v, 0, 6)
    far_l, sib_l, got = after((far_l, sib_l, got), o)
    sib_l += [core_step(far_l)]
    sib_e += [core_step(got)]
    x1, a2, y, du, dx1, dz, do, *known, f_down = feed(
        chain, o, tokens, cotangent, vec,
        (late, near_l, side_l, far_l, *sib_l, early, got, *sib_e), where,
    )

    sum_d = Sum(*tall_grad(chain, where, y, cotangent, o, dz))
    sum_u = Sum(*wide_grad(chain, where, a2, [du], d, "up_grad", True))
    sum_d.got = after(sum_d.got, sum_u.own)
    send_d, send_u = sum_d.start(), sum_u.start()
    got_d, got_u = plane_step(send_d, 0), depth_step(send_u, 0)
    dq, dk, df, dfirst = attend_backward(chain, lengths, q, k, v, o, do, lse, 0, d // (2 * HD), None, (send_d, send_u))
    terms = (dq, dk, df)
    sum_q = Sum(*wide_grad(chain, where, a1, terms, d // 2, "qkv_grad"))
    got_d, got_u = after((got_d, got_u), sum_q.own)
    send_d, send_u = sum_d.upper(got_d), sum_u.upper(got_u)
    got_d, got_u = plane_step(send_d, 1), depth_step(send_u, 1)
    sum_q.got = after(sum_q.got, send_d, send_u)
    send_q = sum_q.start()
    got_q = plane_step(send_q, 0)
    grad_tokens, vec_own, vec_sib = input_grad(
        chain, where, terms, f_qkv, tokens, dx1, vec, known, True, (send_q, send_d, send_u)
    )
    got_q, got_d, got_u, vec_sib = after((got_q, got_d, got_u, vec_sib))
    send_q = sum_q.upper(got_q)
    got_q, got_vec = plane_step(send_q, 1), core_step(vec_sib)
    got_d, got_u = after((got_d, got_u), send_q)
    send_d, send_u = sum_d.upper(got_d), sum_u.upper(got_u)
    got_d, got_u = depth_step(send_d, 0), plane_step(send_u, 0)
    output = final_output(chain, y, x1, vec, f_down, 0, 1, None, (send_q, send_d, send_u))
    got_q, got_d, got_u, got_vec = after((got_q, got_d, got_u, got_vec), output)
    send_q = sum_q.upper(got_q)
    got_d, got_u, got_vec = after((got_d, got_u, got_vec), send_q)
    got_q = depth_step(send_q, 0)
    got_d, got_u = depth_step(sum_d.upper(got_d), 1), plane_step(sum_u.upper(got_u), 1)
    v = vec_own + got_vec
    got_vec = [fsdp_swap(v[bits], 2 * bits) for bits in (1, 2, 3)]
    send_q = sum_q.upper(got_q)
    got_vec = after(got_vec, send_q)
    got_q = depth_step(send_q, 1)
    got_d, got_u = after((got_d, got_u), send_q)
    v = v[0] + sum(got_vec)
    grad_vectors = v + sum(depth_swap(v, bits) for bits in (1, 2, 3))
    grad_down, grad_out = sum_d.total(got_d, slice(0, tall)).reshape(tall * piece, d), sum_d.total(got_d, tall)
    wide = lambda t: t.transpose(1, 0, 2).reshape(piece, -1)
    grad_up = wide(sum_u.total(got_u, slice(None)))
    grad_qkv = wide(sum_q.total(got_q, slice(None)))
    return output, grad_tokens, dfirst, grad_vectors, grad_qkv, grad_out, grad_up, grad_down


def solution(mesh):
    rows = P(AXES, None)
    small = mesh.shape["dp"] == 4 and mesh.shape["fsdp"] == 8
    return jax.shard_map(
        local if small else general,
        mesh=mesh,
        in_specs=(rows, rows, rows, rows, P("fsdp"), rows, rows, rows, rows),
        out_specs=(rows, rows, rows, P("fsdp"), rows, rows, rows, rows),
        check_vma=False,
    )
```

```python
import functools
import math

import jax
import jax.numpy as jnp
from jax import lax
from jax.experimental import pallas as pl
from jax.experimental.pallas import tpu as pltpu
from jax.sharding import PartitionSpec as P

BF = jnp.bfloat16
F32 = jnp.float32
HD = 64
EPSILON = 1e-5
HIDDEN = -1e30
AXES = ("dp", "fsdp")
GELU = math.sqrt(2 / math.pi)
CUBE = 0.044715
MIB = 1 << 20
VMEM = 60
PACE = 0.01


def nn(a, b):
    return jnp.dot(a, b, preferred_element_type=F32)


def nt(a, b):
    return lax.dot_general(a, b, (((1,), (1,)), ((), ())), preferred_element_type=F32)


def tn(a, b):
    return lax.dot_general(a, b, (((0,), (0,)), ((), ())), preferred_element_type=F32)


def shape_of(shape, dtype=BF):
    return jax.ShapeDtypeStruct(shape, dtype)


def whole(a):
    return pl.BlockSpec(a.shape, lambda i: (0,) * a.ndim, pipeline_mode=pl.Buffered(1))


def kept(a):
    return pl.BlockSpec(a.shape, lambda *at: (0,) * a.ndim, pipeline_mode=pl.Buffered(1))


def rows_of(blk, n):
    return pl.BlockSpec((blk, n), lambda i: (i, 0))


def vector_of(n):
    return pl.BlockSpec((1, n), lambda i: (0, 0))


SCALARS = pl.BlockSpec(memory_space=pltpu.SMEM)


class Chain:
    def __init__(self):
        self.mark = None

    def call(
        self, kernel, args, *, grid, in_specs, out_specs, out_shape, vmem, cost, waits=(), into=None, scalars=0,
        scratch_shapes=(), name=None,
    ):
        several = isinstance(out_shape, (list, tuple))
        out_specs = list(out_specs) if several else [out_specs]
        out_shape = list(out_shape) if several else [out_shape]
        into = list(into or ())
        deps = into + ([] if self.mark is None else [self.mark]) + list(waits)
        used, extra, outs = len(args), len(deps), len(out_shape)

        def body(*refs):
            results = used + extra
            mark = refs[results + outs]
            mark[...] = jnp.zeros(mark.shape, mark.dtype)
            kernel(*refs[:used], *refs[results : results + outs], *refs[results + outs + 1 :])

        got = pl.pallas_call(
            body,
            grid_spec=pltpu.PrefetchScalarGridSpec(
                num_scalar_prefetch=scalars,
                grid=grid,
                in_specs=list(in_specs) + [pl.BlockSpec(memory_space=pl.ANY)] * extra,
                out_specs=out_specs + [pl.BlockSpec((8, 128), lambda *at: (0, 0))],
                scratch_shapes=list(scratch_shapes),
            ),
            out_shape=out_shape + [shape_of((8, 128), F32)],
            compiler_params=pltpu.CompilerParams(vmem_limit_bytes=vmem * MIB),
            cost_estimate=pl.CostEstimate(
                flops=int(cost * PACE * 1.15e9), bytes_accessed=int(cost * PACE * 3.69e6), transcendentals=0
            ),
            input_output_aliases={used + i: i for i in range(len(into))},
            name=name,
        )(*args, *deps)
        self.mark = got[-1]
        return got[:-1] if several else got[0]


def half_mask(head):
    return (lax.broadcasted_iota(jnp.int32, (1, 2 * HD), 1) // HD) == head


def causal_tile(blk):
    key = lax.broadcasted_iota(jnp.int32, (blk, blk), 0)
    return key <= lax.broadcasted_iota(jnp.int32, (blk, blk), 1)


def staged(work, *stages):
    first, second, third = stages
    ahead, behind = first(*work[0]), None
    for t in range(len(work) + 1):
        coming = first(*work[t + 1]) if t + 1 < len(work) else None
        now = second(*work[t], *ahead) if t < len(work) else None
        if behind is not None:
            third(*work[t - 1], *behind)
        ahead, behind = coming, now


def attend_forward_kernel(len_ref, q_ref, k_ref, v_ref, o_ref, lse_ref, ot_ref):
    rows = q_ref.shape[0]
    blk, half = 256, rows // 2
    bias = jnp.where(len_ref[0, 0] < rows, HIDDEN, 0.0).astype(F32)
    vt = v_ref[...].T
    causal = causal_tile(blk)

    def scores(head, i):
        q = jnp.where(half_mask(head), q_ref[i * blk : (i + 1) * blk], jnp.zeros((), BF))
        parts = []
        for j in range(i + 1):
            s = nt(k_ref[j * blk : (j + 1) * blk], q)
            if j == i:
                s = jnp.where(causal, s, HIDDEN)
            elif i * blk >= half and (j + 1) * blk <= half:
                s = s + bias
            parts.append(s)
        return (parts,)

    def weights(head, i, parts):
        m = functools.reduce(jnp.maximum, [s.max(axis=0, keepdims=True) for s in parts])
        total = jnp.zeros((1, blk), F32)
        probs = []
        for s in parts:
            p = jnp.exp(s - m)
            total = total + p.sum(axis=0, keepdims=True)
            probs.append(p.astype(BF))
        lse_ref[0, head : head + 1, i * blk : (i + 1) * blk] = m + jnp.log(total)
        return probs, total

    def mix(head, i, probs, total):
        hs = slice(HD * head, HD * head + HD)
        mixed = sum(nn(vt[hs, j * blk : (j + 1) * blk], p) for j, p in enumerate(probs))
        ot_ref[hs, i * blk : (i + 1) * blk] = mixed / total

    staged([(head, i) for i in range(rows // blk) for head in range(2)], scores, weights, mix)
    o_ref[...] = ot_ref[...].T.astype(BF)


def attend_forward(chain, lengths, q, k, v, first, count, into=None):
    rows, width = q.shape
    pair = pl.BlockSpec((rows, 2 * HD), lambda p: (0, p + first))
    return chain.call(
        attend_forward_kernel,
        (lengths, q, k, v),
        grid=(count,),
        in_specs=[SCALARS, pair, pair, pair],
        out_specs=[pair, pl.BlockSpec((1, 2, rows), lambda p: (p + first, 0, 0))],
        out_shape=[shape_of((rows, width)), shape_of((width // (2 * HD), 2, rows), F32)],
        scratch_shapes=[pltpu.VMEM((2 * HD, rows), F32)],
        into=into,
        vmem=VMEM,
        cost=3.5 * count,
        name="attend_forward",
    )


def attend_backward_kernel(
    len_ref, q_ref, k_ref, v_ref, o_ref, do_ref, lse_ref, dq_ref, dk_ref, *rest, first, fresh, parts
):
    dv_refs, (dqt_acc, dv_acc, dk_acc) = rest[:parts], rest[parts:]
    rows = q_ref.shape[0]
    blk, half = 256, rows // 2
    nb = rows // blk
    bias = jnp.where(len_ref[0, 0] < rows, HIDDEN, 0.0).astype(F32)
    prod = (do_ref[...].astype(F32) * o_ref[...].astype(F32)).T
    kt = k_ref[...].T
    causal = causal_tile(blk)
    delta = [prod[HD * h : HD * h + HD].sum(axis=0, keepdims=True) for h in range(2)]
    qh = [jnp.where(half_mask(h), q_ref[...], jnp.zeros((), BF)) for h in range(2)]
    doh = [jnp.where(half_mask(h), do_ref[...], jnp.zeros((), BF)) for h in range(2)]
    block = lambda i: slice(i * blk, (i + 1) * blk)
    sums = {}

    def scores(head, j, i):
        return nt(k_ref[block(j)], qh[head][block(i)]), nt(v_ref[block(j)], doh[head][block(i)])

    def weights(head, j, i, s, dp):
        if i == j:
            s = jnp.where(causal, s, HIDDEN)
        elif i * blk >= half and (j + 1) * blk <= half:
            s = s + bias
        p = jnp.exp(s - lse_ref[0, head : head + 1, block(i)])
        return p.astype(BF), (p * (dp - delta[head][:, block(i)])).astype(BF)

    def mix(head, j, i, p, ds):
        hs, at, kr = slice(HD * head, HD * head + HD), block(i), block(j)
        dv, dk = nn(p, doh[head][at]), nn(ds, qh[head][at])
        if i > j:
            dv, dk = sums[head, j][0] + dv, sums[head, j][1] + dk
        sums[head, j] = dv, dk
        dqt = nn(kt[hs, kr], ds)
        if j == 0:
            dqt_acc[hs, at] = dqt
        else:
            dqt_acc[hs, at] += dqt
        if i == nb - 1:
            dv, dk = sums.pop((head, j))
            if head == 0:
                dv_acc[kr] = dv
                dk_acc[kr] = dk
            else:
                dv_acc[kr] += dv
                dk_acc[kr] += dk

    staged([(h, j, i) for h in range(2) for j in range(nb) for i in range(j, nb)], scores, weights, mix)
    dq_ref[...] = (dqt_acc[...].T * 0.125).astype(BF)
    dk_ref[...] = dk_acc[...].astype(BF)
    dv = dv_acc[...].astype(BF)
    if len(dv_refs) == 1:
        dv_refs[0][...] = dv
        return
    pair = pl.program_id(0) + first

    @pl.when(pair < fresh)
    def _():
        dv_refs[0][...] = dv

    @pl.when(pair >= fresh)
    def _():
        dv_refs[1][...] = dv


def attend_backward(chain, lengths, q, k, v, o, do, lse, first, count, into=None, waits=()):
    rows, width = q.shape
    fresh = width // (4 * HD)
    pair = pl.BlockSpec((rows, 2 * HD), lambda p: (0, p + first))
    new = pl.BlockSpec((rows, 2 * HD), lambda p: (0, jnp.minimum(p + first, fresh - 1)))
    old = pl.BlockSpec((rows, 2 * HD), lambda p: (0, jnp.maximum(p + first - fresh, 0)))
    dvs = [new] * (first < fresh) + [old] * (first + count > fresh)
    return chain.call(
        functools.partial(attend_backward_kernel, first=first, fresh=fresh, parts=len(dvs)),
        (lengths, q, k, v, o, do, lse),
        grid=(count,),
        in_specs=[SCALARS] + [pair] * 5 + [pl.BlockSpec((1, 2, rows), lambda p: (p + first, 0, 0))],
        out_specs=[pair, pair] + dvs,
        out_shape=[shape_of((rows, width))] * 2 + [shape_of((rows, width // 2))] * len(dvs),
        scratch_shapes=[
            pltpu.VMEM((2 * HD, rows), F32),
            pltpu.VMEM((rows, 2 * HD), F32),
            pltpu.VMEM((rows, 2 * HD), F32),
        ],
        vmem=VMEM,
        cost=6 * count,
        into=into,
        waits=waits,
        name="attend_backward",
    )


def row_stats(v):
    center = v - jnp.mean(v, axis=-1, keepdims=True)
    rstd = lax.rsqrt(jnp.mean(center * center, axis=-1, keepdims=True) + EPSILON)
    return center * rstd, rstd


def norm_back(grad, unit, rstd, gain):
    g = grad * gain
    return rstd * (
        g - jnp.mean(g, axis=-1, keepdims=True) - unit * jnp.mean(g * unit, axis=-1, keepdims=True)
    )


def column_sum(v):
    return v.astype(F32).sum(axis=0, keepdims=True)


def clear(*refs):
    @pl.when(pl.program_id(0) == 0)
    def _():
        for r in refs:
            r[...] = jnp.zeros(r.shape, r.dtype)


def vector_parts(ref, d, vd):
    ff = ref.shape[1] - 7 * d - vd
    parts, at = [], 0
    for n in (d, d, d, vd, d, d, d, ff, d):
        parts.append(ref.at[:, at : at + n])
        at += n
    return parts


def project_kernel(*refs, pieces):
    if pieces:
        where_ref, *side = refs[: 2 * pieces + 1]
        x_ref, first_ref, vec_ref, a_ref, q_ref, k_ref, v_ref, w_ref, acc_ref = refs[2 * pieces + 1 :]

        @pl.when(pl.program_id(0) == 0)
        def _():
            load_side(where_ref, side[:pieces], side[pieces:], w_ref, acc_ref)
    else:
        x_ref, first_ref, vec_ref, w_ref, a_ref, q_ref, k_ref, v_ref = refs
    d, vd = x_ref.shape[1], first_ref.shape[1]
    g_ref, b_ref, bq_ref, bv_ref = vector_parts(vec_ref, d, vd)[:4]
    unit, _ = row_stats(x_ref[...].astype(F32))
    a = (unit * g_ref[...] + b_ref[...]).astype(BF)
    a_ref[...] = a
    q = (nn(a, w_ref[:, 0:d]) + bq_ref[...]).astype(BF)
    q_ref[...] = (q.astype(F32) * 0.125).astype(BF)
    k_ref[...] = nn(a, w_ref[:, d : 2 * d]).astype(BF)
    v_ref[:, 0:vd] = (nn(a, w_ref[:, 2 * d :]) + bv_ref[...]).astype(BF)
    v_ref[:, vd:] = first_ref[...]


def project(chain, x, first, vec, w, where=None, blk=256):
    rows, d = x.shape
    pieces = w is not None and where is not None
    args, specs = (x, first, vec), [rows_of(blk, d), rows_of(blk, first.shape[1]), whole(vec)]
    outs, shapes, scratch = [rows_of(blk, d)] * 4, [shape_of((rows, d))] * 4, []
    count = 0
    if pieces:
        own, sib = w
        count = len(own)
        _, r, n = own[0].shape
        n = n * (own[0].shape[0] // 4)
        args = (where, *own, *sib) + args
        specs = [SCALARS] + [kept(t) for t in (*own, *sib)] + specs
        outs = outs + [pl.BlockSpec((32 * r, n), lambda i: (0, 0))]
        shapes = shapes + [shape_of((32 * r, n))]
        scratch = [pltpu.VMEM((32 * r, n), F32)]
    else:
        args, specs = args + (w,), specs + [whole(w)]
    return chain.call(
        functools.partial(project_kernel, pieces=count),
        args,
        grid=(rows // blk,),
        in_specs=specs,
        out_specs=outs,
        out_shape=shapes,
        scratch_shapes=scratch,
        vmem=VMEM,
        cost=8,
        name="project",
    )


def feed_kernel(*refs, pieces, chunk=512):
    if pieces:
        where_ref, *side = refs[: pieces + 1]
        (
            o_ref, x_ref, c_ref, vec_ref, x1_ref, a_ref, y_ref, du_ref, dx_ref, dz_ref, do_ref,
            dbo_ref, dg_ref, db_ref, dbu_ref, dbd_ref, wd_ref, wo_ref, wu_ref, acc,
        ) = refs[pieces + 1 :]

        @pl.when(pl.program_id(0) == 0)
        def _():
            load_feed(where_ref, side[:4], side[4:8], side[8:10], side[10:], wu_ref, wd_ref, wo_ref, acc)
    else:
        (
            o_ref, x_ref, c_ref, vec_ref, wu_ref, wd_ref, wo_ref, x1_ref, a_ref, y_ref, du_ref, dx_ref,
            dz_ref, do_ref, dbo_ref, dg_ref, db_ref, dbu_ref, dbd_ref,
        ) = refs
    clear(dbo_ref, dg_ref, db_ref, dbu_ref, dbd_ref)
    d, ff = wu_ref.shape
    bo_ref, g_ref, b_ref, bu_ref = vector_parts(vec_ref, d, vec_ref.shape[1] - 7 * d - ff)[4:8]
    x1 = x_ref[...].astype(F32) + (nn(o_ref[...], wo_ref[...]) + bo_ref[...])
    x1_ref[...] = x1
    unit, rstd = row_stats(x1)
    a = (unit * g_ref[...] + b_ref[...]).astype(BF)
    a_ref[...] = a
    c = c_ref[...]
    da = jnp.zeros(x1.shape, F32)
    for s in range(0, wu_ref.shape[1], chunk):
        at = slice(s, s + chunk)
        u = nn(a, wu_ref[:, at]) + bu_ref[:, at]
        dy = nt(c, wd_ref[at])
        u2 = u * u
        t = jnp.tanh(u * (GELU + (GELU * CUBE) * u2))
        h = 0.5 * t + 0.5
        y_ref[:, at] = (u * h).astype(BF)
        slope = h + (0.5 * u) * (1.0 - t * t) * (GELU + (3 * GELU * CUBE) * u2)
        du = (slope * dy).astype(BF)
        du_ref[:, at] = du
        dbu_ref[:, at] += column_sum(du)
        da = da + nt(du, wu_ref[:, at])
    c32 = c.astype(F32)
    dbd_ref[...] += column_sum(c)
    db_ref[...] += column_sum(da)
    dg_ref[...] += column_sum(da * unit)
    dx = c32 + norm_back(da, unit, rstd, g_ref[...])
    dx_ref[...] = dx
    dz = dx.astype(BF)
    dz_ref[...] = dz
    dbo_ref[...] += column_sum(dz)
    do_ref[...] = nt(dz, wo_ref[...]).astype(BF)


def feed(chain, o, x, c, vec, weights, where=None, blk=256):
    rows, d = x.shape
    ff = vec.shape[1] - 7 * d - d // 2
    args = (o, x, c, vec)
    specs = [rows_of(blk, d)] * 3 + [whole(vec)]
    outs = [rows_of(blk, n) for n in (d, d, ff, ff, d, d, d)] + [vector_of(n) for n in (d, d, d, ff, d)]
    shapes = [
        shape_of((rows, d), F32), shape_of((rows, d)), shape_of((rows, ff)), shape_of((rows, ff)),
        shape_of((rows, d), F32), shape_of((rows, d)), shape_of((rows, d)),
    ] + [shape_of((1, n), F32) for n in (d, d, d, ff, d)]
    scratch, count = [], 0
    if where is not None:
        count = len(weights)
        args = (where, *weights) + args
        specs = [SCALARS] + [kept(t) for t in weights] + specs
        outs = outs + [pl.BlockSpec((ff, d), lambda i: (0, 0))]
        shapes = shapes + [shape_of((ff, d))]
        scratch = [pltpu.VMEM((d, d), BF), pltpu.VMEM((d, ff), BF), pltpu.VMEM((d, d), F32)]
    else:
        args, specs = args + tuple(weights), specs + [whole(t) for t in weights]
    return chain.call(
        functools.partial(feed_kernel, pieces=count),
        args,
        grid=(rows // blk,),
        in_specs=specs,
        out_specs=outs,
        out_shape=shapes,
        scratch_shapes=scratch,
        vmem=VMEM,
        cost=31,
        name="feed_forward",
    )


def output_kernel(y_ref, x1_ref, vec_ref, wd_ref, out_ref, acc_ref):
    step = pl.program_id(0)

    @pl.when(step == 0)
    def _():
        acc_ref[...] = x1_ref[...] + vec_ref[:, vec_ref.shape[1] - x1_ref.shape[1] :]

    acc_ref[...] += nn(y_ref[...], wd_ref[...])

    @pl.when(step == pl.num_programs(0) - 1)
    def _():
        out_ref[...] = acc_ref[...].astype(BF)


def final_output(chain, y, x1, vec, wd, part=0, parts=1, into=None, waits=(), blk=768):
    rows, ff = y.shape[0] // parts, y.shape[1]
    d = x1.shape[1]
    return chain.call(
        output_kernel,
        (y, x1, vec, wd),
        grid=(ff // blk,),
        in_specs=[
            pl.BlockSpec((rows, blk), lambda i: (part, i)),
            pl.BlockSpec((rows, d), lambda i: (part, 0), pipeline_mode=pl.Buffered(1)),
            whole(vec),
            rows_of(blk, d),
        ],
        out_specs=pl.BlockSpec((rows, d), lambda i: (part, 0)),
        out_shape=shape_of(x1.shape),
        into=into,
        scratch_shapes=[pltpu.VMEM((rows, d), F32)],
        waits=waits,
        vmem=48,
        cost=8,
        name="output",
    )


def input_kernel(
    where_ref, dq_ref, dk_ref, df_ref, w_ref, x_ref, dx_ref, vec_ref,
    dbo_ref, dg2_ref, db2_ref, dbu_ref, dbd_ref, gt_ref, *rest, split,
):
    dvec_ref = rest[-1]
    clear(dvec_ref)
    half = df_ref.shape[1]
    d = x_ref.shape[1]
    dg, db, dbq, dbv, dbo, dg2, db2, dbu, dbd = vector_parts(dvec_ref, d, half)
    dq, dk, df = dq_ref[...], dk_ref[...], df_ref[...]
    da = nt(dq, w_ref[:, 0:d]) + nt(dk, w_ref[:, d : 2 * d]) + nt(df, w_ref[:, 2 * d :])
    dbq[...] += column_sum(dq)
    dbv[...] += column_sum(df)
    unit, rstd = row_stats(x_ref[...].astype(F32))
    db[...] += column_sum(da)
    dg[...] += column_sum(da * unit)
    gt_ref[...] = (dx_ref[...] + norm_back(da, unit, rstd, vec_ref[:, 0:d])).astype(BF)

    @pl.when(pl.program_id(0) == pl.num_programs(0) - 1)
    def _():
        for ref, known in ((dbo, dbo_ref), (dg2, dg2_ref), (db2, db2_ref), (dbu, dbu_ref), (dbd, dbd_ref)):
            ref[...] = known[...]
        if not split:
            rest[0][...] = dvec_ref[...]
            return
        plane, core = where_ref[1], where_ref[2]
        n = rest[0].shape[1]
        parts = [dvec_ref[:, f * n : (f + 1) * n] for f in range(8)]
        for side, out in enumerate(rest[:2]):
            for r in range(4):
                f = jnp.bitwise_xor(plane, r) * 2 + (core if side == 0 else 1 - core)
                v = parts[0]
                for g in range(1, 8):
                    v = jnp.where(f == g, parts[g], v)
                out[r : r + 1, :] = v


def input_grad(chain, where, terms, w, x, dx, vec, known, split, waits=(), blk=256):
    rows, d = x.shape
    n = vec.shape[1]
    vecs = [(4, n // 8)] * 2 if split else [(1, n)]
    return chain.call(
        functools.partial(input_kernel, split=split),
        (where, *terms, w, x, dx, vec, *known),
        grid=(rows // blk,),
        in_specs=[SCALARS] + [rows_of(blk, t.shape[1]) for t in terms] + [whole(w), rows_of(blk, d), rows_of(blk, d)]
        + [whole(t) for t in (vec, *known)],
        out_specs=[rows_of(blk, d)] + [pl.BlockSpec(t, lambda i: (0, 0)) for t in vecs],
        out_shape=[shape_of((rows, d))] + [shape_of(t, F32) for t in vecs],
        scratch_shapes=[pltpu.VMEM((1, n), F32)],
        waits=waits,
        vmem=48,
        cost=9,
        name="input_grad",
    )


def flipped(r):
    return 2 * lax.rem(r, 2) + lax.div(r, 2)


def gathered_slot(r, core):
    return jnp.where(core == 0, r, flipped(r))


def summed_slot(r, core):
    return jnp.where(core == 0, flipped(r), r)


def plane_step(v, step):
    return lax.ppermute(v, "fsdp", [(i, i ^ (2 if i % 2 == step else 4)) for i in range(8)])


def depth_step(v, step):
    pairs = [(i, i ^ (8 if i % 2 == step else 16)) for i in range(32)]
    return lax.ppermute(v, AXES, pairs)


def depth_swap(v, bits):
    return lax.ppermute(v, "dp", [(i, i ^ bits) for i in range(4)])


def fsdp_swap(v, bit):
    return lax.ppermute(v, "fsdp", [(i, i ^ bit) for i in range(8)])


def core_step(v):
    return fsdp_swap(v, 1)


def resident(a):
    return pl.BlockSpec(a.shape, lambda *at: (0,) * a.ndim)


def pack(chain, parts, vec, n):
    rows, columns = parts[0].shape[1:]
    each = columns // n
    m = vec.shape[1]

    def kernel(*refs):
        v_ref, out, acc = refs[len(parts) :]
        at = 0
        for ref in refs[: len(parts)]:
            for i in range(ref.shape[0]):
                for c in range(each):
                    out[at] = ref[i, :, c * n : (c + 1) * n]
                    at += 1
        acc[...] = jnp.zeros(acc.shape, F32)
        for row, lane in enumerate(range(0, m, n)):
            rest = v_ref[:, lane : min(lane + n, m)]
            for term in range(3):
                part = rest.astype(BF).astype(F32)
                acc[3 * term + row : 3 * term + row + 1, 0 : part.shape[1]] = part
                rest = rest - part
        out[at] = acc[...].astype(BF)

    shape = shape_of((each * sum(p.shape[0] for p in parts) + 1, rows, n))
    return chain.call(
        kernel,
        (*parts, vec),
        grid=(1,),
        in_specs=[resident(p) for p in (*parts, vec)],
        out_specs=resident(shape),
        out_shape=shape,
        scratch_shapes=[pltpu.VMEM((rows, n), F32)],
        vmem=8,
        cost=1,
        name="pack",
    )


def places(where_ref, own, sib, straight=False):
    z, plane, core = where_ref[0], where_ref[1], where_ref[2]
    for side, group in enumerate((own, sib)):
        half = core if side == 0 else 1 - core
        for rp, ref in enumerate(group):
            for t in range(4):
                rz = t if straight else gathered_slot(t, half)
                chip = jnp.bitwise_xor(z, rz) * 4 + jnp.bitwise_xor(plane, gathered_slot(rp, half))
                yield ref, t, chip * 2 + half


def load_side(where_ref, own, sib, out, acc):
    rows, n = own[0].shape[1:]
    each = out.shape[1] // n
    for ref, t, device in places(where_ref, own, sib, True):
        at = pl.ds(pl.multiple_of(device * rows, 8), rows)
        for c in range(each):
            acc[at, c * n : (c + 1) * n] = ref[t * each + c].astype(F32)
    out[...] = acc[...].astype(BF)


def load_feed(where_ref, own, sib, own_d, sib_d, wu, wd, wo, acc):
    rows, n = own[0].shape[2:]
    wide = wu.shape[1] // n
    tall = wd.shape[0] // 32
    at = lambda device: pl.ds(pl.multiple_of(device * rows, 8), rows)
    before = {id(ref): d for ref, d in zip((*own, *sib), [(own_d, r) for r in range(4)] + [(sib_d, r) for r in range(4)])}
    for ref, t, device in places(where_ref, own, sib):
        group, rp = before[id(ref)]
        early = group[t // 2]
        parts = [early[t % 2, rp, q] for q in range(early.shape[2])]
        parts += [ref[t, q] for q in range(wide + 1, ref.shape[1])]
        part = jnp.concatenate([p.astype(F32) for p in parts], axis=0)
        wd[pl.ds(pl.multiple_of(device * tall, tall), tall), :] = part.astype(BF)
        acc[at(device), :] = ref[t, wide].astype(F32)
    wo[...] = acc[...].astype(BF)
    for c in range(wide):
        for ref, t, device in places(where_ref, own, sib):
            acc[at(device), :] = ref[t, c].astype(F32)
        wu[:, c * n : (c + 1) * n] = acc[...].astype(BF)


class Sum:
    def __init__(self, own, sib):
        self.own = own
        self.got = tuple(core_step(t) for t in sib)

    def start(self):
        self.terms = [self.own[0], self.got[0]]
        return (self.own[1].astype(F32) + self.got[1].astype(F32)).astype(BF)

    def upper(self, got):
        self.terms.append(got)
        n = got.shape[0]
        return sum(t[n // 2 : n].astype(F32) for t in self.terms).astype(BF)

    def last(self, got):
        return self.terms + [got]


def totals(chain, groups, shapes, name):
    def kernel(*refs):
        outs = list(refs[sum(len(g) for g in groups) :])
        at = 0
        for g, results in zip(groups, shapes):
            terms = refs[at : at + len(g)]
            at += len(g)
            rows, n = g[0].shape[2:]
            q = 0
            for shape in results:
                out = outs.pop(0)
                for r in range(0, shape[0], rows):
                    for c in range(0, shape[1], n):
                        out[r : r + rows, c : c + n] = sum(t[0, q].astype(F32) for t in terms)
                        q += 1

    flat = [t for g in groups for t in g]
    made = [shape_of(s, F32) for results in shapes for s in results]
    return chain.call(
        kernel,
        flat,
        grid=(1,),
        in_specs=[pl.BlockSpec((1, *t.shape[1:]), lambda i: (0, 0, 0, 0)) for t in flat],
        out_specs=[resident(t) for t in made],
        out_shape=made,
        vmem=24,
        cost=3,
        name=name,
    )


def hand_out(where_ref, acc, piece, own, sib, depth_first):
    z, plane, core = where_ref[0], where_ref[1], where_ref[2]
    for refs, half in ((own, core), (sib, 1 - core)):
        for slot in range(16):
            z_slot, p_slot = (slot // 4, slot % 4) if depth_first else (slot % 4, slot // 4)
            pd = jnp.bitwise_xor(plane, summed_slot(p_slot, half))
            zd = jnp.bitwise_xor(z, summed_slot(z_slot, half))
            row = pl.multiple_of(((zd * 4 + pd) * 2 + half) * piece, 8)
            refs[slot // 8][slot % 8, 0] = acc[pl.ds(row, piece)].astype(BF)


def wide_grad(chain, where, left, rights, blk, name, depth_first=False, waits=()):
    rows, m = left.shape
    piece = m // 32
    starts, steps = [], 0
    for r in rights:
        starts.append(steps)
        steps += r.shape[1] // blk

    def kernel(where_ref, l_ref, *refs):
        r_refs, (own_lo, own_hi, sib_lo, sib_hi, lt_ref, r_all, acc) = refs[: len(rights)], refs[len(rights) :]
        step = pl.program_id(0)

        @pl.when(step == 0)
        def _():
            lt_ref[...] = l_ref[...].T

        if len(rights) == 1:
            right = r_refs[0][...]
        else:
            for ref, start, end in zip(r_refs, starts, starts[1:] + [steps]):

                @pl.when((step >= start) & (step < end))
                def _(ref=ref):
                    r_all[...] = ref[...]

            right = r_all[...]
        acc[...] = nn(lt_ref[...], right)
        hand_out(where_ref, acc, piece, (own_lo, own_hi), (sib_lo, sib_hi), depth_first)

    def chunk(r, start):
        n = r.shape[1] // blk
        return pl.BlockSpec((rows, blk), lambda i: (0, jnp.clip(i - start, 0, n - 1)))

    block = pl.BlockSpec((8, 1, piece, blk), lambda i: (0, i, 0, 0))
    own_lo, own_hi, sib_lo, sib_hi = chain.call(
        kernel,
        (where, left, *rights),
        grid=(steps,),
        in_specs=[SCALARS, whole(left)] + [chunk(r, start) for r, start in zip(rights, starts)],
        out_specs=[block] * 4,
        out_shape=[shape_of((8, steps, piece, blk))] * 4,
        scratch_shapes=[pltpu.VMEM((m, rows), BF), pltpu.VMEM((rows, blk), BF), pltpu.VMEM((m, blk), F32)],
        waits=waits,
        vmem=VMEM,
        cost=9,
        name=name,
    )
    return (own_lo, own_hi), (sib_lo, sib_hi)


def tall_grad_kernel(
    where_ref, y_ref, c_ref, o_ref, dz_ref, own_lo, own_hi, sib_lo, sib_hi, acc_ref, out_ref
):
    step = pl.program_id(0)
    tall = y_ref.shape[1] // 8
    flat = o_ref.shape[1] // 32

    @pl.when(step == 0)
    def _():
        out_ref[...] = tn(o_ref[...], dz_ref[...])

    acc_ref[...] = tn(y_ref[...], c_ref[...])
    plane, core = where_ref[1], where_ref[2]
    for refs, half in (((own_lo, own_hi), core), ((sib_lo, sib_hi), 1 - core)):
        for slot in range(4):
            near = jnp.bitwise_xor(plane, summed_slot(slot, half)) * 2 + half
            out = refs[slot // 2]
            for q in range(tall // flat):
                row = pl.multiple_of(near * tall + q * flat, 8)
                out[slot % 2, 0, q] = acc_ref[pl.ds(row, flat)].astype(BF)
            row = pl.multiple_of((step * 8 + near) * flat, 8)
            out[slot % 2, 0, tall // flat] = out_ref[pl.ds(row, flat)].astype(BF)


def tall_grad(chain, where, y, c, o, dz):
    rows, ff = y.shape
    d = c.shape[1]
    piece = d // 32
    chunks = ff // d + 1

    def slot(flip):
        def index(i, where_ref):
            core = where_ref[2]
            return (0, summed_slot(jnp.bitwise_xor(i, where_ref[0]), 1 - core if flip else core), 0, 0, 0)

        return pl.BlockSpec((2, 1, chunks, piece, d), index)

    got = chain.call(
        tall_grad_kernel,
        (where, y, c, o, dz),
        scalars=1,
        grid=(4,),
        in_specs=[pl.BlockSpec((rows, ff // 4), lambda i, w: (0, i)), kept(c), kept(o), kept(dz)],
        out_specs=[slot(False), slot(False), slot(True), slot(True)],
        out_shape=[shape_of((2, 4, chunks, piece, d))] * 4,
        scratch_shapes=[pltpu.VMEM((ff // 4, d), F32), pltpu.VMEM((d, d), F32)],
        vmem=VMEM,
        cost=12.5,
        name="down_out_grad",
    )
    own_lo, own_hi, sib_lo, sib_hi = (t.reshape(8, chunks, piece, d) for t in got)
    return (own_lo, own_hi), (sib_lo, sib_hi)


def arrange_vectors(chain, where, own, sib, m):
    last, rows, n = own[0].shape

    def kernel(where_ref, *refs):
        plane, core = where_ref[1], where_ref[2]
        out = refs[8]
        found = []
        for ref in refs[:8]:
            t = ref[0].astype(F32)
            found.append(t[0:3] + t[3:6] + t[6:9])
        for f in range(8):
            mine = core == f % 2
            slot = gathered_slot(jnp.bitwise_xor(plane, f // 2), f % 2)
            v = jnp.where(mine, found[0], found[4])
            for r in range(1, 4):
                v = jnp.where(slot == r, jnp.where(mine, found[r], found[4 + r]), v)
            for row, at in enumerate(range(0, m, n)):
                w = min(n, m - at)
                out[:, f * m + at : f * m + at + w] = v[row : row + 1, 0:w]

    block = pl.BlockSpec((1, rows, n), lambda i: (last - 1, 0, 0))
    return chain.call(
        kernel,
        (where, *own, *sib),
        grid=(1,),
        in_specs=[SCALARS] + [block] * 8,
        out_specs=vector_of(8 * m),
        out_shape=shape_of((1, 8 * m), F32),
        vmem=8,
        cost=1,
        name="arrange_vectors",
    )


def after(values, *deps):
    return lax.optimization_barrier((values, deps))[0]


def whole_gather(w, axes=AXES):
    return lax.all_gather(w, axes, axis=0, tiled=True)


def general(tokens, first_values, cotangent, lengths, vectors, w_qkv, w_out, w_up, w_down):
    d = tokens.shape[1]
    chain = Chain()
    scatter = lambda g: lax.psum_scatter(g, AXES, scatter_dimension=0, tiled=True)
    vec = whole_gather(vectors, "fsdp").reshape(1, -1)
    f_qkv, f_out, f_up, f_down = (whole_gather(w) for w in (w_qkv, w_out, w_up, w_down))
    where = jnp.zeros((3,), jnp.int32)
    a1, q, k, v = project(chain, tokens, first_values, vec, f_qkv)
    n = d // (4 * HD)
    o, lse = attend_forward(chain, lengths, q, k, v, 0, 2 * n)
    x1, a2, y, du, dx1, dz, do, *known = feed(chain, o, tokens, cotangent, vec, (f_up, f_down, f_out))
    output = final_output(chain, y, x1, vec, f_down)
    dq, dk, df, dfirst = attend_backward(chain, lengths, q, k, v, o, do, lse, 0, 2 * n)
    terms = (dq, dk, df)
    grad_tokens, dvec = input_grad(chain, where, terms, f_qkv, tokens, dx1, vec, known, False)
    n = vectors.shape[0]
    grad_vectors = lax.dynamic_slice_in_dim(lax.psum(dvec[0], AXES), lax.axis_index("fsdp") * n, n, 0)
    return (
        output, grad_tokens, dfirst, grad_vectors,
        scatter(tn(a1, jnp.concatenate(terms, axis=1))), scatter(tn(o, dz)), scatter(tn(a2, du)), scatter(tn(y, cotangent)),
    )


def local(tokens, first_values, cotangent, lengths, vectors, w_qkv, w_out, w_up, w_down):
    d = tokens.shape[1]
    index = lax.axis_index("fsdp")
    plane, core = lax.div(index, 2), lax.rem(index, 2)
    where = jnp.stack([lax.axis_index("dp"), plane, core]).astype(jnp.int32)
    piece = w_qkv.shape[0]
    tall = w_down.shape[0] // piece
    chain = Chain()

    grow = lambda a, b: jnp.concatenate([a, b], axis=0)
    chunks = w_down.reshape(tall, piece, d)
    early = chunks[: tall // 2][None]
    late = jnp.concatenate([w_up.reshape(piece, -1, d).transpose(1, 0, 2), w_out[None], chunks[tall // 2 :]], axis=0)[None]
    m = [w_qkv[None]] + [depth_swap(w_qkv[None], bits) for bits in (1, 2, 3)]
    m, near_e, side_e, early, late = after((m, plane_step(early, 0), plane_step(early, 1), early, late))

    m = pack(chain, m, vectors[None], d // 2)
    near, side = plane_step(m, 0), plane_step(m, 1)
    far_e, got = plane_step(near_e, 1), depth_step(late, 0)
    m, near, side, far_e, late, got = after((m, near, side, far_e, late, got))

    late = grow(late, got)
    early = jnp.concatenate([early, near_e, side_e, far_e], axis=0)[None]
    far, sib, got = plane_step(near, 1), core_step(m), depth_step(late, 1)
    far, sib, got, late, early = after((far, sib, got, late, early))

    late = grow(late, got)
    own, sib = [m, near, side, far], [sib] + [core_step(t) for t in (near, side, far)]
    near_l, side_l, got = plane_step(late, 0), plane_step(late, 1), depth_step(early, 0)
    vec = arrange_vectors(chain, where, own, sib, vectors.shape[0])
    a1, q, k, v, f_qkv = project(chain, tokens, first_values, vec, (own, sib), where)
    early, got, late, near_l, side_l = after((early, got, late, near_l, side_l), a1)

    early = grow(early, got)
    got, sib_e = depth_step(early, 1), [core_step(early)]
    far_l = plane_step(near_l, 1)
    sib_l = [core_step(t) for t in (late, near_l, side_l)]
    o, lse = attend_forward(chain, lengths, q, k, v, 0, 6)
    far_l, sib_l, got = after((far_l, sib_l, got), o)
    sib_l += [core_step(far_l)]
    sib_e += [core_step(got)]
    x1, a2, y, du, dx1, dz, do, *known, f_down = feed(
        chain, o, tokens, cotangent, vec,
        (late, near_l, side_l, far_l, *sib_l, early, got, *sib_e), where,
    )

    sum_d = Sum(*tall_grad(chain, where, y, cotangent, o, dz))
    sum_u = Sum(*wide_grad(chain, where, a2, [du], d, "up_grad", True))
    sum_d.got = after(sum_d.got, sum_u.own)
    send_d, send_u = sum_d.start(), sum_u.start()
    got_d, got_u = plane_step(send_d, 0), depth_step(send_u, 0)
    dq, dk, df, dfirst = attend_backward(chain, lengths, q, k, v, o, do, lse, 0, d // (2 * HD), None, (send_d, send_u))
    terms = (dq, dk, df)
    sum_q = Sum(*wide_grad(chain, where, a1, terms, d // 2, "qkv_grad"))
    got_d, got_u = after((got_d, got_u), sum_q.own)
    send_d, send_u = sum_d.upper(got_d), sum_u.upper(got_u)
    got_d, got_u = plane_step(send_d, 1), depth_step(send_u, 1)
    sum_q.got = after(sum_q.got, send_d, send_u)
    send_q = sum_q.start()
    got_q = plane_step(send_q, 0)
    grad_tokens, vec_own, vec_sib = input_grad(
        chain, where, terms, f_qkv, tokens, dx1, vec, known, True, (send_q, send_d, send_u)
    )
    got_q, got_d, got_u, vec_sib = after((got_q, got_d, got_u, vec_sib))
    send_q = sum_q.upper(got_q)
    got_q, got_vec = plane_step(send_q, 1), core_step(vec_sib)
    got_d, got_u = after((got_d, got_u), send_q)
    send_d, send_u = sum_d.upper(got_d), sum_u.upper(got_u)
    got_d, got_u = depth_step(send_d, 0), plane_step(send_u, 0)
    output = final_output(chain, y, x1, vec, f_down, 0, 1, None, (send_q, send_d, send_u))
    got_q, got_d, got_u, got_vec = after((got_q, got_d, got_u, got_vec), output)
    send_q = sum_q.upper(got_q)
    got_d, got_u, got_vec = after((got_d, got_u, got_vec), send_q)
    got_q = depth_step(send_q, 0)
    got_d, got_u = depth_step(sum_d.upper(got_d), 1), plane_step(sum_u.upper(got_u), 1)
    v = vec_own + got_vec
    got_vec = [fsdp_swap(v[bits], 2 * bits) for bits in (1, 2, 3)]
    send_q = sum_q.upper(got_q)
    got_vec = after(got_vec, send_q)
    got_q = depth_step(send_q, 1)
    got_d, got_u = after((got_d, got_u), send_q)
    v = v[0] + sum(got_vec)
    grad_vectors = v + sum(depth_swap(v, bits) for bits in (1, 2, 3))
    grad_down, grad_out, grad_up = totals(
        chain,
        [sum_d.last(got_d), sum_u.last(got_u)],
        [[(tall * piece, d), (piece, d)], [(piece, tall * d)]],
        "feed_sums",
    )
    got_q = after(got_q, grad_up)
    grad_qkv, = totals(chain, [sum_q.last(got_q)], [[(piece, w_qkv.shape[1])]], "qkv_sum")
    return output, grad_tokens, dfirst, grad_vectors, grad_qkv, grad_out, grad_up, grad_down


def solution(mesh):
    rows = P(AXES, None)
    small = mesh.shape["dp"] == 4 and mesh.shape["fsdp"] == 8
    return jax.shard_map(
        local if small else general,
        mesh=mesh,
        in_specs=(rows, rows, rows, rows, P("fsdp"), rows, rows, rows, rows),
        out_specs=(rows, rows, rows, P("fsdp"), rows, rows, rows, rows),
        check_vma=False,
    )
```

```python
import functools
import math

import jax
import jax.numpy as jnp
from jax import lax
from jax.experimental import pallas as pl
from jax.experimental.pallas import tpu as pltpu
from jax.sharding import PartitionSpec as P

BF = jnp.bfloat16
F32 = jnp.float32
HD = 64
EPSILON = 1e-5
HIDDEN = -1e30
AXES = ("dp", "fsdp")
GELU = math.sqrt(2 / math.pi)
CUBE = 0.044715
MIB = 1 << 20
VMEM = 60
PACE = 0.01


def nn(a, b):
    return jnp.dot(a, b, preferred_element_type=F32)


def nt(a, b):
    return lax.dot_general(a, b, (((1,), (1,)), ((), ())), preferred_element_type=F32)


def tn(a, b):
    return lax.dot_general(a, b, (((0,), (0,)), ((), ())), preferred_element_type=F32)


def shape_of(shape, dtype=BF):
    return jax.ShapeDtypeStruct(shape, dtype)


def whole(a):
    return pl.BlockSpec(a.shape, lambda i: (0,) * a.ndim, pipeline_mode=pl.Buffered(1))


def kept(a):
    return pl.BlockSpec(a.shape, lambda *at: (0,) * a.ndim, pipeline_mode=pl.Buffered(1))


def rows_of(blk, n):
    return pl.BlockSpec((blk, n), lambda i: (i, 0))


def vector_of(n):
    return pl.BlockSpec((1, n), lambda i: (0, 0))


SCALARS = pl.BlockSpec(memory_space=pltpu.SMEM)


class Chain:
    def __init__(self):
        self.mark = None

    def call(
        self, kernel, args, *, grid, in_specs, out_specs, out_shape, vmem, cost, waits=(), into=None, scalars=0,
        scratch_shapes=(), name=None,
    ):
        several = isinstance(out_shape, (list, tuple))
        out_specs = list(out_specs) if several else [out_specs]
        out_shape = list(out_shape) if several else [out_shape]
        into = list(into or ())
        deps = into + ([] if self.mark is None else [self.mark]) + list(waits)
        used, extra, outs = len(args), len(deps), len(out_shape)

        def body(*refs):
            results = used + extra
            mark = refs[results + outs]
            mark[...] = jnp.zeros(mark.shape, mark.dtype)
            kernel(*refs[:used], *refs[results : results + outs], *refs[results + outs + 1 :])

        got = pl.pallas_call(
            body,
            grid_spec=pltpu.PrefetchScalarGridSpec(
                num_scalar_prefetch=scalars,
                grid=grid,
                in_specs=list(in_specs) + [pl.BlockSpec(memory_space=pl.ANY)] * extra,
                out_specs=out_specs + [pl.BlockSpec((8, 128), lambda *at: (0, 0))],
                scratch_shapes=list(scratch_shapes),
            ),
            out_shape=out_shape + [shape_of((8, 128), F32)],
            compiler_params=pltpu.CompilerParams(vmem_limit_bytes=vmem * MIB),
            cost_estimate=pl.CostEstimate(
                flops=int(cost * PACE * 1.15e9), bytes_accessed=int(cost * PACE * 3.69e6), transcendentals=0
            ),
            input_output_aliases={used + i: i for i in range(len(into))},
            name=name,
        )(*args, *deps)
        self.mark = got[-1]
        return got[:-1] if several else got[0]


def half_mask(head):
    return (lax.broadcasted_iota(jnp.int32, (1, 2 * HD), 1) // HD) == head


def causal_tile(blk):
    key = lax.broadcasted_iota(jnp.int32, (blk, blk), 0)
    return key <= lax.broadcasted_iota(jnp.int32, (blk, blk), 1)


def staged(work, *stages):
    first, second, third = stages
    ahead, behind = first(*work[0]), None
    for t in range(len(work) + 1):
        coming = first(*work[t + 1]) if t + 1 < len(work) else None
        now = second(*work[t], *ahead) if t < len(work) else None
        if behind is not None:
            third(*work[t - 1], *behind)
        ahead, behind = coming, now


def attend_forward_kernel(len_ref, q_ref, k_ref, v_ref, o_ref, lse_ref, ot_ref):
    rows = q_ref.shape[0]
    blk, half = 256, rows // 2
    bias = jnp.where(len_ref[0, 0] < rows, HIDDEN, 0.0).astype(F32)
    vt = v_ref[...].T
    causal = causal_tile(blk)

    def scores(head, i):
        q = jnp.where(half_mask(head), q_ref[i * blk : (i + 1) * blk], jnp.zeros((), BF))
        parts = []
        for j in range(i + 1):
            s = nt(k_ref[j * blk : (j + 1) * blk], q)
            if j == i:
                s = jnp.where(causal, s, HIDDEN)
            elif i * blk >= half and (j + 1) * blk <= half:
                s = s + bias
            parts.append(s)
        return (parts,)

    def weights(head, i, parts):
        m = functools.reduce(jnp.maximum, [s.max(axis=0, keepdims=True) for s in parts])
        total = jnp.zeros((1, blk), F32)
        probs = []
        for s in parts:
            p = jnp.exp(s - m)
            total = total + p.sum(axis=0, keepdims=True)
            probs.append(p.astype(BF))
        lse_ref[0, head : head + 1, i * blk : (i + 1) * blk] = m + jnp.log(total)
        return probs, total

    def mix(head, i, probs, total):
        hs = slice(HD * head, HD * head + HD)
        mixed = sum(nn(vt[hs, j * blk : (j + 1) * blk], p) for j, p in enumerate(probs))
        ot_ref[hs, i * blk : (i + 1) * blk] = mixed / total

    staged([(head, i) for i in range(rows // blk) for head in range(2)], scores, weights, mix)
    o_ref[...] = ot_ref[...].T.astype(BF)


def attend_forward(chain, lengths, q, k, v, first, count, into=None):
    rows, width = q.shape
    pair = pl.BlockSpec((rows, 2 * HD), lambda p: (0, p + first))
    return chain.call(
        attend_forward_kernel,
        (lengths, q, k, v),
        grid=(count,),
        in_specs=[SCALARS, pair, pair, pair],
        out_specs=[pair, pl.BlockSpec((1, 2, rows), lambda p: (p + first, 0, 0))],
        out_shape=[shape_of((rows, width)), shape_of((width // (2 * HD), 2, rows), F32)],
        scratch_shapes=[pltpu.VMEM((2 * HD, rows), F32)],
        into=into,
        vmem=VMEM,
        cost=3.5 * count,
        name="attend_forward",
    )


def attend_backward_kernel(
    len_ref, q_ref, k_ref, v_ref, o_ref, do_ref, lse_ref, dq_ref, dk_ref, *rest, first, fresh, parts
):
    dv_refs, (dqt_acc, dv_acc, dk_acc) = rest[:parts], rest[parts:]
    rows = q_ref.shape[0]
    blk, half = 256, rows // 2
    nb = rows // blk
    bias = jnp.where(len_ref[0, 0] < rows, HIDDEN, 0.0).astype(F32)
    prod = (do_ref[...].astype(F32) * o_ref[...].astype(F32)).T
    kt = k_ref[...].T
    causal = causal_tile(blk)
    delta = [prod[HD * h : HD * h + HD].sum(axis=0, keepdims=True) for h in range(2)]
    qh = [jnp.where(half_mask(h), q_ref[...], jnp.zeros((), BF)) for h in range(2)]
    doh = [jnp.where(half_mask(h), do_ref[...], jnp.zeros((), BF)) for h in range(2)]
    block = lambda i: slice(i * blk, (i + 1) * blk)
    sums = {}

    def scores(head, j, i):
        return nt(k_ref[block(j)], qh[head][block(i)]), nt(v_ref[block(j)], doh[head][block(i)])

    def weights(head, j, i, s, dp):
        if i == j:
            s = jnp.where(causal, s, HIDDEN)
        elif i * blk >= half and (j + 1) * blk <= half:
            s = s + bias
        p = jnp.exp(s - lse_ref[0, head : head + 1, block(i)])
        return p.astype(BF), (p * (dp - delta[head][:, block(i)])).astype(BF)

    def mix(head, j, i, p, ds):
        hs, at, kr = slice(HD * head, HD * head + HD), block(i), block(j)
        dv, dk = nn(p, doh[head][at]), nn(ds, qh[head][at])
        if i > j:
            dv, dk = sums[head, j][0] + dv, sums[head, j][1] + dk
        sums[head, j] = dv, dk
        dqt = nn(kt[hs, kr], ds)
        if j == 0:
            dqt_acc[hs, at] = dqt
        else:
            dqt_acc[hs, at] += dqt
        if i == nb - 1:
            dv, dk = sums.pop((head, j))
            if head == 0:
                dv_acc[kr] = dv
                dk_acc[kr] = dk
            else:
                dv_acc[kr] += dv
                dk_acc[kr] += dk

    staged([(h, j, i) for h in range(2) for j in range(nb) for i in range(j, nb)], scores, weights, mix)
    dq_ref[...] = (dqt_acc[...].T * 0.125).astype(BF)
    dk_ref[...] = dk_acc[...].astype(BF)
    dv = dv_acc[...].astype(BF)
    if len(dv_refs) == 1:
        dv_refs[0][...] = dv
        return
    pair = pl.program_id(0) + first

    @pl.when(pair < fresh)
    def _():
        dv_refs[0][...] = dv

    @pl.when(pair >= fresh)
    def _():
        dv_refs[1][...] = dv


def attend_backward(chain, lengths, q, k, v, o, do, lse, first, count, into=None, waits=()):
    rows, width = q.shape
    fresh = width // (4 * HD)
    pair = pl.BlockSpec((rows, 2 * HD), lambda p: (0, p + first))
    new = pl.BlockSpec((rows, 2 * HD), lambda p: (0, jnp.minimum(p + first, fresh - 1)))
    old = pl.BlockSpec((rows, 2 * HD), lambda p: (0, jnp.maximum(p + first - fresh, 0)))
    dvs = [new] * (first < fresh) + [old] * (first + count > fresh)
    return chain.call(
        functools.partial(attend_backward_kernel, first=first, fresh=fresh, parts=len(dvs)),
        (lengths, q, k, v, o, do, lse),
        grid=(count,),
        in_specs=[SCALARS] + [pair] * 5 + [pl.BlockSpec((1, 2, rows), lambda p: (p + first, 0, 0))],
        out_specs=[pair, pair] + dvs,
        out_shape=[shape_of((rows, width))] * 2 + [shape_of((rows, width // 2))] * len(dvs),
        scratch_shapes=[
            pltpu.VMEM((2 * HD, rows), F32),
            pltpu.VMEM((rows, 2 * HD), F32),
            pltpu.VMEM((rows, 2 * HD), F32),
        ],
        vmem=VMEM,
        cost=6 * count,
        into=into,
        waits=waits,
        name="attend_backward",
    )


def row_stats(v):
    center = v - jnp.mean(v, axis=-1, keepdims=True)
    rstd = lax.rsqrt(jnp.mean(center * center, axis=-1, keepdims=True) + EPSILON)
    return center * rstd, rstd


def norm_back(grad, unit, rstd, gain):
    g = grad * gain
    return rstd * (
        g - jnp.mean(g, axis=-1, keepdims=True) - unit * jnp.mean(g * unit, axis=-1, keepdims=True)
    )


def column_sum(v):
    return v.astype(F32).sum(axis=0, keepdims=True)


def clear(*refs):
    @pl.when(pl.program_id(0) == 0)
    def _():
        for r in refs:
            r[...] = jnp.zeros(r.shape, r.dtype)


def vector_parts(ref, d, vd):
    ff = ref.shape[1] - 7 * d - vd
    parts, at = [], 0
    for n in (d, d, d, vd, d, d, d, ff, d):
        parts.append(ref.at[:, at : at + n])
        at += n
    return parts


def project_kernel(*refs, pieces):
    if pieces:
        where_ref, *side = refs[: 2 * pieces + 1]
        x_ref, first_ref, vec_ref, a_ref, q_ref, k_ref, v_ref, w_ref, acc_ref = refs[2 * pieces + 1 :]

        @pl.when(pl.program_id(0) == 0)
        def _():
            load_side(where_ref, side[:pieces], side[pieces:], w_ref, acc_ref)
    else:
        x_ref, first_ref, vec_ref, w_ref, a_ref, q_ref, k_ref, v_ref = refs
    d, vd = x_ref.shape[1], first_ref.shape[1]
    g_ref, b_ref, bq_ref, bv_ref = vector_parts(vec_ref, d, vd)[:4]
    unit, _ = row_stats(x_ref[...].astype(F32))
    a = (unit * g_ref[...] + b_ref[...]).astype(BF)
    a_ref[...] = a
    q = (nn(a, w_ref[:, 0:d]) + bq_ref[...]).astype(BF)
    q_ref[...] = (q.astype(F32) * 0.125).astype(BF)
    k_ref[...] = nn(a, w_ref[:, d : 2 * d]).astype(BF)
    v_ref[:, 0:vd] = (nn(a, w_ref[:, 2 * d :]) + bv_ref[...]).astype(BF)
    v_ref[:, vd:] = first_ref[...]


def project(chain, x, first, vec, w, where=None, blk=256):
    rows, d = x.shape
    pieces = w is not None and where is not None
    args, specs = (x, first, vec), [rows_of(blk, d), rows_of(blk, first.shape[1]), whole(vec)]
    outs, shapes, scratch = [rows_of(blk, d)] * 4, [shape_of((rows, d))] * 4, []
    count = 0
    if pieces:
        own, sib = w
        count = len(own)
        _, r, n = own[0].shape
        n = n * (own[0].shape[0] // 4)
        args = (where, *own, *sib) + args
        specs = [SCALARS] + [kept(t) for t in (*own, *sib)] + specs
        outs = outs + [pl.BlockSpec((32 * r, n), lambda i: (0, 0))]
        shapes = shapes + [shape_of((32 * r, n))]
        scratch = [pltpu.VMEM((32 * r, n), F32)]
    else:
        args, specs = args + (w,), specs + [whole(w)]
    return chain.call(
        functools.partial(project_kernel, pieces=count),
        args,
        grid=(rows // blk,),
        in_specs=specs,
        out_specs=outs,
        out_shape=shapes,
        scratch_shapes=scratch,
        vmem=VMEM,
        cost=8,
        name="project",
    )


def feed_kernel(*refs, pieces, chunk=256):
    if pieces:
        where_ref, *side = refs[: pieces + 1]
        (
            o_ref, x_ref, c_ref, vec_ref, x1_ref, a_ref, y_ref, du_ref, dx_ref, dz_ref, do_ref,
            dbo_ref, dg_ref, db_ref, dbu_ref, dbd_ref, wd_ref, wo_ref, wu_ref, acc,
        ) = refs[pieces + 1 :]

        @pl.when(pl.program_id(0) == 0)
        def _():
            load_feed(where_ref, side[:4], side[4:8], side[8:10], side[10:], wu_ref, wd_ref, wo_ref, acc)
    else:
        (
            o_ref, x_ref, c_ref, vec_ref, wu_ref, wd_ref, wo_ref, x1_ref, a_ref, y_ref, du_ref, dx_ref,
            dz_ref, do_ref, dbo_ref, dg_ref, db_ref, dbu_ref, dbd_ref,
        ) = refs
    clear(dbo_ref, dg_ref, db_ref, dbu_ref, dbd_ref)
    d, ff = wu_ref.shape
    bo_ref, g_ref, b_ref, bu_ref = vector_parts(vec_ref, d, vec_ref.shape[1] - 7 * d - ff)[4:8]
    x1 = x_ref[...].astype(F32) + (nn(o_ref[...], wo_ref[...]) + bo_ref[...])
    x1_ref[...] = x1
    unit, rstd = row_stats(x1)
    a = (unit * g_ref[...] + b_ref[...]).astype(BF)
    a_ref[...] = a
    c = c_ref[...]
    da = jnp.zeros(x1.shape, F32)
    spans = [slice(n, n + chunk) for n in range(0, wu_ref.shape[1], chunk)]

    def products(at):
        return nn(a, wu_ref[:, at]) + bu_ref[:, at], nt(c, wd_ref[at])

    ahead = products(spans[0])
    for i, at in enumerate(spans):
        u, dy = ahead
        if i + 1 < len(spans):
            ahead = products(spans[i + 1])
        u2 = u * u
        t = jnp.tanh(u * (GELU + (GELU * CUBE) * u2))
        h = 0.5 * t + 0.5
        y = u * h
        y_ref[:, at] = y.astype(BF)
        slope = h + (y - y * h) * (2 * GELU + (6 * GELU * CUBE) * u2)
        du = (slope * dy).astype(BF)
        du_ref[:, at] = du
        dbu_ref[:, at] += column_sum(du)
        da = da + nt(du, wu_ref[:, at])
    c32 = c.astype(F32)
    dbd_ref[...] += column_sum(c)
    db_ref[...] += column_sum(da)
    dg_ref[...] += column_sum(da * unit)
    dx = c32 + norm_back(da, unit, rstd, g_ref[...])
    dx_ref[...] = dx
    dz = dx.astype(BF)
    dz_ref[...] = dz
    dbo_ref[...] += column_sum(dz)
    do_ref[...] = nt(dz, wo_ref[...]).astype(BF)


def feed(chain, o, x, c, vec, weights, where=None, blk=256):
    rows, d = x.shape
    ff = vec.shape[1] - 7 * d - d // 2
    args = (o, x, c, vec)
    specs = [rows_of(blk, d)] * 3 + [whole(vec)]
    outs = [rows_of(blk, n) for n in (d, d, ff, ff, d, d, d)] + [vector_of(n) for n in (d, d, d, ff, d)]
    shapes = [
        shape_of((rows, d), F32), shape_of((rows, d)), shape_of((rows, ff)), shape_of((rows, ff)),
        shape_of((rows, d), F32), shape_of((rows, d)), shape_of((rows, d)),
    ] + [shape_of((1, n), F32) for n in (d, d, d, ff, d)]
    scratch, count = [], 0
    if where is not None:
        count = len(weights)
        args = (where, *weights) + args
        specs = [SCALARS] + [kept(t) for t in weights] + specs
        outs = outs + [pl.BlockSpec((ff, d), lambda i: (0, 0))]
        shapes = shapes + [shape_of((ff, d))]
        scratch = [pltpu.VMEM((d, d), BF), pltpu.VMEM((d, ff), BF), pltpu.VMEM((d, d), F32)]
    else:
        args, specs = args + tuple(weights), specs + [whole(t) for t in weights]
    return chain.call(
        functools.partial(feed_kernel, pieces=count),
        args,
        grid=(rows // blk,),
        in_specs=specs,
        out_specs=outs,
        out_shape=shapes,
        scratch_shapes=scratch,
        vmem=VMEM,
        cost=31,
        name="feed_forward",
    )


def output_kernel(y_ref, x1_ref, vec_ref, wd_ref, out_ref, acc_ref):
    step = pl.program_id(0)

    @pl.when(step == 0)
    def _():
        acc_ref[...] = x1_ref[...] + vec_ref[:, vec_ref.shape[1] - x1_ref.shape[1] :]

    acc_ref[...] += nn(y_ref[...], wd_ref[...])

    @pl.when(step == pl.num_programs(0) - 1)
    def _():
        out_ref[...] = acc_ref[...].astype(BF)


def final_output(chain, y, x1, vec, wd, part=0, parts=1, into=None, waits=(), blk=768):
    rows, ff = y.shape[0] // parts, y.shape[1]
    d = x1.shape[1]
    return chain.call(
        output_kernel,
        (y, x1, vec, wd),
        grid=(ff // blk,),
        in_specs=[
            pl.BlockSpec((rows, blk), lambda i: (part, i)),
            pl.BlockSpec((rows, d), lambda i: (part, 0), pipeline_mode=pl.Buffered(1)),
            whole(vec),
            rows_of(blk, d),
        ],
        out_specs=pl.BlockSpec((rows, d), lambda i: (part, 0)),
        out_shape=shape_of(x1.shape),
        into=into,
        scratch_shapes=[pltpu.VMEM((rows, d), F32)],
        waits=waits,
        vmem=48,
        cost=8,
        name="output",
    )


def input_kernel(
    where_ref, dq_ref, dk_ref, df_ref, w_ref, x_ref, dx_ref, vec_ref,
    dbo_ref, dg2_ref, db2_ref, dbu_ref, dbd_ref, gt_ref, *rest, split,
):
    dvec_ref = rest[-1]
    clear(dvec_ref)
    half = df_ref.shape[1]
    d = x_ref.shape[1]
    dg, db, dbq, dbv, dbo, dg2, db2, dbu, dbd = vector_parts(dvec_ref, d, half)
    dq, dk, df = dq_ref[...], dk_ref[...], df_ref[...]
    da = nt(dq, w_ref[:, 0:d]) + nt(dk, w_ref[:, d : 2 * d]) + nt(df, w_ref[:, 2 * d :])
    dbq[...] += column_sum(dq)
    dbv[...] += column_sum(df)
    unit, rstd = row_stats(x_ref[...].astype(F32))
    db[...] += column_sum(da)
    dg[...] += column_sum(da * unit)
    gt_ref[...] = (dx_ref[...] + norm_back(da, unit, rstd, vec_ref[:, 0:d])).astype(BF)

    @pl.when(pl.program_id(0) == pl.num_programs(0) - 1)
    def _():
        for ref, known in ((dbo, dbo_ref), (dg2, dg2_ref), (db2, db2_ref), (dbu, dbu_ref), (dbd, dbd_ref)):
            ref[...] = known[...]
        if not split:
            rest[0][...] = dvec_ref[...]
            return
        plane, core = where_ref[1], where_ref[2]
        n = rest[0].shape[1]
        parts = [dvec_ref[:, f * n : (f + 1) * n] for f in range(8)]
        for side, out in enumerate(rest[:2]):
            for r in range(4):
                f = jnp.bitwise_xor(plane, r) * 2 + (core if side == 0 else 1 - core)
                v = parts[0]
                for g in range(1, 8):
                    v = jnp.where(f == g, parts[g], v)
                out[r : r + 1, :] = v


def input_grad(chain, where, terms, w, x, dx, vec, known, split, waits=(), blk=256):
    rows, d = x.shape
    n = vec.shape[1]
    vecs = [(4, n // 8)] * 2 if split else [(1, n)]
    return chain.call(
        functools.partial(input_kernel, split=split),
        (where, *terms, w, x, dx, vec, *known),
        grid=(rows // blk,),
        in_specs=[SCALARS] + [rows_of(blk, t.shape[1]) for t in terms] + [whole(w), rows_of(blk, d), rows_of(blk, d)]
        + [whole(t) for t in (vec, *known)],
        out_specs=[rows_of(blk, d)] + [pl.BlockSpec(t, lambda i: (0, 0)) for t in vecs],
        out_shape=[shape_of((rows, d))] + [shape_of(t, F32) for t in vecs],
        scratch_shapes=[pltpu.VMEM((1, n), F32)],
        waits=waits,
        vmem=48,
        cost=9,
        name="input_grad",
    )


def flipped(r):
    return 2 * lax.rem(r, 2) + lax.div(r, 2)


def gathered_slot(r, core):
    return jnp.where(core == 0, r, flipped(r))


def summed_slot(r, core):
    return jnp.where(core == 0, flipped(r), r)


def plane_step(v, step):
    return lax.ppermute(v, "fsdp", [(i, i ^ (2 if i % 2 == step else 4)) for i in range(8)])


def depth_step(v, step):
    pairs = [(i, i ^ (8 if i % 2 == step else 16)) for i in range(32)]
    return lax.ppermute(v, AXES, pairs)


def depth_swap(v, bits):
    return lax.ppermute(v, "dp", [(i, i ^ bits) for i in range(4)])


def fsdp_swap(v, bit):
    return lax.ppermute(v, "fsdp", [(i, i ^ bit) for i in range(8)])


def core_step(v):
    return fsdp_swap(v, 1)


def resident(a):
    return pl.BlockSpec(a.shape, lambda *at: (0,) * a.ndim)


def pack(chain, parts, vec, n):
    rows, columns = parts[0].shape[1:]
    each = columns // n
    m = vec.shape[1]

    def kernel(*refs):
        v_ref, out, acc = refs[len(parts) :]
        at = 0
        for ref in refs[: len(parts)]:
            for i in range(ref.shape[0]):
                for c in range(each):
                    out[at] = ref[i, :, c * n : (c + 1) * n]
                    at += 1
        acc[...] = jnp.zeros(acc.shape, F32)
        for row, lane in enumerate(range(0, m, n)):
            rest = v_ref[:, lane : min(lane + n, m)]
            for term in range(3):
                part = rest.astype(BF).astype(F32)
                acc[3 * term + row : 3 * term + row + 1, 0 : part.shape[1]] = part
                rest = rest - part
        out[at] = acc[...].astype(BF)

    shape = shape_of((each * sum(p.shape[0] for p in parts) + 1, rows, n))
    return chain.call(
        kernel,
        (*parts, vec),
        grid=(1,),
        in_specs=[resident(p) for p in (*parts, vec)],
        out_specs=resident(shape),
        out_shape=shape,
        scratch_shapes=[pltpu.VMEM((rows, n), F32)],
        vmem=8,
        cost=1,
        name="pack",
    )


def places(where_ref, own, sib, straight=False):
    z, plane, core = where_ref[0], where_ref[1], where_ref[2]
    for side, group in enumerate((own, sib)):
        half = core if side == 0 else 1 - core
        for rp, ref in enumerate(group):
            for t in range(4):
                rz = t if straight else gathered_slot(t, half)
                chip = jnp.bitwise_xor(z, rz) * 4 + jnp.bitwise_xor(plane, gathered_slot(rp, half))
                yield ref, t, chip * 2 + half


def load_side(where_ref, own, sib, out, acc):
    rows, n = own[0].shape[1:]
    each = out.shape[1] // n
    for ref, t, device in places(where_ref, own, sib, True):
        at = pl.ds(pl.multiple_of(device * rows, 8), rows)
        for c in range(each):
            acc[at, c * n : (c + 1) * n] = ref[t * each + c].astype(F32)
    out[...] = acc[...].astype(BF)


def load_feed(where_ref, own, sib, own_d, sib_d, wu, wd, wo, acc):
    rows, n = own[0].shape[2:]
    wide = wu.shape[1] // n
    tall = wd.shape[0] // 32
    at = lambda device: pl.ds(pl.multiple_of(device * rows, 8), rows)
    before = {id(ref): d for ref, d in zip((*own, *sib), [(own_d, r) for r in range(4)] + [(sib_d, r) for r in range(4)])}
    for ref, t, device in places(where_ref, own, sib):
        group, rp = before[id(ref)]
        early = group[t // 2]
        parts = [early[t % 2, rp, q] for q in range(early.shape[2])]
        parts += [ref[t, q] for q in range(wide + 1, ref.shape[1])]
        part = jnp.concatenate([p.astype(F32) for p in parts], axis=0)
        wd[pl.ds(pl.multiple_of(device * tall, tall), tall), :] = part.astype(BF)
        acc[at(device), :] = ref[t, wide].astype(F32)
    wo[...] = acc[...].astype(BF)
    for c in range(wide):
        for ref, t, device in places(where_ref, own, sib):
            acc[at(device), :] = ref[t, c].astype(F32)
        wu[:, c * n : (c + 1) * n] = acc[...].astype(BF)


class Sum:
    def __init__(self, own, sib):
        self.own = own
        self.got = tuple(core_step(t) for t in sib)

    def start(self):
        self.terms = [self.own[0], self.got[0]]
        return (self.own[1].astype(F32) + self.got[1].astype(F32)).astype(BF)

    def upper(self, got):
        self.terms.append(got)
        n = got.shape[0]
        return sum(t[n // 2 : n].astype(F32) for t in self.terms).astype(BF)

    def last(self, got):
        return self.terms + [got]


def totals(chain, groups, shapes, name):
    def kernel(*refs):
        outs = list(refs[sum(len(g) for g in groups) :])
        at = 0
        for g, results in zip(groups, shapes):
            terms = refs[at : at + len(g)]
            at += len(g)
            rows, n = g[0].shape[2:]
            q = 0
            for shape in results:
                out = outs.pop(0)
                for r in range(0, shape[0], rows):
                    for c in range(0, shape[1], n):
                        out[r : r + rows, c : c + n] = sum(t[0, q].astype(F32) for t in terms)
                        q += 1

    flat = [t for g in groups for t in g]
    made = [shape_of(s, F32) for results in shapes for s in results]
    return chain.call(
        kernel,
        flat,
        grid=(1,),
        in_specs=[pl.BlockSpec((1, *t.shape[1:]), lambda i: (0, 0, 0, 0)) for t in flat],
        out_specs=[resident(t) for t in made],
        out_shape=made,
        vmem=24,
        cost=3,
        name=name,
    )


def hand_out(where_ref, acc, piece, own, sib, depth_first):
    z, plane, core = where_ref[0], where_ref[1], where_ref[2]
    for refs, half in ((own, core), (sib, 1 - core)):
        for slot in range(16):
            z_slot, p_slot = (slot // 4, slot % 4) if depth_first else (slot % 4, slot // 4)
            pd = jnp.bitwise_xor(plane, summed_slot(p_slot, half))
            zd = jnp.bitwise_xor(z, summed_slot(z_slot, half))
            row = pl.multiple_of(((zd * 4 + pd) * 2 + half) * piece, 8)
            refs[slot // 8][slot % 8, 0] = acc[pl.ds(row, piece)].astype(BF)


def wide_grad(chain, where, left, rights, blk, name, depth_first=False, waits=()):
    rows, m = left.shape
    piece = m // 32
    starts, steps = [], 0
    for r in rights:
        starts.append(steps)
        steps += r.shape[1] // blk

    def kernel(where_ref, l_ref, *refs):
        r_refs, (own_lo, own_hi, sib_lo, sib_hi, lt_ref, r_all, acc) = refs[: len(rights)], refs[len(rights) :]
        step = pl.program_id(0)

        @pl.when(step == 0)
        def _():
            lt_ref[...] = l_ref[...].T

        if len(rights) == 1:
            right = r_refs[0][...]
        else:
            for ref, start, end in zip(r_refs, starts, starts[1:] + [steps]):

                @pl.when((step >= start) & (step < end))
                def _(ref=ref):
                    r_all[...] = ref[...]

            right = r_all[...]
        acc[...] = nn(lt_ref[...], right)
        hand_out(where_ref, acc, piece, (own_lo, own_hi), (sib_lo, sib_hi), depth_first)

    def chunk(r, start):
        n = r.shape[1] // blk
        return pl.BlockSpec((rows, blk), lambda i: (0, jnp.clip(i - start, 0, n - 1)))

    block = pl.BlockSpec((8, 1, piece, blk), lambda i: (0, i, 0, 0))
    own_lo, own_hi, sib_lo, sib_hi = chain.call(
        kernel,
        (where, left, *rights),
        grid=(steps,),
        in_specs=[SCALARS, whole(left)] + [chunk(r, start) for r, start in zip(rights, starts)],
        out_specs=[block] * 4,
        out_shape=[shape_of((8, steps, piece, blk))] * 4,
        scratch_shapes=[pltpu.VMEM((m, rows), BF), pltpu.VMEM((rows, blk), BF), pltpu.VMEM((m, blk), F32)],
        waits=waits,
        vmem=VMEM,
        cost=9,
        name=name,
    )
    return (own_lo, own_hi), (sib_lo, sib_hi)


def tall_grad_kernel(
    where_ref, y_ref, c_ref, o_ref, dz_ref, own_lo, own_hi, sib_lo, sib_hi, acc_ref, out_ref
):
    step = pl.program_id(0)
    tall = y_ref.shape[1] // 8
    flat = o_ref.shape[1] // 32

    @pl.when(step == 0)
    def _():
        out_ref[...] = tn(o_ref[...], dz_ref[...])

    acc_ref[...] = tn(y_ref[...], c_ref[...])
    plane, core = where_ref[1], where_ref[2]
    for refs, half in (((own_lo, own_hi), core), ((sib_lo, sib_hi), 1 - core)):
        for slot in range(4):
            near = jnp.bitwise_xor(plane, summed_slot(slot, half)) * 2 + half
            out = refs[slot // 2]
            for q in range(tall // flat):
                row = pl.multiple_of(near * tall + q * flat, 8)
                out[slot % 2, 0, q] = acc_ref[pl.ds(row, flat)].astype(BF)
            row = pl.multiple_of((step * 8 + near) * flat, 8)
            out[slot % 2, 0, tall // flat] = out_ref[pl.ds(row, flat)].astype(BF)


def tall_grad(chain, where, y, c, o, dz):
    rows, ff = y.shape
    d = c.shape[1]
    piece = d // 32
    chunks = ff // d + 1

    def slot(flip):
        def index(i, where_ref):
            core = where_ref[2]
            return (0, summed_slot(jnp.bitwise_xor(i, where_ref[0]), 1 - core if flip else core), 0, 0, 0)

        return pl.BlockSpec((2, 1, chunks, piece, d), index)

    got = chain.call(
        tall_grad_kernel,
        (where, y, c, o, dz),
        scalars=1,
        grid=(4,),
        in_specs=[pl.BlockSpec((rows, ff // 4), lambda i, w: (0, i)), kept(c), kept(o), kept(dz)],
        out_specs=[slot(False), slot(False), slot(True), slot(True)],
        out_shape=[shape_of((2, 4, chunks, piece, d))] * 4,
        scratch_shapes=[pltpu.VMEM((ff // 4, d), F32), pltpu.VMEM((d, d), F32)],
        vmem=VMEM,
        cost=12.5,
        name="down_out_grad",
    )
    own_lo, own_hi, sib_lo, sib_hi = (t.reshape(8, chunks, piece, d) for t in got)
    return (own_lo, own_hi), (sib_lo, sib_hi)


def arrange_vectors(chain, where, own, sib, m):
    last, rows, n = own[0].shape

    def kernel(where_ref, *refs):
        plane, core = where_ref[1], where_ref[2]
        out = refs[8]
        found = []
        for ref in refs[:8]:
            t = ref[0].astype(F32)
            found.append(t[0:3] + t[3:6] + t[6:9])
        for f in range(8):
            mine = core == f % 2
            slot = gathered_slot(jnp.bitwise_xor(plane, f // 2), f % 2)
            v = jnp.where(mine, found[0], found[4])
            for r in range(1, 4):
                v = jnp.where(slot == r, jnp.where(mine, found[r], found[4 + r]), v)
            for row, at in enumerate(range(0, m, n)):
                w = min(n, m - at)
                out[:, f * m + at : f * m + at + w] = v[row : row + 1, 0:w]

    block = pl.BlockSpec((1, rows, n), lambda i: (last - 1, 0, 0))
    return chain.call(
        kernel,
        (where, *own, *sib),
        grid=(1,),
        in_specs=[SCALARS] + [block] * 8,
        out_specs=vector_of(8 * m),
        out_shape=shape_of((1, 8 * m), F32),
        vmem=8,
        cost=1,
        name="arrange_vectors",
    )


def after(values, *deps):
    return lax.optimization_barrier((values, deps))[0]


def whole_gather(w, axes=AXES):
    return lax.all_gather(w, axes, axis=0, tiled=True)


def general(tokens, first_values, cotangent, lengths, vectors, w_qkv, w_out, w_up, w_down):
    d = tokens.shape[1]
    chain = Chain()
    scatter = lambda g: lax.psum_scatter(g, AXES, scatter_dimension=0, tiled=True)
    vec = whole_gather(vectors, "fsdp").reshape(1, -1)
    f_qkv, f_out, f_up, f_down = (whole_gather(w) for w in (w_qkv, w_out, w_up, w_down))
    where = jnp.zeros((3,), jnp.int32)
    a1, q, k, v = project(chain, tokens, first_values, vec, f_qkv)
    n = d // (4 * HD)
    o, lse = attend_forward(chain, lengths, q, k, v, 0, 2 * n)
    x1, a2, y, du, dx1, dz, do, *known = feed(chain, o, tokens, cotangent, vec, (f_up, f_down, f_out))
    output = final_output(chain, y, x1, vec, f_down)
    dq, dk, df, dfirst = attend_backward(chain, lengths, q, k, v, o, do, lse, 0, 2 * n)
    terms = (dq, dk, df)
    grad_tokens, dvec = input_grad(chain, where, terms, f_qkv, tokens, dx1, vec, known, False)
    n = vectors.shape[0]
    grad_vectors = lax.dynamic_slice_in_dim(lax.psum(dvec[0], AXES), lax.axis_index("fsdp") * n, n, 0)
    return (
        output, grad_tokens, dfirst, grad_vectors,
        scatter(tn(a1, jnp.concatenate(terms, axis=1))), scatter(tn(o, dz)), scatter(tn(a2, du)), scatter(tn(y, cotangent)),
    )


def local(tokens, first_values, cotangent, lengths, vectors, w_qkv, w_out, w_up, w_down):
    d = tokens.shape[1]
    index = lax.axis_index("fsdp")
    plane, core = lax.div(index, 2), lax.rem(index, 2)
    where = jnp.stack([lax.axis_index("dp"), plane, core]).astype(jnp.int32)
    piece = w_qkv.shape[0]
    tall = w_down.shape[0] // piece
    chain = Chain()

    grow = lambda a, b: jnp.concatenate([a, b], axis=0)
    chunks = w_down.reshape(tall, piece, d)
    early = chunks[: tall // 2][None]
    late = jnp.concatenate([w_up.reshape(piece, -1, d).transpose(1, 0, 2), w_out[None], chunks[tall // 2 :]], axis=0)[None]
    m = [w_qkv[None]] + [depth_swap(w_qkv[None], bits) for bits in (1, 2, 3)]
    m, near_e, side_e, early, late = after((m, plane_step(early, 0), plane_step(early, 1), early, late))

    m = pack(chain, m, vectors[None], d // 2)
    near, side = plane_step(m, 0), plane_step(m, 1)
    far_e, got = plane_step(near_e, 1), depth_step(late, 0)
    m, near, side, far_e, late, got = after((m, near, side, far_e, late, got))

    late = grow(late, got)
    early = jnp.concatenate([early, near_e, side_e, far_e], axis=0)[None]
    far, sib, got = plane_step(near, 1), core_step(m), depth_step(late, 1)
    far, sib, got, late, early = after((far, sib, got, late, early))

    late = grow(late, got)
    own, sib = [m, near, side, far], [sib] + [core_step(t) for t in (near, side, far)]
    near_l, side_l, got = plane_step(late, 0), plane_step(late, 1), depth_step(early, 0)
    vec = arrange_vectors(chain, where, own, sib, vectors.shape[0])
    a1, q, k, v, f_qkv = project(chain, tokens, first_values, vec, (own, sib), where)
    early, got, late, near_l, side_l = after((early, got, late, near_l, side_l), a1)

    early = grow(early, got)
    got, sib_e = depth_step(early, 1), [core_step(early)]
    far_l = plane_step(near_l, 1)
    sib_l = [core_step(t) for t in (late, near_l, side_l)]
    o, lse = attend_forward(chain, lengths, q, k, v, 0, 6)
    far_l, sib_l, got = after((far_l, sib_l, got), o)
    sib_l += [core_step(far_l)]
    sib_e += [core_step(got)]
    x1, a2, y, du, dx1, dz, do, *known, f_down = feed(
        chain, o, tokens, cotangent, vec,
        (late, near_l, side_l, far_l, *sib_l, early, got, *sib_e), where,
    )

    sum_d = Sum(*tall_grad(chain, where, y, cotangent, o, dz))
    sum_u = Sum(*wide_grad(chain, where, a2, [du], d, "up_grad", True))
    sum_d.got = after(sum_d.got, sum_u.own)
    send_d, send_u = sum_d.start(), sum_u.start()
    got_d, got_u = plane_step(send_d, 0), depth_step(send_u, 0)
    dq, dk, df, dfirst = attend_backward(chain, lengths, q, k, v, o, do, lse, 0, d // (2 * HD), None, (send_d, send_u))
    terms = (dq, dk, df)
    sum_q = Sum(*wide_grad(chain, where, a1, terms, d // 2, "qkv_grad"))
    got_d, got_u = after((got_d, got_u), sum_q.own)
    send_d, send_u = sum_d.upper(got_d), sum_u.upper(got_u)
    got_d, got_u = plane_step(send_d, 1), depth_step(send_u, 1)
    sum_q.got = after(sum_q.got, send_d, send_u)
    send_q = sum_q.start()
    got_q = plane_step(send_q, 0)
    grad_tokens, vec_own, vec_sib = input_grad(
        chain, where, terms, f_qkv, tokens, dx1, vec, known, True, (send_q, send_d, send_u)
    )
    got_q, got_d, got_u, vec_sib = after((got_q, got_d, got_u, vec_sib))
    send_q = sum_q.upper(got_q)
    got_q, got_vec = plane_step(send_q, 1), core_step(vec_sib)
    got_d, got_u = after((got_d, got_u), send_q)
    send_d, send_u = sum_d.upper(got_d), sum_u.upper(got_u)
    got_d, got_u = depth_step(send_d, 0), plane_step(send_u, 0)
    output = final_output(chain, y, x1, vec, f_down, 0, 1, None, (send_q, send_d, send_u))
    got_q, got_d, got_u, got_vec = after((got_q, got_d, got_u, got_vec), output)
    send_q = sum_q.upper(got_q)
    got_d, got_u, got_vec = after((got_d, got_u, got_vec), send_q)
    got_q = depth_step(send_q, 0)
    got_d, got_u = depth_step(sum_d.upper(got_d), 1), plane_step(sum_u.upper(got_u), 1)
    v = vec_own + got_vec
    got_vec = [fsdp_swap(v[bits], 2 * bits) for bits in (1, 2, 3)]
    send_q = sum_q.upper(got_q)
    got_vec = after(got_vec, send_q)
    got_q = depth_step(send_q, 1)
    got_d, got_u = after((got_d, got_u), send_q)
    v = v[0] + sum(got_vec)
    grad_vectors = v + sum(depth_swap(v, bits) for bits in (1, 2, 3))
    grad_down, grad_out, grad_up = totals(
        chain,
        [sum_d.last(got_d), sum_u.last(got_u)],
        [[(tall * piece, d), (piece, d)], [(piece, tall * d)]],
        "feed_sums",
    )
    got_q = after(got_q, grad_up)
    grad_qkv, = totals(chain, [sum_q.last(got_q)], [[(piece, w_qkv.shape[1])]], "qkv_sum")
    return output, grad_tokens, dfirst, grad_vectors, grad_qkv, grad_out, grad_up, grad_down


def solution(mesh):
    rows = P(AXES, None)
    small = mesh.shape["dp"] == 4 and mesh.shape["fsdp"] == 8
    return jax.shard_map(
        local if small else general,
        mesh=mesh,
        in_specs=(rows, rows, rows, rows, P("fsdp"), rows, rows, rows, rows),
        out_specs=(rows, rows, rows, P("fsdp"), rows, rows, rows, rows),
        check_vma=False,
    )
```
